256 devices in a mesh: dp: 32 (over z_hi, y, x), owner: 8 (over z_lo, core).
Axes of the slice: x: 4, y: 4, z: 8 (z_hi: 2, z_lo: 4; z = z_hi * 4 + z_lo), core: 2. Of those that a mesh axis runs over, the one named last changes fastest.
Arguments:
- grad_partial: bfloat16 [32, 32, 1024, 1024], P('dp', None, 'owner')
- factor_stats: float32 [32, 8, 256, 1024], P('dp', 'owner'), as said below
- owner_table: int32 [32], P('dp'), may hold values from 0 to 7, as said below
Outputs:
- direction: float32 [32, 1024, 1024], P('dp', 'owner')
The draws below stay inside these ranges and needn't reach their ends.
Inputs may be any that keep to these rules, and one draw needn't show every extreme that they name: `factor_stats`: left_stats and right_stats of every block are symmetric positive definite. `owner_table`: every slot is the first slot of the left factor of exactly 4 blocks.
All inputs are finite; a program needn't handle non-finite values.
Results may differ from the reference program's by a relative error of at most 0.0067.
Values may be sent and summed in bfloat16 or wider, within the bound.
No kernel may reach another device: no remote copies, remote signals or barrier semaphores. Data moves between devices by JAX's collectives and lax.ppermute only.
A program may use at most 128 MiB of HBM per device.

```python
import jax
import jax.numpy as jnp
from jax import lax

B = 1024
NBLK = 32
SB = 256
N_DP = 32
N_OWNER = 8


rank_terms = 8


def shared_terms(key):
    key_slots = jax.random.fold_in(key, 5)
    key_left = jax.random.fold_in(key, 6)
    key_right = jax.random.fold_in(key, 7)
    cycle = jnp.arange(NBLK, dtype=jnp.int32) % N_OWNER
    offsets = jax.random.permutation(key_slots, cycle).astype(jnp.int32)
    left_dirs = jax.random.normal(key_left, (NBLK, B, rank_terms), jnp.float32) / float(B) ** 0.5
    right_dirs = jax.random.normal(key_right, (NBLK, B, rank_terms), jnp.float32) / float(B) ** 0.5
    return (offsets, left_dirs, right_dirs)


def draw_owner_table(key, part):
    offsets, left_dirs, right_dirs = shared_terms(key)
    return offsets


def draw_grad_partial(key, part):
    offsets, left_dirs, right_dirs = shared_terms(key)
    key = jax.random.fold_in(key, 11)
    key_rows = jax.random.fold_in(key, 1)
    key_cols = jax.random.fold_in(key, 2)
    key_noise = jax.random.fold_in(key, 3)
    key_amps = jax.random.fold_in(key, 5)
    trend = 30.0 ** (jnp.arange(B, dtype=jnp.float32) / B)
    row_scale = trend * 10.0 ** jax.random.uniform(key_rows, (NBLK, B), jnp.float32)
    col_scale = 10.0 ** jax.random.uniform(key_cols, (NBLK, B), jnp.float32)
    noise = jax.random.normal(key_noise, (N_DP, NBLK, B, B), jnp.float32)
    amps = jax.random.normal(key_amps, (N_DP, NBLK, rank_terms), jnp.float32)
    noise_scale = 0.001
    common_scale = 0.087 * B
    values = noise_scale * noise * row_scale[None, :, :, None] * col_scale[None, :, None, :]
    common = jnp.einsum('ibk,bxk,byk->ibxy', amps * common_scale, left_dirs, right_dirs)
    return (values + common).astype(jnp.bfloat16)


def place_slots(block_pieces, slot_order):
    return jnp.take(block_pieces, slot_order, axis=0)


def draw_factor_stats(key, part):
    offsets, left_dirs, right_dirs = shared_terms(key)
    key = jax.random.fold_in(key, 23)
    key_x = jax.random.fold_in(key, 1)
    key_rows = jax.random.fold_in(key, 2)
    key_diag = jax.random.fold_in(key, 3)
    depth = B // 2
    base = jax.random.normal(key_x, (NBLK, 2, B, depth), jnp.float32)
    rows = 10.0 ** (0.25 * jax.random.uniform(key_rows, (NBLK, 2, B, 1), jnp.float32))
    lifted = base * rows
    gram = jnp.einsum('nfim,nfjm->nfij', lifted, lifted) / depth
    dirs = jnp.stack((left_dirs, right_dirs), axis=1)
    weights = 10.0 * float(B) ** 0.5 * 0.5 ** jnp.arange(rank_terms, dtype=jnp.float32)
    leading = jnp.einsum('nfik,nfjk->nfij', dirs * weights, dirs)
    diag = 0.2 * 10.0 ** jax.random.uniform(key_diag, (NBLK, 2, B), jnp.float32)
    eye = jnp.eye(B, dtype=jnp.float32)
    full = gram + leading + diag[:, :, :, None] * eye
    full = 0.5 * (full + jnp.swapaxes(full, 2, 3))
    pieces = full.reshape(NBLK, N_OWNER, SB, B)
    slot_order = ((jnp.arange(N_OWNER, dtype=jnp.int32)[None, :] - offsets[:, None]) % N_OWNER).astype(jnp.int32)
    return jax.vmap(place_slots)(pieces, slot_order)


def setup_inputs(seed: int = 0) -> dict:
    streams_of = jax.random.split(jax.random.key(seed), 4)
    grad_partial = draw_grad_partial(jax.random.fold_in(streams_of[3], 71), 0)
    factor_stats = draw_factor_stats(jax.random.fold_in(streams_of[3], 71), 0)
    owner_table = draw_owner_table(jax.random.fold_in(streams_of[3], 71), 0)
    return {"grad_partial": grad_partial, "factor_stats": factor_stats, "owner_table": owner_table}


def newton_root(stats_mat):
    eye = jnp.eye(B, dtype=jnp.float32)
    scale = jnp.sqrt(jnp.sum(stats_mat * stats_mat))
    normed = stats_mat / scale
    start = normed.astype(jnp.bfloat16)
    first = (1.5 * eye - 0.5 * normed).astype(jnp.bfloat16)
    second = jnp.dot(start, first, preferred_element_type=jnp.float32).astype(jnp.bfloat16)
    third = (1.5 * eye - 0.5 * jnp.dot(first, second, preferred_element_type=jnp.float32)).astype(jnp.bfloat16)
    return jnp.dot(third, first, preferred_element_type=jnp.float32).astype(jnp.bfloat16)

def reference(grad_partial, factor_stats, owner_table):

    def one_block(index):
        pieces = lax.dynamic_index_in_dim(grad_partial, index, 1, keepdims=False)
        grad = lax.optimization_barrier(jnp.sum(pieces.astype(jnp.float32), axis=0)).astype(jnp.bfloat16)
        slots = lax.dynamic_index_in_dim(factor_stats, index, 0, keepdims=False)
        offset = lax.dynamic_index_in_dim(owner_table, index, 0, keepdims=False).astype(jnp.int32)
        order = ((offset + jnp.arange(N_OWNER, dtype=jnp.int32)) % N_OWNER).astype(jnp.int32)
        stacked = jnp.take(slots, order, axis=0).reshape(2 * B, B)
        left_stats = stacked[:B]
        right_stats = stacked[B:]
        left_root = newton_root(left_stats)
        right_root = newton_root(right_stats)
        mixed = jnp.dot(left_root, grad, preferred_element_type=jnp.float32).astype(jnp.bfloat16)
        precond = jnp.dot(mixed, right_root, preferred_element_type=jnp.float32)
        grad_wide = grad.astype(jnp.float32)
        grad_mean = jnp.sum(grad_wide * grad_wide) / (B * B)
        cond_mean = jnp.sum(precond * precond) / (B * B)
        return precond * jnp.sqrt(grad_mean / (cond_mean + 1e-06))
    return lax.map(one_block, jnp.arange(NBLK, dtype=jnp.int32))
```

```python
import functools

import jax
import jax.numpy as jnp
from jax import lax
from jax.experimental import pallas as pl
from jax.experimental.pallas import tpu as pltpu
from jax.sharding import Mesh
from jax.sharding import PartitionSpec as P

FINE = ("zh", "y", "x", "zl", "c")


def fine_mesh(mesh):
    return Mesh(mesh.devices.reshape(2, 4, 4, 4, 2), FINE)


def shift(array, axis, step):
    size = lax.axis_size(axis)
    return lax.ppermute(array, axis, [(i, (i + step) % size) for i in range(size)])


def swap(array, axis, mask):
    size = lax.axis_size(axis)
    return lax.ppermute(array, axis, [(i, i ^ mask) for i in range(size)])


def f32sum(*terms):
    total = terms[0].astype(jnp.float32)
    for term in terms[1:]:
        total = total + term.astype(jnp.float32)
    return total


def narrow(*terms):
    return f32sum(*terms).astype(jnp.bfloat16)


VMEM = pl.BlockSpec(memory_space=pltpu.VMEM)
SMEM = pl.BlockSpec(memory_space=pltpu.SMEM)
HBM = pl.BlockSpec(memory_space=pltpu.HBM)


def call(kernel, name, out_shape, in_specs, operands, scratch=(), mib=16, flops=0, moved=0):
    outs = (VMEM,) * len(out_shape) if isinstance(out_shape, tuple) else VMEM
    return pl.pallas_call(
        kernel,
        out_shape=out_shape,
        in_specs=in_specs,
        out_specs=outs,
        scratch_shapes=list(scratch),
        compiler_params=pltpu.CompilerParams(vmem_limit_bytes=mib * 2**20),
        cost_estimate=pl.CostEstimate(flops=flops, bytes_accessed=moved, transcendentals=0),
        name=name,
    )(*operands)


def ring_first(up, down, axis):
    return shift(up, axis, 1), shift(down, axis, -1)


def pass_kernel(mid_ref, up_ref, down_ref, last_up_ref, last_down_ref):
    count, rows, _ = last_up_ref.shape
    for block in range(count):
        for row in range(0, rows, 32):
            at = pl.ds(row, 32)
            last_up_ref[block, at] = narrow(mid_ref[block, at], up_ref[block, at])
            last_down_ref[block, at] = narrow(mid_ref[count + block, at], down_ref[block, at])


def ring_second(mid, up, down, axis):
    count = mid.shape[0] // 2
    last = jax.ShapeDtypeStruct((count,) + mid.shape[1:], mid.dtype)
    last_up, last_down = call(
        pass_kernel, "pass_on", (last, last), [VMEM] * 3, (mid, up, down), flops=mid.size, moved=6 * mid.size
    )
    return shift(last_up, axis, 1), shift(last_down, axis, -1)


def turn_kernel(place_ref, own_ref, up_ref, down_ref, last_up_ref, last_down_ref, next_up, next_down, next_mid, next_own, sum_ref):
    rows = own_ref.shape[1]
    half = rows // 2
    for block in range(2):
        for row in range(0, rows, 32):
            at = pl.ds(row, 32)
            sum_ref[block, at] = narrow(own_ref[block, at], last_up_ref[block, at], down_ref[2 + block, at])
            sum_ref[2 + block, at] = narrow(own_ref[2 + block, at], up_ref[2 + block, at], last_down_ref[block, at])
    low, high = pl.ds(0, half), pl.ds(half, half)
    here = place_ref[0]
    ahead, across, behind = (lax.rem(here + step, 4) for step in (1, 2, 3))
    next_up[0] = sum_ref[across, low]
    next_up[1] = sum_ref[ahead, high]
    next_down[0] = sum_ref[across, high]
    next_down[1] = sum_ref[behind, low]
    next_mid[0] = sum_ref[ahead, low]
    next_mid[1] = sum_ref[behind, high]
    next_own[0] = sum_ref[here, low]
    next_own[1] = sum_ref[here, high]


def turn(place, own, up, down, last_up, last_down):
    rows, size = own.shape[1:]
    part = jax.ShapeDtypeStruct((2, rows // 2, size), own.dtype)
    return call(
        turn_kernel,
        "turn",
        (part,) * 4,
        [SMEM] + [VMEM] * 5,
        (place, own, up, down, last_up, last_down),
        scratch=[pltpu.VMEM(own.shape, own.dtype)],
        flops=2 * own.size,
        moved=8 * own.size,
    )


def pieces_kernel(*refs):
    out_ref = refs[-1]
    width = out_ref.shape[2]
    for side in range(2):
        own, up, down, last_up, last_down = refs[5 * side : 5 * side + 5]
        half = own.shape[1]
        for row in range(0, half, 32):
            at = pl.ds(row, 32)
            low = narrow(own[0, at], last_up[0, at], down[1, at])
            high = narrow(own[1, at], up[1, at], last_down[0, at])
            for piece in range(8):
                columns = slice(piece * width, (piece + 1) * width)
                out_ref[8 * side + piece, at] = low[:, columns]
                out_ref[8 * side + piece, pl.ds(half + row, 32)] = high[:, columns]


def make_pieces(*parts):
    rows, size = 2 * parts[0].shape[1], parts[0].shape[2]
    out = jax.ShapeDtypeStruct((16, rows, size // 8), jnp.bfloat16)
    return call(
        pieces_kernel, "pieces", out, [VMEM] * 10, parts, flops=4 * rows * size, moved=16 * rows * size
    )


def begin_blocks(grads_ref, moves, sems):
    copies = [
        pltpu.make_async_copy(grads_ref.at[where], out.at[slot], sems.at[i])
        for i, (where, out, slot) in enumerate(moves)
    ]
    for each in copies:
        each.start()
    return copies


def steps(place_ref, which):
    return tuple(lax.rem(place_ref[which] + step, 4) for step in range(4))


def send_kernel(place_ref, grads_ref, stats_ref, x_up, x_down, y_up, y_down, narrow_ref, sems, wide_ref):
    x, y = steps(place_ref, 0), steps(place_ref, 1)
    moves = []
    for i in range(2):
        moves += [
            ((0, i, x[2]), x_up, i),
            ((0, 2 + i, x[1]), x_up, 2 + i),
            ((0, 2 + i, x[2]), x_down, i),
            ((0, i, x[3]), x_down, 2 + i),
            ((1, y[2], i), y_up, i),
            ((1, y[1], 2 + i), y_up, 2 + i),
            ((1, y[2], 2 + i), y_down, i),
            ((1, y[3], i), y_down, 2 + i),
        ]
    stats_copy = pltpu.make_async_copy(stats_ref, wide_ref, sems.at[16])
    stats_copy.start()
    copies = begin_blocks(grads_ref, moves, sems)
    stats_copy.wait()
    for row in range(0, wide_ref.shape[0], 32):
        at = pl.ds(row, 32)
        narrow_ref[at] = wide_ref[at].astype(jnp.bfloat16)
    for each in copies:
        each.wait()


def keep_kernel(place_ref, grads_ref, x_mid, x_own, y_mid, y_own, sems):
    x, y = steps(place_ref, 0), steps(place_ref, 1)
    moves = []
    for i in range(2):
        moves += [
            ((0, i, x[1]), x_mid, i),
            ((0, 2 + i, x[3]), x_mid, 2 + i),
            ((1, y[1], i), y_mid, i),
            ((1, y[3], 2 + i), y_mid, 2 + i),
        ]
    for i in range(4):
        moves += [((0, i, x[0]), x_own, i), ((1, y[0], i), y_own, i)]
    for each in begin_blocks(grads_ref, moves, sems):
        each.wait()


def pack(kernel, place, grads, stats=None):
    mib = 16 if stats is None else 48
    outs = (jax.ShapeDtypeStruct((4,) + grads.shape[3:], grads.dtype),) * 4
    specs, operands = [SMEM, HBM], (place, grads)
    scratch = [pltpu.SemaphoreType.DMA((17,))]
    if stats is not None:
        outs += (jax.ShapeDtypeStruct(stats.shape, jnp.bfloat16),)
        specs, operands = specs + [HBM], operands + (stats,)
        scratch += [pltpu.VMEM(stats.shape, stats.dtype)]
    return call(kernel, kernel.__name__[:4], outs, specs, operands, scratch=scratch, mib=mib, moved=2**23)


def root_kernel(side, offset_ref, stats_ref, out_ref, start_ref, first_ref, second_ref, third_ref):
    size = out_ref.shape[0]
    slot = size // 4

    def eye_rows(tile):
        row_ids = lax.broadcasted_iota(jnp.int32, (slot, size), 0) + tile * slot
        col_ids = lax.broadcasted_iota(jnp.int32, (slot, size), 1)
        return jnp.where(row_ids == col_ids, 1.0, 0.0).astype(jnp.float32)

    def rows(tile):
        return pl.ds(tile * slot, slot)

    def held(tile):
        at = lax.rem(offset_ref[0] + side * 4 + tile, 8)
        return stats_ref[pl.ds(pl.multiple_of(at * slot, slot), slot), :].astype(jnp.float32)

    total = jnp.zeros((1, size), jnp.float32)
    for tile in range(4):
        values = held(tile)
        total = total + jnp.sum(values * values, axis=0, keepdims=True)
    inverse = 1.0 / jnp.sqrt(jnp.sum(total))

    for tile in range(4):
        normed = held(tile) * inverse
        start_ref[rows(tile), :] = normed.astype(jnp.bfloat16)
        first_ref[rows(tile), :] = (1.5 * eye_rows(tile) - 0.5 * normed).astype(jnp.bfloat16)
    for tile in range(4):
        product = jnp.dot(start_ref[rows(tile), :], first_ref[...], preferred_element_type=jnp.float32)
        second_ref[rows(tile), :] = product.astype(jnp.bfloat16)
    for tile in range(4):
        product = jnp.dot(first_ref[rows(tile), :], second_ref[...], preferred_element_type=jnp.float32)
        third_ref[rows(tile), :] = (1.5 * eye_rows(tile) - 0.5 * product).astype(jnp.bfloat16)
    for tile in range(4):
        product = jnp.dot(third_ref[rows(tile), :], first_ref[...], preferred_element_type=jnp.float32)
        out_ref[rows(tile), :] = product.astype(jnp.bfloat16)


def inverse_root(side, stats, offset):
    size = stats.shape[1]
    return call(
        functools.partial(root_kernel, side),
        ("left_root", "right_root")[side],
        jax.ShapeDtypeStruct((size, size), jnp.bfloat16),
        [SMEM, VMEM],
        (offset, stats),
        scratch=[pltpu.VMEM((size, size), jnp.bfloat16)] * 4,
        mib=24,
        flops=6 * size**3,
        moved=4 * size * size,
    )


def lanes(squares):
    rows, columns = squares.shape
    total = jnp.sum(squares.reshape(rows // 8, 8, columns), axis=0)
    return sum(total[:, at : at + 128] for at in range(0, columns, 128))


def mix_kernel(pieces_ref, left_ref, out_ref, energy_ref, grad_ref):
    count, rows, _ = out_ref.shape
    energy = jnp.zeros(energy_ref.shape, jnp.float32)
    for piece in range(count):
        grad = narrow(pieces_ref[piece], pieces_ref[count + piece])
        grad_ref[pl.ds(piece * rows, rows), :] = grad
        wide = grad.astype(jnp.float32)
        energy = energy + lanes(wide * wide)
    energy_ref[...] = energy
    for piece in range(0, count, 2):
        product = jnp.dot(
            left_ref[pl.ds(piece * rows, 2 * rows), :], grad_ref[...], preferred_element_type=jnp.float32
        ).astype(jnp.bfloat16)
        out_ref[piece] = product[:rows]
        out_ref[piece + 1] = product[rows:]


def mix(pieces, left_root):
    _, rows, width = pieces.shape
    return call(
        mix_kernel,
        "mix",
        (jax.ShapeDtypeStruct((8, rows, width), jnp.bfloat16), jax.ShapeDtypeStruct((8, 128), jnp.float32)),
        [VMEM] * 2,
        (pieces, left_root),
        scratch=[pltpu.VMEM((8 * rows, width), jnp.bfloat16)],
        flops=2 * left_root.size * width,
        moved=2 * left_root.size,
    )


def condition_kernel(mixed_ref, right_ref, energy_ref, out_ref, totals_ref, rows_ref):
    count, _, width = mixed_ref.shape
    for piece in range(count):
        rows_ref[:, pl.ds(piece * width, width)] = mixed_ref[piece]
    total = jnp.zeros(energy_ref.shape, jnp.float32)
    for at in range(0, out_ref.shape[1], 256):
        product = jnp.dot(rows_ref[...], right_ref[:, pl.ds(at, 256)], preferred_element_type=jnp.float32)
        out_ref[:, pl.ds(at, 256)] = product
        total = total + lanes(product * product)
    totals_ref[:8] = energy_ref[...]
    totals_ref[8:] = total


def condition(mixed, right_root, energy):
    _, rows, width = mixed.shape
    size = right_root.shape[1]
    return call(
        condition_kernel,
        "condition",
        (jax.ShapeDtypeStruct((rows, size), jnp.float32), jax.ShapeDtypeStruct((16, 128), jnp.float32)),
        [VMEM] * 3,
        (mixed, right_root, energy),
        scratch=[pltpu.VMEM((rows, size), jnp.bfloat16)],
        flops=2 * rows * right_root.size,
        moved=2 * right_root.size,
    )


def finish_kernel(count, totals_ref, precond_ref, out_ref):
    grad_mean = jnp.sum(totals_ref[:8]) / count
    cond_mean = jnp.sum(totals_ref[8:]) / count
    factor = jnp.sqrt(grad_mean / (cond_mean + 1e-06))
    for row in range(0, out_ref.shape[0], 32):
        at = pl.ds(row, 32)
        out_ref[at] = precond_ref[at] * factor


def finish(totals, precond, count):
    return call(
        functools.partial(finish_kernel, count),
        "finish",
        jax.ShapeDtypeStruct(precond.shape, jnp.float32),
        [VMEM] * 2,
        (totals, precond),
        flops=precond.size,
        moved=8 * precond.size,
    )


def local(grad_partial, factor_stats, owner_table):
    size = grad_partial.shape[3]
    rows_here = grad_partial.shape[2]
    owner = ("zl", "c")
    grads = grad_partial.reshape(2, 4, 4, rows_here, size)
    x, y = lax.axis_index("x").astype(jnp.int32), lax.axis_index("y").astype(jnp.int32)
    place = jnp.stack((x, y))

    x_up, x_down, y_up, y_down, own = pack(send_kernel, place, grads, factor_stats[0, 0])
    place, x_up, own = lax.optimization_barrier((place, x_up, own))
    stats = lax.all_gather(own, owner, axis=0, tiled=True)
    x_ends = ring_first(x_up, x_down, "x")
    y_ends = ring_first(y_up, y_down, "y")
    x_mid, x_own, y_mid, y_own = pack(keep_kernel, place, grads)

    x_last = ring_second(x_mid, *x_ends, "x")
    y_last = ring_second(y_mid, *y_ends, "y")
    lower_up, lower_down, lower_mid, lower_own = turn(y[None], x_own, *x_ends, *x_last)
    lower_ends = ring_first(lower_up, lower_down, "y")
    upper_up, upper_down, upper_mid, upper_own = turn(x[None], y_own, *y_ends, *y_last)
    upper_ends = ring_first(upper_up, upper_down, "x")
    lower_last = ring_second(lower_mid, *lower_ends, "y")
    upper_last = ring_second(upper_mid, *upper_ends, "x")
    pieces = make_pieces(lower_own, *lower_ends, *lower_last, upper_own, *upper_ends, *upper_last)
    pieces, stats = lax.optimization_barrier((pieces, stats))
    pieces = lax.all_to_all(pieces, ("zh",) + owner, split_axis=0, concat_axis=0, tiled=True)
    left_root = inverse_root(0, stats, owner_table)
    right_root = inverse_root(1, stats, owner_table)

    mixed, energy = mix(pieces, left_root)
    mixed, right_root = lax.optimization_barrier((mixed, right_root))
    mixed = lax.all_to_all(mixed, owner, split_axis=0, concat_axis=0, tiled=True)
    precond, totals = condition(mixed, right_root, energy)
    totals = totals + swap(totals, "c", 1)
    totals = totals + swap(totals, "zl", 1)
    totals = totals + swap(totals, "zl", 2)
    return finish(totals, precond, float(size * size))[None]


def solution(mesh):
    dp, owner = ("zh", "y", "x"), ("zl", "c")
    placed = (P(dp, None, owner, None), P(dp, owner, None, None), P(dp))
    return jax.shard_map(
        local, mesh=fine_mesh(mesh), in_specs=placed, out_specs=P(dp, owner, None), check_vma=False
    )
```

```python
import functools

import jax
import jax.numpy as jnp
from jax import lax
from jax.experimental import pallas as pl
from jax.experimental.pallas import tpu as pltpu
from jax.sharding import Mesh
from jax.sharding import PartitionSpec as P

FINE = ("zh", "y", "x", "zl", "c")


def fine_mesh(mesh):
    return Mesh(mesh.devices.reshape(2, 4, 4, 4, 2), FINE)


def shift(array, axis, step):
    size = lax.axis_size(axis)
    return lax.ppermute(array, axis, [(i, (i + step) % size) for i in range(size)])


def swap(array, axis, mask):
    size = lax.axis_size(axis)
    return lax.ppermute(array, axis, [(i, i ^ mask) for i in range(size)])


def f32sum(*terms):
    total = terms[0].astype(jnp.float32)
    for term in terms[1:]:
        total = total + term.astype(jnp.float32)
    return total


def narrow(*terms):
    return f32sum(*terms).astype(jnp.bfloat16)


VMEM = pl.BlockSpec(memory_space=pltpu.VMEM)
SMEM = pl.BlockSpec(memory_space=pltpu.SMEM)
HBM = pl.BlockSpec(memory_space=pltpu.HBM)


def call(kernel, name, out_shape, in_specs, operands, scratch=(), mib=16, flops=0, moved=0):
    outs = (VMEM,) * len(out_shape) if isinstance(out_shape, tuple) else VMEM
    return pl.pallas_call(
        kernel,
        out_shape=out_shape,
        in_specs=in_specs,
        out_specs=outs,
        scratch_shapes=list(scratch),
        compiler_params=pltpu.CompilerParams(vmem_limit_bytes=mib * 2**20),
        cost_estimate=pl.CostEstimate(flops=flops, bytes_accessed=moved, transcendentals=0),
        name=name,
    )(*operands)


def ring_first(up, down, axis):
    return shift(up, axis, 1), shift(down, axis, -1)


def pass_kernel(mid_ref, up_ref, down_ref, last_up_ref, last_down_ref):
    count, rows, _ = last_up_ref.shape
    for block in range(count):
        for row in range(0, rows, 32):
            at = pl.ds(row, 32)
            last_up_ref[block, at] = narrow(mid_ref[block, at], up_ref[block, at])
            last_down_ref[block, at] = narrow(mid_ref[count + block, at], down_ref[block, at])


def ring_second(mid, up, down, axis):
    count = mid.shape[0] // 2
    last = jax.ShapeDtypeStruct((count,) + mid.shape[1:], mid.dtype)
    last_up, last_down = call(
        pass_kernel, "pass_on", (last, last), [VMEM] * 3, (mid, up, down), flops=mid.size, moved=6 * mid.size
    )
    return shift(last_up, axis, 1), shift(last_down, axis, -1)


def turn_kernel(place_ref, own_ref, up_ref, down_ref, last_up_ref, last_down_ref, next_up, next_down, next_mid, next_own, sum_ref):
    rows = own_ref.shape[1]
    half = rows // 2
    for block in range(2):
        for row in range(0, rows, 32):
            at = pl.ds(row, 32)
            sum_ref[block, at] = narrow(own_ref[block, at], last_up_ref[block, at], down_ref[2 + block, at])
            sum_ref[2 + block, at] = narrow(own_ref[2 + block, at], up_ref[2 + block, at], last_down_ref[block, at])
    low, high = pl.ds(0, half), pl.ds(half, half)
    here = place_ref[0]
    ahead, across, behind = (lax.rem(here + step, 4) for step in (1, 2, 3))
    next_up[0] = sum_ref[across, low]
    next_up[1] = sum_ref[ahead, high]
    next_down[0] = sum_ref[across, high]
    next_down[1] = sum_ref[behind, low]
    next_mid[0] = sum_ref[ahead, low]
    next_mid[1] = sum_ref[behind, high]
    next_own[0] = sum_ref[here, low]
    next_own[1] = sum_ref[here, high]


def turn(place, own, up, down, last_up, last_down):
    rows, size = own.shape[1:]
    part = jax.ShapeDtypeStruct((2, rows // 2, size), own.dtype)
    return call(
        turn_kernel,
        "turn",
        (part,) * 4,
        [SMEM] + [VMEM] * 5,
        (place, own, up, down, last_up, last_down),
        scratch=[pltpu.VMEM(own.shape, own.dtype)],
        flops=2 * own.size,
        moved=8 * own.size,
    )


def settle_kernel(place_ref, *refs):
    keep_ref, give_up, give_down = refs[10:]
    half = give_up.shape[0]
    for side in range(2):
        own, up, down, last_up, last_down = refs[5 * side : 5 * side + 5]

        def settle(low_ref, low_at, high_ref, high_at):
            for row in range(0, half, 32):
                at = pl.ds(row, 32)
                low_ref[pl.ds(low_at + row, 32)] = narrow(own[0, at], last_up[0, at], down[1, at])
                high_ref[pl.ds(high_at + row, 32)] = narrow(own[1, at], up[1, at], last_down[0, at])

        pl.when(place_ref[0] == side)(functools.partial(settle, keep_ref, 0, keep_ref, half))
        pl.when(place_ref[0] != side)(functools.partial(settle, give_up, 0, give_down, 0))


def settle(place, *parts):
    _, half, size = parts[0].shape
    keep = jax.ShapeDtypeStruct((2 * half, size), jnp.bfloat16)
    give = jax.ShapeDtypeStruct((half, size), jnp.bfloat16)
    return call(
        settle_kernel,
        "settle",
        (keep, give, give),
        [SMEM] + [VMEM] * 10,
        (place,) + parts,
        flops=8 * half * size,
        moved=32 * half * size,
    )


def begin_blocks(grads_ref, moves, sems):
    copies = [
        pltpu.make_async_copy(grads_ref.at[where], out.at[slot], sems.at[i])
        for i, (where, out, slot) in enumerate(moves)
    ]
    for each in copies:
        each.start()
    return copies


def steps(place_ref, which):
    return tuple(lax.rem(place_ref[which] + step, 4) for step in range(4))


def send_x_kernel(place_ref, grads_ref, x_up, x_down, sems):
    x = steps(place_ref, 0)
    moves = []
    for i in range(2):
        moves += [
            ((0, i, x[2]), x_up, i),
            ((0, 2 + i, x[1]), x_up, 2 + i),
            ((0, 2 + i, x[2]), x_down, i),
            ((0, i, x[3]), x_down, 2 + i),
        ]
    for each in begin_blocks(grads_ref, moves, sems):
        each.wait()


def send_y_kernel(place_ref, grads_ref, y_up, y_down, sems):
    y = steps(place_ref, 1)
    moves = []
    for i in range(2):
        moves += [
            ((1, y[2], i), y_up, i),
            ((1, y[1], 2 + i), y_up, 2 + i),
            ((1, y[2], 2 + i), y_down, i),
            ((1, y[3], i), y_down, 2 + i),
        ]
    for each in begin_blocks(grads_ref, moves, sems):
        each.wait()


def keep_kernel(place_ref, grads_ref, x_mid, x_own, y_mid, y_own, sems):
    x, y = steps(place_ref, 0), steps(place_ref, 1)
    moves = []
    for i in range(2):
        moves += [
            ((0, i, x[1]), x_mid, i),
            ((0, 2 + i, x[3]), x_mid, 2 + i),
            ((1, y[1], i), y_mid, i),
            ((1, y[3], 2 + i), y_mid, 2 + i),
        ]
    for i in range(4):
        moves += [((0, i, x[0]), x_own, i), ((1, y[0], i), y_own, i)]
    for each in begin_blocks(grads_ref, moves, sems):
        each.wait()


def pack(kernel, count, mib, place, grads):
    payload = jax.ShapeDtypeStruct((4,) + grads.shape[3:], grads.dtype)
    return call(
        kernel,
        kernel.__name__[:-7],
        (payload,) * count,
        [SMEM, HBM],
        (place, grads),
        scratch=[pltpu.SemaphoreType.DMA((16,))],
        mib=mib,
        moved=count * 2**21,
    )


def trim_kernel(index_ref, stats_ref, out_ref):
    rows = stats_ref.shape[0]
    half = rows // 2

    def block(at):
        return pl.ds(at % 4 * rows, rows)

    for index in range(4):

        @pl.when(index_ref[0] == index)
        def _():
            out_ref[:, block(0)] = stats_ref[:, block(index)].astype(jnp.bfloat16)
            out_ref[:, block(1)] = stats_ref[:, block(index + 1)].astype(jnp.bfloat16)
            if index < 2:
                opposite = stats_ref[:, pl.ds((index + 2) * rows, half)]
            else:
                opposite = stats_ref[pl.ds(half, half), block(index + 2)].T
            out_ref[:, pl.ds(2 * rows, half)] = opposite.astype(jnp.bfloat16)


def trim(index, stats):
    rows = stats.shape[0]
    out = jax.ShapeDtypeStruct((rows, 2 * rows + rows // 2), jnp.bfloat16)
    return call(trim_kernel, "trim", out, [SMEM, VMEM], (index, stats), flops=stats.size, moved=6 * stats.size)


def root_kernel(side, where_ref, *refs):
    given, (out_ref, slots_ref, start_ref, first_ref, second_ref, third_ref) = refs[:8], refs[8:]
    size = out_ref.shape[0]
    slot = size // 4
    half = slot // 2
    offset, zl, c = where_ref[0], where_ref[1], where_ref[2]

    def span(tile):
        return pl.ds(tile * slot, slot)

    for tile in range(4):
        position = lax.rem(offset + (4 * side + tile), 8)
        back = lax.rem(zl + 4 - lax.div(position, 2), 4)
        source = 2 * back + lax.rem(position + c, 2)
        for i, ref in enumerate(given):

            @pl.when(source == i)
            def _():
                slots_ref[tile] = ref[...]

    total = jnp.zeros((8, slot // 2), jnp.float32)
    for tile in range(4):
        values = slots_ref[tile].astype(jnp.float32)
        squares = values * values
        total = total + lanes(squares[:, :slot]) + 2.0 * lanes(squares[:, slot:])
    inverse = 1.0 / jnp.sqrt(jnp.sum(total))

    row_ids = lax.broadcasted_iota(jnp.int32, (slot, slot), 0)
    col_ids = lax.broadcasted_iota(jnp.int32, (slot, slot), 1)
    eye = jnp.where(row_ids == col_ids, 1.0, 0.0).astype(jnp.float32)

    def place(row, column, normed, diagonal):
        start_ref[span(row), span(column)] = normed.astype(jnp.bfloat16)
        term = 1.5 * eye - 0.5 * normed if diagonal else -0.5 * normed
        first_ref[span(row), span(column)] = term.astype(jnp.bfloat16)

    for tile in range(4):
        after = (tile + 1) % 4
        place(tile, tile, slots_ref[tile, :, :slot].astype(jnp.float32) * inverse, True)
        normed = slots_ref[tile, :, slot : 2 * slot].astype(jnp.float32) * inverse
        place(tile, after, normed, False)
        place(after, tile, normed.T, False)
    for tile in range(2):
        parts = [slots_ref[at, :, 2 * slot :].astype(jnp.float32) * inverse for at in (tile, tile + 2)]
        normed = jnp.concatenate(parts, axis=1)
        place(tile, tile + 2, normed, False)
        place(tile + 2, tile, normed.T, False)

    def eye_rows(tile):
        row_ids = lax.broadcasted_iota(jnp.int32, (slot, size), 0) + tile * slot
        col_ids = lax.broadcasted_iota(jnp.int32, (slot, size), 1)
        return jnp.where(row_ids == col_ids, 1.0, 0.0).astype(jnp.float32)

    for tile in range(4):
        product = jnp.dot(start_ref[span(tile), :], first_ref[...], preferred_element_type=jnp.float32)
        second_ref[span(tile), :] = product.astype(jnp.bfloat16)
    for tile in range(4):
        product = jnp.dot(first_ref[span(tile), :], second_ref[...], preferred_element_type=jnp.float32)
        third_ref[span(tile), :] = (1.5 * eye_rows(tile) - 0.5 * product).astype(jnp.bfloat16)
    for tile in range(4):
        product = jnp.dot(third_ref[span(tile), :], first_ref[...], preferred_element_type=jnp.float32)
        out_ref[span(tile), :] = product.astype(jnp.bfloat16)


def inverse_root(side, where, slots):
    rows, kept = slots[0].shape
    size = 4 * rows
    return call(
        functools.partial(root_kernel, side),
        ("left_root", "right_root")[side],
        jax.ShapeDtypeStruct((size, size), jnp.bfloat16),
        [SMEM] + [VMEM] * 8,
        (where,) + slots,
        scratch=[pltpu.VMEM((4, rows, kept), jnp.bfloat16)] + [pltpu.VMEM((size, size), jnp.bfloat16)] * 4,
        mib=24,
        flops=6 * size**3,
        moved=4 * size * size,
    )


def lanes(squares):
    rows, columns = squares.shape
    total = jnp.sum(squares.reshape(rows // 8, 8, columns), axis=0)
    return sum(total[:, at : at + 128] for at in range(0, columns, 128))


def right_kernel(keep_ref, up_ref, down_ref, right_ref, out_ref, energy_ref, grad_ref):
    half = up_ref.shape[0]
    width = out_ref.shape[2]
    energy = jnp.zeros(energy_ref.shape, jnp.float32)
    for part, ref in enumerate((up_ref, down_ref)):
        at = pl.ds(part * half, half)
        grad = narrow(keep_ref[at], ref[...])
        grad_ref[at] = grad
        wide = grad.astype(jnp.float32)
        energy = energy + lanes(wide * wide)
    energy_ref[...] = energy
    for piece in range(0, 8, 2):
        columns = pl.ds(piece * width, 2 * width)
        product = jnp.dot(grad_ref[...], right_ref[:, columns], preferred_element_type=jnp.float32)
        product = product.astype(jnp.bfloat16)
        out_ref[piece] = product[:, :width]
        out_ref[piece + 1] = product[:, width:]


def right_product(keep, up, down, right_root):
    rows, size = keep.shape
    return call(
        right_kernel,
        "right_product",
        (jax.ShapeDtypeStruct((8, rows, size // 8), jnp.bfloat16), jax.ShapeDtypeStruct((8, 128), jnp.float32)),
        [VMEM] * 4,
        (keep, up, down, right_root),
        scratch=[pltpu.VMEM((rows, size), jnp.bfloat16)],
        flops=2 * rows * right_root.size,
        moved=2 * right_root.size,
    )


TAIL = 16


def thirds(sums):
    high = sums.astype(jnp.bfloat16).astype(jnp.float32)
    middle = (sums - high).astype(jnp.bfloat16).astype(jnp.float32)
    return high, middle, sums - high - middle


def left_kernel(cols_ref, left_ref, energy_ref, out_ref, held_ref):
    count, rows, width = cols_ref.shape
    for piece in range(count):
        held_ref[pl.ds(piece * rows, rows), :] = cols_ref[piece]
    total = jnp.zeros(energy_ref.shape, jnp.float32)
    for piece in range(0, count, 2):
        product = jnp.dot(
            left_ref[pl.ds(piece * rows, 2 * rows), :], held_ref[...], preferred_element_type=jnp.float32
        )
        total = total + lanes(product * product)
        out_ref[piece, pl.ds(0, rows)] = product[:rows].astype(jnp.bfloat16)
        out_ref[piece + 1, pl.ds(0, rows)] = product[rows:].astype(jnp.bfloat16)
    grad_sums = jnp.sum(energy_ref[...], axis=0, keepdims=True)
    cond_sums = jnp.sum(total, axis=0, keepdims=True)
    row_ids = lax.broadcasted_iota(jnp.int32, (TAIL, width), 0)
    tail = jnp.zeros((TAIL, width), jnp.float32)
    for row, values in enumerate(thirds(grad_sums) + thirds(cond_sums)):
        tail = jnp.where(row_ids == row, values, tail)
    for piece in range(count):
        out_ref[piece, pl.ds(rows, TAIL)] = tail.astype(jnp.bfloat16)


def left_product(cols, left_root, energy):
    _, rows, width = cols.shape
    return call(
        left_kernel,
        "left_product",
        jax.ShapeDtypeStruct((8, rows + TAIL, width), jnp.bfloat16),
        [VMEM] * 3,
        (cols, left_root, energy),
        scratch=[pltpu.VMEM((8 * rows, width), jnp.bfloat16)],
        flops=2 * left_root.size * width,
        moved=2 * left_root.size,
    )


def finish_kernel(pieces_ref, out_ref):
    count, _, width = pieces_ref.shape
    rows = out_ref.shape[0]
    sums = sum(pieces_ref[piece, pl.ds(rows, TAIL)].astype(jnp.float32) for piece in range(count))
    row_ids = lax.broadcasted_iota(jnp.int32, (TAIL, width), 0)
    entries = float(count * rows * count * width)
    grad_mean = jnp.sum(jnp.where(row_ids < 3, sums, 0.0)) / entries
    cond_mean = jnp.sum(jnp.where(row_ids >= 3, sums, 0.0)) / entries
    factor = jnp.sqrt(grad_mean / (cond_mean + 1e-06))
    for piece in range(count):
        out_ref[:, pl.ds(piece * width, width)] = pieces_ref[piece, pl.ds(0, rows)].astype(jnp.float32) * factor


def finish(pieces):
    count, rows, width = pieces.shape
    out = jax.ShapeDtypeStruct((rows - TAIL, count * width), jnp.float32)
    return call(finish_kernel, "finish", out, [VMEM], (pieces,), flops=out.size, moved=6 * out.size)


def after(dep, *values):
    return lax.optimization_barrier((dep,) + values)[1:]


def local(grad_partial, factor_stats, owner_table):
    size = grad_partial.shape[3]
    rows_here = grad_partial.shape[2]
    owner = ("zl", "c")
    grads = grad_partial.reshape(2, 4, 4, rows_here, size)
    zh, y, x, zl, c = (lax.axis_index(axis).astype(jnp.int32) for axis in FINE)
    place = jnp.stack((x, y))

    x_up, x_down = pack(send_x_kernel, 2, 48, place, grads)
    x_ends = ring_first(x_up, x_down, "x")
    (place,) = after(x_up, place)
    y_up, y_down = pack(send_y_kernel, 2, 48, place, grads)
    y_ends = ring_first(y_up, y_down, "y")

    where = jnp.stack((owner_table[0], zl, c))
    (index,) = after(y_up, (2 * zl + c - owner_table + 8) % 4)
    own = trim(index, factor_stats[0, 0])
    near = [own]
    for _ in range(3):
        near.append(shift(near[-1], "zl", 1))
    far = [swap(each, "c", 1) for each in near]
    (place,) = after(near[2], place)
    x_mid, x_own, y_mid, y_own = pack(keep_kernel, 4, 16, place, grads)
    (x_own,) = after(near[3], x_own)
    y_own = after(far[0], *after(far[1], y_own))[0]

    x_last = ring_second(x_mid, *x_ends, "x")
    y_last = ring_second(y_mid, *y_ends, "y")
    lower_up, lower_down, lower_mid, lower_own = turn(y[None], x_own, *x_ends, *x_last)
    lower_ends = ring_first(lower_up, lower_down, "y")
    upper_up, upper_down, upper_mid, upper_own = turn(x[None], y_own, *y_ends, *y_last)
    upper_ends = ring_first(upper_up, upper_down, "x")
    lower_own = after(far[2], *after(far[3], lower_own))[0]
    lower_last = ring_second(lower_mid, *lower_ends, "y")
    upper_last = ring_second(upper_mid, *upper_ends, "x")

    keep, up, down = settle(zh[None], lower_own, *lower_ends, *lower_last, upper_own, *upper_ends, *upper_last)
    slots = tuple(each for pair in zip(near, far) for each in pair)
    for _ in range(2):
        up, down = shift(up, ("zh", "zl"), 2), shift(down, ("zh", "zl"), -2)
    right_root = inverse_root(1, where, after(keep, *slots))
    columns, energy = right_product(keep, up, down, right_root)
    left_slots = after(columns, *slots)
    columns = lax.all_to_all(columns, owner, split_axis=0, concat_axis=0, tiled=True)
    left_root = inverse_root(0, where, left_slots)
    pieces = left_product(columns, left_root, energy)
    pieces = lax.all_to_all(pieces, owner, split_axis=0, concat_axis=0, tiled=True)
    return finish(pieces)[None]


def solution(mesh):
    dp, owner = ("zh", "y", "x"), ("zl", "c")
    placed = (P(dp, None, owner, None), P(dp, owner, None, None), P(dp))
    return jax.shard_map(
        local, mesh=fine_mesh(mesh), in_specs=placed, out_specs=P(dp, owner, None), check_vma=False
    )
```

```python
import functools

import jax
import jax.numpy as jnp
from jax import lax
from jax.experimental import pallas as pl
from jax.experimental.pallas import tpu as pltpu
from jax.sharding import Mesh
from jax.sharding import PartitionSpec as P

FINE = ("zh", "y", "x", "zl", "c")


def fine_mesh(mesh):
    return Mesh(mesh.devices.reshape(2, 4, 4, 4, 2), FINE)


def shift(array, axis, step):
    size = lax.axis_size(axis)
    return lax.ppermute(array, axis, [(i, (i + step) % size) for i in range(size)])


def swap(array, axis, mask):
    size = lax.axis_size(axis)
    return lax.ppermute(array, axis, [(i, i ^ mask) for i in range(size)])


def f32sum(*terms):
    total = terms[0].astype(jnp.float32)
    for term in terms[1:]:
        total = total + term.astype(jnp.float32)
    return total


def narrow(*terms):
    return f32sum(*terms).astype(jnp.bfloat16)


VMEM = pl.BlockSpec(memory_space=pltpu.VMEM)
SMEM = pl.BlockSpec(memory_space=pltpu.SMEM)
HBM = pl.BlockSpec(memory_space=pltpu.HBM)


def call(kernel, name, out_shape, in_specs, operands, scratch=(), mib=16, flops=0, moved=0):
    outs = (VMEM,) * len(out_shape) if isinstance(out_shape, tuple) else VMEM
    return pl.pallas_call(
        kernel,
        out_shape=out_shape,
        in_specs=in_specs,
        out_specs=outs,
        scratch_shapes=list(scratch),
        compiler_params=pltpu.CompilerParams(vmem_limit_bytes=mib * 2**20),
        cost_estimate=pl.CostEstimate(flops=flops, bytes_accessed=moved, transcendentals=0),
        name=name,
    )(*operands)


def ring_first(up, down, axis):
    return shift(up, axis, 1), shift(down, axis, -1)


def pass_kernel(mid_ref, up_ref, down_ref, last_up_ref, last_down_ref):
    count, rows, _ = last_up_ref.shape
    for block in range(count):
        for row in range(0, rows, 32):
            at = pl.ds(row, 32)
            last_up_ref[block, at] = narrow(mid_ref[block, at], up_ref[block, at])
            last_down_ref[block, at] = narrow(mid_ref[count + block, at], down_ref[block, at])


def pass_on(mid, up, down):
    count = mid.shape[0] // 2
    last = jax.ShapeDtypeStruct((count,) + mid.shape[1:], mid.dtype)
    last_up, last_down = call(
        pass_kernel, "pass_on", (last, last), [VMEM] * 3, (mid, up, down), flops=mid.size, moved=6 * mid.size
    )
    return last_up, last_down


def turn_kernel(place_ref, own_ref, up_ref, down_ref, last_up_ref, last_down_ref, next_up, next_down, next_mid, next_own, sum_ref):
    rows = own_ref.shape[1]
    half = rows // 2
    for block in range(2):
        for row in range(0, rows, 32):
            at = pl.ds(row, 32)
            sum_ref[block, at] = narrow(own_ref[block, at], last_up_ref[block, at], down_ref[2 + block, at])
            sum_ref[2 + block, at] = narrow(own_ref[2 + block, at], up_ref[2 + block, at], last_down_ref[block, at])
    low, high = pl.ds(0, half), pl.ds(half, half)
    here = place_ref[0]
    ahead, across, behind = (lax.rem(here + step, 4) for step in (1, 2, 3))
    next_up[0] = sum_ref[across, low]
    next_up[1] = sum_ref[ahead, high]
    next_down[0] = sum_ref[across, high]
    next_down[1] = sum_ref[behind, low]
    next_mid[0] = sum_ref[ahead, low]
    next_mid[1] = sum_ref[behind, high]
    next_own[0] = sum_ref[here, low]
    next_own[1] = sum_ref[here, high]


def turn(place, own, up, down, last_up, last_down):
    rows, size = own.shape[1:]
    part = jax.ShapeDtypeStruct((2, rows // 2, size), own.dtype)
    return call(
        turn_kernel,
        "turn",
        (part,) * 4,
        [SMEM] + [VMEM] * 5,
        (place, own, up, down, last_up, last_down),
        scratch=[pltpu.VMEM(own.shape, own.dtype)],
        flops=2 * own.size,
        moved=8 * own.size,
    )


def pieces_kernel(*refs):
    out_ref = refs[-1]
    width = out_ref.shape[2]
    for side in range(2):
        own, up, down, last_up, last_down = refs[5 * side : 5 * side + 5]
        half = own.shape[1]
        for row in range(0, half, 32):
            at = pl.ds(row, 32)
            low = narrow(own[0, at], last_up[0, at], down[1, at])
            high = narrow(own[1, at], up[1, at], last_down[0, at])
            for piece in range(8):
                columns = slice(piece * width, (piece + 1) * width)
                out_ref[8 * side + piece, at] = low[:, columns]
                out_ref[8 * side + piece, pl.ds(half + row, 32)] = high[:, columns]


def make_pieces(*parts):
    rows, size = 2 * parts[0].shape[1], parts[0].shape[2]
    out = jax.ShapeDtypeStruct((16, rows, size // 8), jnp.bfloat16)
    return call(
        pieces_kernel, "pieces", out, [VMEM] * 10, parts, flops=4 * rows * size, moved=16 * rows * size
    )


CUT = 2


def begin_blocks(grads_ref, moves, sems):
    rows = grads_ref.shape[3] // CUT
    copies = [
        pltpu.make_async_copy(
            grads_ref.at[where + (pl.ds(part * rows, rows),)],
            out.at[slot, pl.ds(part * rows, rows)],
            sems.at[CUT * i + part],
        )
        for i, (where, out, slot) in enumerate(moves)
        for part in range(CUT)
    ]
    for each in copies:
        each.start()
    return copies


def steps(place_ref, which):
    return tuple(lax.rem(place_ref[which] + step, 4) for step in range(4))


def trim(index, stats_ref, out_ref):
    rows = stats_ref.shape[0]
    half = rows // 2

    def block(at):
        return pl.ds(at % 4 * rows, rows)

    out_ref[:, block(0)] = stats_ref[:, block(index)].astype(jnp.bfloat16)
    out_ref[:, block(1)] = stats_ref[:, block(index + 1)].astype(jnp.bfloat16)
    if index < 2:
        opposite = stats_ref[:, pl.ds((index + 2) * rows, half)]
    else:
        opposite = stats_ref[pl.ds(half, half), block(index + 2)].T
    out_ref[:, pl.ds(2 * rows, half)] = opposite.astype(jnp.bfloat16)


def send_kernel(place_ref, grads_ref, stats_ref, x_up, x_down, y_up, y_down, own_ref, wide_ref, trim_ref, sems, more):
    x, y = steps(place_ref, 0), steps(place_ref, 1)
    rows = wide_ref.shape[0] // 8
    parts = [pl.ds(part * rows, rows) for part in range(8)]
    stats_in = [pltpu.make_async_copy(stats_ref.at[at], wide_ref.at[at], more.at[i]) for i, at in enumerate(parts)]
    for each in stats_in:
        each.start()
    moves = []
    for i in range(2):
        moves += [
            ((0, i, x[2]), x_up, i),
            ((0, 2 + i, x[1]), x_up, 2 + i),
            ((0, 2 + i, x[2]), x_down, i),
            ((0, i, x[3]), x_down, 2 + i),
            ((1, y[2], i), y_up, i),
            ((1, y[1], 2 + i), y_up, 2 + i),
            ((1, y[2], 2 + i), y_down, i),
            ((1, y[3], i), y_down, 2 + i),
        ]
    copies = begin_blocks(grads_ref, moves, sems)
    for each in stats_in:
        each.wait()
    for index in range(4):
        pl.when(place_ref[2] == index)(functools.partial(trim, index, wide_ref, trim_ref))
    stats_out = [pltpu.make_async_copy(trim_ref.at[at], own_ref.at[at], more.at[8 + i]) for i, at in enumerate(parts)]
    for each in stats_out:
        each.start()
    for each in copies + stats_out:
        each.wait()


def send(place, grads, stats):
    payload = jax.ShapeDtypeStruct((4,) + grads.shape[3:], grads.dtype)
    rows = stats.shape[0]
    own = jax.ShapeDtypeStruct((rows, 2 * rows + rows // 2), jnp.bfloat16)
    return pl.pallas_call(
        send_kernel,
        out_shape=(payload,) * 4 + (own,),
        in_specs=[SMEM, HBM, HBM],
        out_specs=(VMEM,) * 4 + (HBM,),
        scratch_shapes=[
            pltpu.VMEM(stats.shape, stats.dtype),
            pltpu.VMEM(own.shape, own.dtype),
            pltpu.SemaphoreType.DMA((16 * CUT,)),
            pltpu.SemaphoreType.DMA((16,)),
        ],
        compiler_params=pltpu.CompilerParams(vmem_limit_bytes=48 * 2**20),
        cost_estimate=pl.CostEstimate(flops=0, bytes_accessed=2**23, transcendentals=0),
        name="send",
    )(place, grads, stats)


def keep_kernel(place_ref, grads_ref, x_mid, x_own, y_mid, y_own, sems):
    x, y = steps(place_ref, 0), steps(place_ref, 1)
    moves = []
    for i in range(2):
        moves += [
            ((0, i, x[1]), x_mid, i),
            ((0, 2 + i, x[3]), x_mid, 2 + i),
            ((1, y[1], i), y_mid, i),
            ((1, y[3], 2 + i), y_mid, 2 + i),
        ]
    for i in range(4):
        moves += [((0, i, x[0]), x_own, i), ((1, y[0], i), y_own, i)]
    for each in begin_blocks(grads_ref, moves, sems):
        each.wait()


def keep(place, grads):
    payload = jax.ShapeDtypeStruct((4,) + grads.shape[3:], grads.dtype)
    return call(
        keep_kernel,
        "keep",
        (payload,) * 4,
        [SMEM, HBM],
        (place, grads),
        scratch=[pltpu.SemaphoreType.DMA((16 * CUT,))],
        moved=2**23,
    )


def half_kernel(side, offset_ref, stats_ref, first_ref, second_ref, start_ref):
    size = first_ref.shape[0]
    slot = size // 4
    half = slot // 2

    def span(tile):
        return pl.ds(tile * slot, slot)

    def held(tile, columns):
        position = lax.rem(offset_ref[0] + (4 * side + tile), 8)
        return stats_ref[pl.ds(pl.multiple_of(position * slot, slot), slot), columns].astype(jnp.float32)

    diagonal, following, opposite = pl.ds(0, slot), pl.ds(slot, slot), pl.ds(2 * slot, half)
    total = jnp.zeros((8, slot // 2), jnp.float32)
    for tile in range(4):
        for columns, weight in ((diagonal, 1.0), (following, 2.0), (opposite, 2.0)):
            values = held(tile, columns)
            total = total + weight * lanes(values * values)
    inverse = 1.0 / jnp.sqrt(jnp.sum(total))

    row_ids = lax.broadcasted_iota(jnp.int32, (slot, slot), 0)
    col_ids = lax.broadcasted_iota(jnp.int32, (slot, slot), 1)
    eye = jnp.where(row_ids == col_ids, 1.0, 0.0).astype(jnp.float32)

    def place(row, column, normed, on_diagonal):
        start_ref[span(row), span(column)] = normed.astype(jnp.bfloat16)
        term = 1.5 * eye - 0.5 * normed if on_diagonal else -0.5 * normed
        first_ref[span(row), span(column)] = term.astype(jnp.bfloat16)

    for tile in range(4):
        after = (tile + 1) % 4
        place(tile, tile, held(tile, diagonal) * inverse, True)
        normed = held(tile, following) * inverse
        place(tile, after, normed, False)
        place(after, tile, normed.T, False)
    for tile in range(2):
        parts = [held(at, opposite) * inverse for at in (tile, tile + 2)]
        normed = jnp.concatenate(parts, axis=1)
        place(tile, tile + 2, normed, False)
        place(tile + 2, tile, normed.T, False)

    for tile in range(4):
        product = jnp.dot(start_ref[span(tile), :], first_ref[...], preferred_element_type=jnp.float32)
        second_ref[span(tile), :] = product.astype(jnp.bfloat16)


def root_kernel(first_ref, second_ref, out_ref, third_ref):
    size = out_ref.shape[0]
    slot = size // 4
    for tile in range(4):
        at = pl.ds(tile * slot, slot)
        row_ids = lax.broadcasted_iota(jnp.int32, (slot, size), 0) + tile * slot
        col_ids = lax.broadcasted_iota(jnp.int32, (slot, size), 1)
        eye = jnp.where(row_ids == col_ids, 1.0, 0.0).astype(jnp.float32)
        product = jnp.dot(first_ref[at, :], second_ref[...], preferred_element_type=jnp.float32)
        third_ref[at, :] = (1.5 * eye - 0.5 * product).astype(jnp.bfloat16)
    for tile in range(4):
        at = pl.ds(tile * slot, slot)
        product = jnp.dot(third_ref[at, :], first_ref[...], preferred_element_type=jnp.float32)
        out_ref[at, :] = product.astype(jnp.bfloat16)


def half_root(side, offset, stats):
    size = stats.shape[0] // 2
    matrix = jax.ShapeDtypeStruct((size, size), jnp.bfloat16)
    return call(
        functools.partial(half_kernel, side),
        ("left_half", "right_half")[side],
        (matrix, matrix),
        [SMEM, VMEM],
        (offset, stats),
        scratch=[pltpu.VMEM((size, size), jnp.bfloat16)],
        flops=2 * size**3,
        moved=4 * size * size,
    )


def inverse_root(first, second):
    size = first.shape[0]
    return call(
        root_kernel,
        "root",
        jax.ShapeDtypeStruct((size, size), jnp.bfloat16),
        [VMEM] * 2,
        (first, second),
        scratch=[pltpu.VMEM((size, size), jnp.bfloat16)],
        flops=4 * size**3,
        moved=6 * size * size,
    )


def lanes(squares):
    rows, columns = squares.shape
    total = jnp.sum(squares.reshape(rows // 8, 8, columns), axis=0)
    return sum(total[:, at : at + 128] for at in range(0, columns, 128))


def mix_kernel(pieces_ref, left_ref, out_ref, energy_ref, grad_ref):
    count, rows, _ = out_ref.shape
    energy = jnp.zeros(energy_ref.shape, jnp.float32)
    for piece in range(count):
        grad = narrow(pieces_ref[piece], pieces_ref[count + piece])
        grad_ref[pl.ds(piece * rows, rows), :] = grad
        wide = grad.astype(jnp.float32)
        energy = energy + lanes(wide * wide)
    energy_ref[...] = energy
    for piece in range(0, count, 2):
        product = jnp.dot(
            left_ref[pl.ds(piece * rows, 2 * rows), :], grad_ref[...], preferred_element_type=jnp.float32
        ).astype(jnp.bfloat16)
        out_ref[piece] = product[:rows]
        out_ref[piece + 1] = product[rows:]


def mix(pieces, left_root):
    _, rows, width = pieces.shape
    return call(
        mix_kernel,
        "mix",
        (jax.ShapeDtypeStruct((8, rows, width), jnp.bfloat16), jax.ShapeDtypeStruct((8, 128), jnp.float32)),
        [VMEM] * 2,
        (pieces, left_root),
        scratch=[pltpu.VMEM((8 * rows, width), jnp.bfloat16)],
        flops=2 * left_root.size * width,
        moved=2 * left_root.size,
    )


def condition_kernel(mixed_ref, right_ref, energy_ref, out_ref, totals_ref, rows_ref):
    count, _, width = mixed_ref.shape
    for piece in range(count):
        rows_ref[:, pl.ds(piece * width, width)] = mixed_ref[piece]
    total = jnp.zeros(energy_ref.shape, jnp.float32)
    for at in range(0, out_ref.shape[1], 256):
        product = jnp.dot(rows_ref[...], right_ref[:, pl.ds(at, 256)], preferred_element_type=jnp.float32)
        out_ref[:, pl.ds(at, 256)] = product
        total = total + lanes(product * product)
    totals_ref[:8] = energy_ref[...]
    totals_ref[8:] = total


def condition(mixed, right_root, energy):
    _, rows, width = mixed.shape
    size = right_root.shape[1]
    return call(
        condition_kernel,
        "condition",
        (jax.ShapeDtypeStruct((rows, size), jnp.float32), jax.ShapeDtypeStruct((16, 128), jnp.float32)),
        [VMEM] * 3,
        (mixed, right_root, energy),
        scratch=[pltpu.VMEM((rows, size), jnp.bfloat16)],
        flops=2 * rows * right_root.size,
        moved=2 * right_root.size,
    )


def finish_kernel(count, totals_ref, precond_ref, out_ref):
    grad_mean = jnp.sum(totals_ref[:8]) / count
    cond_mean = jnp.sum(totals_ref[8:]) / count
    factor = jnp.sqrt(grad_mean / (cond_mean + 1e-06))
    for row in range(0, out_ref.shape[0], 32):
        at = pl.ds(row, 32)
        out_ref[at] = precond_ref[at] * factor


def finish(totals, precond, count):
    return call(
        functools.partial(finish_kernel, count),
        "finish",
        jax.ShapeDtypeStruct(precond.shape, jnp.float32),
        [VMEM] * 2,
        (totals, precond),
        flops=precond.size,
        moved=8 * precond.size,
    )


def after(dep, *values):
    return lax.optimization_barrier((dep,) + values)[1:]


def local(grad_partial, factor_stats, owner_table):
    size = grad_partial.shape[3]
    rows_here = grad_partial.shape[2]
    owner = ("zl", "c")
    grads = grad_partial.reshape(2, 4, 4, rows_here, size)
    zh, y, x, zl, c = (lax.axis_index(axis).astype(jnp.int32) for axis in FINE)
    slot = (2 * zl + c - owner_table[0] + 8) % 4
    place = jnp.stack((x, y, slot))

    x_up, x_down, y_up, y_down, own = send(place, grads, factor_stats[0, 0])
    stats = lax.all_gather(own, owner, axis=0, tiled=True)
    x_ends = ring_first(x_up, x_down, "x")
    y_ends = ring_first(y_up, y_down, "y")
    x_mid, x_own, y_mid, y_own = keep(*after(x_up, place), grads)

    x_last = ring_first(*pass_on(x_mid, *x_ends), "x")
    y_last = ring_first(*pass_on(y_mid, *y_ends), "y")
    lower_up, lower_down, lower_mid, lower_own = turn(y[None], x_own, *x_ends, *x_last)
    lower_ends = ring_first(lower_up, lower_down, "y")
    upper_up, upper_down, upper_mid, upper_own = turn(x[None], y_own, *y_ends, *y_last)
    upper_ends = ring_first(upper_up, upper_down, "x")
    lower_last = ring_first(*pass_on(lower_mid, *lower_ends), "y")
    upper_last = ring_first(*pass_on(upper_mid, *upper_ends), "x")
    pieces = make_pieces(lower_own, *lower_ends, *lower_last, upper_own, *upper_ends, *upper_last)

    (stats,) = after(pieces, stats)
    pieces = lax.all_to_all(pieces, ("zh",) + owner, split_axis=0, concat_axis=0, tiled=True)
    left_root = inverse_root(*half_root(0, owner_table, stats))
    first, second = half_root(1, owner_table, stats)
    (pieces,) = after(second, pieces)
    mixed, energy = mix(pieces, left_root)
    (second,) = after(mixed, second)
    mixed = lax.all_to_all(mixed, owner, split_axis=0, concat_axis=0, tiled=True)
    right_root = inverse_root(first, second)
    precond, totals = condition(mixed, right_root, energy)
    totals = totals + swap(totals, "c", 1)
    totals = totals + shift(totals, "zl", 1) + shift(totals, "zl", 2) + shift(totals, "zl", 3)
    return finish(totals, precond, float(size * size))[None]


def solution(mesh):
    dp, owner = ("zh", "y", "x"), ("zl", "c")
    placed = (P(dp, None, owner, None), P(dp, owner, None, None), P(dp))
    return jax.shard_map(
        local, mesh=fine_mesh(mesh), in_specs=placed, out_specs=P(dp, owner, None), check_vma=False
    )
```

```python
import functools

import jax
import jax.numpy as jnp
from jax import lax
from jax.experimental import pallas as pl
from jax.experimental.pallas import tpu as pltpu
from jax.sharding import Mesh
from jax.sharding import PartitionSpec as P

FINE = ("zh", "y", "x", "zl", "c")


def fine_mesh(mesh):
    return Mesh(mesh.devices.reshape(2, 4, 4, 4, 2), FINE)


def shift(array, axis, step):
    size = lax.axis_size(axis)
    return lax.ppermute(array, axis, [(i, (i + step) % size) for i in range(size)])


def swap(array, axis, mask):
    size = lax.axis_size(axis)
    return lax.ppermute(array, axis, [(i, i ^ mask) for i in range(size)])


def f32sum(*terms):
    total = terms[0].astype(jnp.float32)
    for term in terms[1:]:
        total = total + term.astype(jnp.float32)
    return total


def narrow(*terms):
    return f32sum(*terms).astype(jnp.bfloat16)


VMEM = pl.BlockSpec(memory_space=pltpu.VMEM)
SMEM = pl.BlockSpec(memory_space=pltpu.SMEM)
HBM = pl.BlockSpec(memory_space=pltpu.HBM)


def call(kernel, name, out_shape, in_specs, operands, scratch=(), mib=16, flops=0, moved=0):
    outs = (VMEM,) * len(out_shape) if isinstance(out_shape, tuple) else VMEM
    return pl.pallas_call(
        kernel,
        out_shape=out_shape,
        in_specs=in_specs,
        out_specs=outs,
        scratch_shapes=list(scratch),
        compiler_params=pltpu.CompilerParams(vmem_limit_bytes=mib * 2**20),
        cost_estimate=pl.CostEstimate(flops=flops, bytes_accessed=moved, transcendentals=0),
        name=name,
    )(*operands)


def ring_first(up, down, axis):
    return shift(up, axis, 1), shift(down, axis, -1)


def pass_kernel(mid_ref, up_ref, down_ref, last_up_ref, last_down_ref):
    count, rows, _ = last_up_ref.shape
    for block in range(count):
        for row in range(0, rows, 32):
            at = pl.ds(row, 32)
            last_up_ref[block, at] = narrow(mid_ref[block, at], up_ref[block, at])
            last_down_ref[block, at] = narrow(mid_ref[count + block, at], down_ref[block, at])


def pass_on(mid, up, down):
    count = mid.shape[0] // 2
    last = jax.ShapeDtypeStruct((count,) + mid.shape[1:], mid.dtype)
    last_up, last_down = call(
        pass_kernel, "pass_on", (last, last), [VMEM] * 3, (mid, up, down), flops=mid.size, moved=6 * mid.size
    )
    return last_up, last_down


def turn_kernel(place_ref, own_ref, up_ref, down_ref, last_up_ref, last_down_ref, next_up, next_down, next_mid, next_own, sum_ref):
    rows = own_ref.shape[1]
    half = rows // 2
    for block in range(2):
        for row in range(0, rows, 32):
            at = pl.ds(row, 32)
            sum_ref[block, at] = narrow(own_ref[block, at], last_up_ref[block, at], down_ref[2 + block, at])
            sum_ref[2 + block, at] = narrow(own_ref[2 + block, at], up_ref[2 + block, at], last_down_ref[block, at])
    low, high = pl.ds(0, half), pl.ds(half, half)
    here = place_ref[0]
    ahead, across, behind = (lax.rem(here + step, 4) for step in (1, 2, 3))
    next_up[0] = sum_ref[across, low]
    next_up[1] = sum_ref[ahead, high]
    next_down[0] = sum_ref[across, high]
    next_down[1] = sum_ref[behind, low]
    next_mid[0] = sum_ref[ahead, low]
    next_mid[1] = sum_ref[behind, high]
    next_own[0] = sum_ref[here, low]
    next_own[1] = sum_ref[here, high]


def turn(place, own, up, down, last_up, last_down):
    rows, size = own.shape[1:]
    part = jax.ShapeDtypeStruct((2, rows // 2, size), own.dtype)
    return call(
        turn_kernel,
        "turn",
        (part,) * 4,
        [SMEM] + [VMEM] * 5,
        (place, own, up, down, last_up, last_down),
        scratch=[pltpu.VMEM(own.shape, own.dtype)],
        flops=2 * own.size,
        moved=8 * own.size,
    )


def pieces_kernel(*refs):
    out_ref = refs[-1]
    width = out_ref.shape[2]
    for side in range(2):
        own, up, down, last_up, last_down = refs[5 * side : 5 * side + 5]
        half = own.shape[1]
        for row in range(0, half, 32):
            at = pl.ds(row, 32)
            low = narrow(own[0, at], last_up[0, at], down[1, at])
            high = narrow(own[1, at], up[1, at], last_down[0, at])
            for piece in range(8):
                columns = slice(piece * width, (piece + 1) * width)
                out_ref[8 * side + piece, at] = low[:, columns]
                out_ref[8 * side + piece, pl.ds(half + row, 32)] = high[:, columns]


def make_pieces(*parts):
    rows, size = 2 * parts[0].shape[1], parts[0].shape[2]
    out = jax.ShapeDtypeStruct((16, rows, size // 8), jnp.bfloat16)
    return call(
        pieces_kernel, "pieces", out, [VMEM] * 10, parts, flops=4 * rows * size, moved=16 * rows * size
    )


CUT = 4


def copy_blocks(grads_ref, moves, sems):
    rows = grads_ref.shape[3] // CUT
    copies = [
        pltpu.make_async_copy(
            grads_ref.at[where + (pl.ds(part * rows, rows),)],
            out.at[slot, pl.ds(part * rows, rows)],
            sems.at[CUT * i + part],
        )
        for i, (where, out, slot) in enumerate(moves)
        for part in range(CUT)
    ]
    for each in copies:
        each.start()
    for each in copies:
        each.wait()


def steps(place_ref, which):
    return tuple(lax.rem(place_ref[which] + step, 4) for step in range(4))


def trim_kernel(index_ref, stats_ref, out_ref):
    rows = stats_ref.shape[0]
    half = rows // 2

    def block(at):
        return pl.ds(at % 4 * rows, rows)

    for index in range(4):

        @pl.when(index_ref[0] == index)
        def _():
            out_ref[:, block(0)] = stats_ref[:, block(index)].astype(jnp.bfloat16)
            out_ref[:, block(1)] = stats_ref[:, block(index + 1)].astype(jnp.bfloat16)
            if index < 2:
                opposite = stats_ref[:, pl.ds((index + 2) * rows, half)]
            else:
                opposite = stats_ref[pl.ds(half, half), block(index + 2)].T
            out_ref[:, pl.ds(2 * rows, half)] = opposite.astype(jnp.bfloat16)


def trim(index, stats):
    rows = stats.shape[0]
    out = jax.ShapeDtypeStruct((rows, 2 * rows + rows // 2), jnp.bfloat16)
    return call(trim_kernel, "trim", out, [SMEM, VMEM], (index, stats), flops=stats.size, moved=6 * stats.size)


def send_kernel(place_ref, grads_ref, x_up, x_down, y_up, y_down, sems):
    x, y = steps(place_ref, 0), steps(place_ref, 1)
    moves = []
    for i in range(2):
        moves += [
            ((0, i, x[2]), x_up, i),
            ((0, 2 + i, x[1]), x_up, 2 + i),
            ((0, 2 + i, x[2]), x_down, i),
            ((0, i, x[3]), x_down, 2 + i),
            ((1, y[2], i), y_up, i),
            ((1, y[1], 2 + i), y_up, 2 + i),
            ((1, y[2], 2 + i), y_down, i),
            ((1, y[3], i), y_down, 2 + i),
        ]
    copy_blocks(grads_ref, moves, sems)


def keep_kernel(place_ref, grads_ref, x_mid, x_own, y_mid, y_own, sems):
    x, y = steps(place_ref, 0), steps(place_ref, 1)
    moves = []
    for i in range(2):
        moves += [
            ((0, i, x[1]), x_mid, i),
            ((0, 2 + i, x[3]), x_mid, 2 + i),
            ((1, y[1], i), y_mid, i),
            ((1, y[3], 2 + i), y_mid, 2 + i),
        ]
    for i in range(4):
        moves += [((0, i, x[0]), x_own, i), ((1, y[0], i), y_own, i)]
    copy_blocks(grads_ref, moves, sems)


def pack(kernel, mib, place, grads):
    payload = jax.ShapeDtypeStruct((4,) + grads.shape[3:], grads.dtype)
    return call(
        kernel,
        kernel.__name__[:4],
        (payload,) * 4,
        [SMEM, HBM],
        (place, grads),
        scratch=[pltpu.SemaphoreType.DMA((16 * CUT,))],
        mib=mib,
        moved=2**23,
    )


def root_kernel(side, where_ref, *refs):
    given, (out_ref, slots_ref, start_ref, first_ref, second_ref, third_ref) = refs[:8], refs[8:]
    size = out_ref.shape[0]
    slot = size // 4
    half = slot // 2
    offset, zl, c = where_ref[0], where_ref[1], where_ref[2]

    def span(tile):
        return pl.ds(tile * slot, slot)

    for tile in range(4):
        position = lax.rem(offset + (4 * side + tile), 8)
        back = lax.rem(zl + 4 - lax.div(position, 2), 4)
        source = 2 * back + lax.rem(position + c, 2)
        for i, ref in enumerate(given):

            @pl.when(source == i)
            def _():
                slots_ref[tile] = ref[...]

    total = jnp.zeros((8, slot // 2), jnp.float32)
    for tile in range(4):
        values = slots_ref[tile].astype(jnp.float32)
        squares = values * values
        total = total + lanes(squares[:, :slot]) + 2.0 * lanes(squares[:, slot:])
    inverse = 1.0 / jnp.sqrt(jnp.sum(total))

    row_ids = lax.broadcasted_iota(jnp.int32, (slot, slot), 0)
    col_ids = lax.broadcasted_iota(jnp.int32, (slot, slot), 1)
    eye = jnp.where(row_ids == col_ids, 1.0, 0.0).astype(jnp.float32)

    def place(row, column, normed, diagonal):
        start_ref[span(row), span(column)] = normed.astype(jnp.bfloat16)
        term = 1.5 * eye - 0.5 * normed if diagonal else -0.5 * normed
        first_ref[span(row), span(column)] = term.astype(jnp.bfloat16)

    for tile in range(4):
        after = (tile + 1) % 4
        place(tile, tile, slots_ref[tile, :, :slot].astype(jnp.float32) * inverse, True)
        normed = slots_ref[tile, :, slot : 2 * slot].astype(jnp.float32) * inverse
        place(tile, after, normed, False)
        place(after, tile, normed.T, False)
    for tile in range(2):
        parts = [slots_ref[at, :, 2 * slot :].astype(jnp.float32) * inverse for at in (tile, tile + 2)]
        normed = jnp.concatenate(parts, axis=1)
        place(tile, tile + 2, normed, False)
        place(tile + 2, tile, normed.T, False)

    def eye_rows(tile):
        row_ids = lax.broadcasted_iota(jnp.int32, (slot, size), 0) + tile * slot
        col_ids = lax.broadcasted_iota(jnp.int32, (slot, size), 1)
        return jnp.where(row_ids == col_ids, 1.0, 0.0).astype(jnp.float32)

    for tile in range(4):
        product = jnp.dot(start_ref[span(tile), :], first_ref[...], preferred_element_type=jnp.float32)
        second_ref[span(tile), :] = product.astype(jnp.bfloat16)
    for tile in range(4):
        product = jnp.dot(first_ref[span(tile), :], second_ref[...], preferred_element_type=jnp.float32)
        third_ref[span(tile), :] = (1.5 * eye_rows(tile) - 0.5 * product).astype(jnp.bfloat16)
    for tile in range(4):
        product = jnp.dot(third_ref[span(tile), :], first_ref[...], preferred_element_type=jnp.float32)
        out_ref[span(tile), :] = product.astype(jnp.bfloat16)


def inverse_root(side, where, slots):
    rows, kept = slots[0].shape
    size = 4 * rows
    return call(
        functools.partial(root_kernel, side),
        ("left_root", "right_root")[side],
        jax.ShapeDtypeStruct((size, size), jnp.bfloat16),
        [SMEM] + [VMEM] * 8,
        (where,) + slots,
        scratch=[pltpu.VMEM((4, rows, kept), jnp.bfloat16)] + [pltpu.VMEM((size, size), jnp.bfloat16)] * 4,
        flops=6 * size**3,
        moved=4 * size * size,
    )


def lanes(squares):
    rows, columns = squares.shape
    total = jnp.sum(squares.reshape(rows // 8, 8, columns), axis=0)
    return sum(total[:, at : at + 128] for at in range(0, columns, 128))


def mix_kernel(pieces_ref, left_ref, out_ref, energy_ref, grad_ref):
    count, rows, _ = out_ref.shape
    energy = jnp.zeros(energy_ref.shape, jnp.float32)
    for piece in range(count):
        grad = narrow(pieces_ref[piece], pieces_ref[count + piece])
        grad_ref[pl.ds(piece * rows, rows), :] = grad
        wide = grad.astype(jnp.float32)
        energy = energy + lanes(wide * wide)
    energy_ref[...] = energy
    for piece in range(0, count, 2):
        product = jnp.dot(
            left_ref[pl.ds(piece * rows, 2 * rows), :], grad_ref[...], preferred_element_type=jnp.float32
        ).astype(jnp.bfloat16)
        out_ref[piece] = product[:rows]
        out_ref[piece + 1] = product[rows:]


def mix(pieces, left_root):
    _, rows, width = pieces.shape
    return call(
        mix_kernel,
        "mix",
        (jax.ShapeDtypeStruct((8, rows, width), jnp.bfloat16), jax.ShapeDtypeStruct((8, 128), jnp.float32)),
        [VMEM] * 2,
        (pieces, left_root),
        scratch=[pltpu.VMEM((8 * rows, width), jnp.bfloat16)],
        flops=2 * left_root.size * width,
        moved=2 * left_root.size,
    )


def condition_kernel(mixed_ref, right_ref, energy_ref, out_ref, totals_ref, rows_ref):
    count, _, width = mixed_ref.shape
    for piece in range(count):
        rows_ref[:, pl.ds(piece * width, width)] = mixed_ref[piece]
    total = jnp.zeros(energy_ref.shape, jnp.float32)
    for at in range(0, out_ref.shape[1], 256):
        product = jnp.dot(rows_ref[...], right_ref[:, pl.ds(at, 256)], preferred_element_type=jnp.float32)
        out_ref[:, pl.ds(at, 256)] = product
        total = total + lanes(product * product)
    totals_ref[:8] = energy_ref[...]
    totals_ref[8:] = total


def condition(mixed, right_root, energy):
    _, rows, width = mixed.shape
    size = right_root.shape[1]
    return call(
        condition_kernel,
        "condition",
        (jax.ShapeDtypeStruct((rows, size), jnp.float32), jax.ShapeDtypeStruct((16, 128), jnp.float32)),
        [VMEM] * 3,
        (mixed, right_root, energy),
        scratch=[pltpu.VMEM((rows, size), jnp.bfloat16)],
        flops=2 * rows * right_root.size,
        moved=2 * right_root.size,
    )


def finish_kernel(count, totals_ref, precond_ref, out_ref):
    grad_mean = jnp.sum(totals_ref[:8]) / count
    cond_mean = jnp.sum(totals_ref[8:]) / count
    factor = jnp.sqrt(grad_mean / (cond_mean + 1e-06))
    for row in range(0, out_ref.shape[0], 32):
        at = pl.ds(row, 32)
        out_ref[at] = precond_ref[at] * factor


def finish(totals, precond, count):
    return call(
        functools.partial(finish_kernel, count),
        "finish",
        jax.ShapeDtypeStruct(precond.shape, jnp.float32),
        [VMEM] * 2,
        (totals, precond),
        flops=precond.size,
        moved=8 * precond.size,
    )


def after(dep, *values):
    return lax.optimization_barrier((dep,) + values)[1:]


def local(grad_partial, factor_stats, owner_table):
    size = grad_partial.shape[3]
    rows_here = grad_partial.shape[2]
    owner = ("zl", "c")
    grads = grad_partial.reshape(2, 4, 4, rows_here, size)
    zh, y, x, zl, c = (lax.axis_index(axis).astype(jnp.int32) for axis in FINE)
    place = jnp.stack((x, y))

    x_up, x_down, y_up, y_down = pack(send_kernel, 50, place, grads)
    x_ends = ring_first(x_up, x_down, "x")
    y_ends = ring_first(y_up, y_down, "y")

    place, table = after(x_up, place, owner_table)
    near = [trim((2 * zl + c - table + 8) % 4, factor_stats[0, 0])]
    near.append(shift(near[0], "zl", 1))
    x_mid, x_own, y_mid, y_own = pack(keep_kernel, 16, place, grads)
    near.append(shift(*after(x_mid, near[1]), "zl", 1))
    near.append(shift(near[2], "zl", 1))
    (x_mid,) = after(near[2], x_mid)
    x_last = pass_on(x_mid, *x_ends)
    y_last = pass_on(y_mid, *y_ends)
    far = [swap(each, "c", 1) for each in near[:3]]
    far.append(swap(*after(x_last[0], near[3]), "c", 1))
    slots = tuple(each for pair in zip(near, far) for each in pair)
    where = jnp.stack((table[0], zl, c))

    x_last = ring_first(*x_last, "x")
    y_last = ring_first(*y_last, "y")

    lower_up, lower_down, lower_mid, lower_own = turn(y[None], x_own, *x_ends, *x_last)
    lower_ends = ring_first(lower_up, lower_down, "y")
    upper_up, upper_down, upper_mid, upper_own = turn(x[None], y_own, *y_ends, *y_last)
    upper_ends = ring_first(upper_up, upper_down, "x")
    lower_last = ring_first(*pass_on(lower_mid, *lower_ends), "y")
    upper_last = ring_first(*pass_on(upper_mid, *upper_ends), "x")
    pieces = make_pieces(lower_own, *lower_ends, *lower_last, upper_own, *upper_ends, *upper_last)

    slots = after(pieces, *slots)
    pieces = lax.all_to_all(pieces, ("zh",) + owner, split_axis=0, concat_axis=0, tiled=True)
    left_root = inverse_root(0, where, slots)
    mixed, energy = mix(pieces, left_root)
    right_root = inverse_root(1, where, after(mixed, *slots))
    mixed = lax.all_to_all(mixed, owner, split_axis=0, concat_axis=0, tiled=True)
    precond, totals = condition(mixed, right_root, energy)
    totals = totals + swap(totals, "c", 1)
    totals = totals + shift(totals, "zl", 1) + shift(totals, "zl", 2) + shift(totals, "zl", 3)
    return finish(totals, precond, float(size * size))[None]


def solution(mesh):
    dp, owner = ("zh", "y", "x"), ("zl", "c")
    placed = (P(dp, None, owner, None), P(dp, owner, None, None), P(dp))
    return jax.shard_map(
        local, mesh=fine_mesh(mesh), in_specs=placed, out_specs=P(dp, owner, None), check_vma=False
    )
```

```python
import functools

import jax
import jax.numpy as jnp
from jax import lax
from jax.experimental import pallas as pl
from jax.experimental.pallas import tpu as pltpu
from jax.sharding import Mesh
from jax.sharding import PartitionSpec as P

FINE = ("zh", "y", "x", "zl", "c")


def fine_mesh(mesh):
    return Mesh(mesh.devices.reshape(2, 4, 4, 4, 2), FINE)


def shift(array, axis, step):
    size = lax.axis_size(axis)
    return lax.ppermute(array, axis, [(i, (i + step) % size) for i in range(size)])


def swap(array, axis, mask):
    size = lax.axis_size(axis)
    return lax.ppermute(array, axis, [(i, i ^ mask) for i in range(size)])


def f32sum(*terms):
    total = terms[0].astype(jnp.float32)
    for term in terms[1:]:
        total = total + term.astype(jnp.float32)
    return total


def narrow(*terms):
    return f32sum(*terms).astype(jnp.bfloat16)


VMEM = pl.BlockSpec(memory_space=pltpu.VMEM)
SMEM = pl.BlockSpec(memory_space=pltpu.SMEM)
HBM = pl.BlockSpec(memory_space=pltpu.HBM)


def call(kernel, name, out_shape, in_specs, operands, scratch=(), mib=16, flops=0, moved=0):
    outs = (VMEM,) * len(out_shape) if isinstance(out_shape, tuple) else VMEM
    return pl.pallas_call(
        kernel,
        out_shape=out_shape,
        in_specs=in_specs,
        out_specs=outs,
        scratch_shapes=list(scratch),
        compiler_params=pltpu.CompilerParams(vmem_limit_bytes=mib * 2**20),
        cost_estimate=pl.CostEstimate(flops=flops, bytes_accessed=moved, transcendentals=0),
        name=name,
    )(*operands)


def ring_first(up, down, axis):
    return shift(up, axis, 1), shift(down, axis, -1)


def pass_kernel(mid_ref, up_ref, down_ref, last_up_ref, last_down_ref):
    count, rows, _ = last_up_ref.shape
    for block in range(count):
        for row in range(0, rows, 32):
            at = pl.ds(row, 32)
            last_up_ref[block, at] = narrow(mid_ref[block, at], up_ref[block, at])
            last_down_ref[block, at] = narrow(mid_ref[count + block, at], down_ref[block, at])


def pass_on(mid, up, down):
    count = mid.shape[0] // 2
    last = jax.ShapeDtypeStruct((count,) + mid.shape[1:], mid.dtype)
    last_up, last_down = call(
        pass_kernel, "pass_on", (last, last), [VMEM] * 3, (mid, up, down), flops=mid.size, moved=6 * mid.size
    )
    return last_up, last_down


def turn_kernel(place_ref, own_ref, up_ref, down_ref, last_up_ref, last_down_ref, next_up, next_down, next_mid, next_own, sum_ref):
    rows = own_ref.shape[1]
    half = rows // 2
    for block in range(2):
        for row in range(0, rows, 32):
            at = pl.ds(row, 32)
            sum_ref[block, at] = narrow(own_ref[block, at], last_up_ref[block, at], down_ref[2 + block, at])
            sum_ref[2 + block, at] = narrow(own_ref[2 + block, at], up_ref[2 + block, at], last_down_ref[block, at])
    low, high = pl.ds(0, half), pl.ds(half, half)
    here = place_ref[0]
    ahead, across, behind = (lax.rem(here + step, 4) for step in (1, 2, 3))
    next_up[0] = sum_ref[across, low]
    next_up[1] = sum_ref[ahead, high]
    next_down[0] = sum_ref[across, high]
    next_down[1] = sum_ref[behind, low]
    next_mid[0] = sum_ref[ahead, low]
    next_mid[1] = sum_ref[behind, high]
    next_own[0] = sum_ref[here, low]
    next_own[1] = sum_ref[here, high]


def turn(place, own, up, down, last_up, last_down):
    rows, size = own.shape[1:]
    part = jax.ShapeDtypeStruct((2, rows // 2, size), own.dtype)
    return call(
        turn_kernel,
        "turn",
        (part,) * 4,
        [SMEM] + [VMEM] * 5,
        (place, own, up, down, last_up, last_down),
        scratch=[pltpu.VMEM(own.shape, own.dtype)],
        flops=2 * own.size,
        moved=8 * own.size,
    )


def pieces_kernel(*refs):
    out_ref = refs[-1]
    width = out_ref.shape[2]
    for side in range(2):
        own, up, down, last_up, last_down = refs[5 * side : 5 * side + 5]
        half = own.shape[1]
        for row in range(0, half, 32):
            at = pl.ds(row, 32)
            low = narrow(own[0, at], last_up[0, at], down[1, at])
            high = narrow(own[1, at], up[1, at], last_down[0, at])
            for piece in range(8):
                columns = slice(piece * width, (piece + 1) * width)
                out_ref[8 * side + piece, at] = low[:, columns]
                out_ref[8 * side + piece, pl.ds(half + row, 32)] = high[:, columns]


def make_pieces(*parts):
    rows, size = 2 * parts[0].shape[1], parts[0].shape[2]
    out = jax.ShapeDtypeStruct((16, rows, size // 8), jnp.bfloat16)
    return call(
        pieces_kernel, "pieces", out, [VMEM] * 10, parts, flops=4 * rows * size, moved=16 * rows * size
    )


def copy_blocks(grads_ref, moves, cut, sems):
    rows = grads_ref.shape[3] // cut
    copies = [
        pltpu.make_async_copy(
            grads_ref.at[where + (pl.ds(part * rows, rows),)],
            out.at[slot, pl.ds(part * rows, rows)],
            sems.at[cut * i + part],
        )
        for i, (where, out, slot) in enumerate(moves)
        for part in range(cut)
    ]
    for each in copies:
        each.start()
    for each in copies:
        each.wait()


def steps(place_ref, which):
    return tuple(lax.rem(place_ref[which] + step, 4) for step in range(4))


def trim_kernel(index_ref, stats_ref, out_ref):
    rows = stats_ref.shape[0]
    half = rows // 2

    def block(at):
        return pl.ds(at % 4 * rows, rows)

    for index in range(4):

        @pl.when(index_ref[0] == index)
        def _():
            out_ref[:, block(0)] = stats_ref[:, block(index)].astype(jnp.bfloat16)
            out_ref[:, block(1)] = stats_ref[:, block(index + 1)].astype(jnp.bfloat16)
            if index < 2:
                opposite = stats_ref[:, pl.ds((index + 2) * rows, half)]
            else:
                opposite = stats_ref[pl.ds(half, half), block(index + 2)].T
            out_ref[:, pl.ds(2 * rows, half)] = opposite.astype(jnp.bfloat16)


def trim(index, stats):
    rows = stats.shape[0]
    out = jax.ShapeDtypeStruct((rows, 2 * rows + rows // 2), jnp.bfloat16)
    return call(trim_kernel, "trim", out, [SMEM, VMEM], (index, stats), flops=stats.size, moved=6 * stats.size)


def send_kernel(place_ref, grads_ref, x_up, x_down, y_up, y_down, sems):
    x, y = steps(place_ref, 0), steps(place_ref, 1)
    moves = []
    for i in range(2):
        moves += [
            ((0, i, x[2]), x_up, i),
            ((0, 2 + i, x[1]), x_up, 2 + i),
            ((0, 2 + i, x[2]), x_down, i),
            ((0, i, x[3]), x_down, 2 + i),
            ((1, y[2], i), y_up, i),
            ((1, y[1], 2 + i), y_up, 2 + i),
            ((1, y[2], 2 + i), y_down, i),
            ((1, y[3], i), y_down, 2 + i),
        ]
    copy_blocks(grads_ref, moves, 4, sems)


def keep_kernel(place_ref, grads_ref, x_mid, x_own, y_mid, y_own, sems):
    x, y = steps(place_ref, 0), steps(place_ref, 1)
    moves = []
    for i in range(2):
        moves += [
            ((0, i, x[1]), x_mid, i),
            ((0, 2 + i, x[3]), x_mid, 2 + i),
            ((1, y[1], i), y_mid, i),
            ((1, y[3], 2 + i), y_mid, 2 + i),
        ]
    for i in range(4):
        moves += [((0, i, x[0]), x_own, i), ((1, y[0], i), y_own, i)]
    copy_blocks(grads_ref, moves, 1, sems)


def pack(kernel, mib, place, grads):
    payload = jax.ShapeDtypeStruct((4,) + grads.shape[3:], grads.dtype)
    return call(
        kernel,
        kernel.__name__[:4],
        (payload,) * 4,
        [SMEM, HBM],
        (place, grads),
        scratch=[pltpu.SemaphoreType.DMA((64,))],
        mib=mib,
        moved=2**23,
    )


def root_kernel(where_ref, *refs):
    given, (out_ref, slots_ref, start_ref, first_ref, second_ref, third_ref) = refs[:8], refs[8:]
    size = out_ref.shape[0]
    slot = size // 4
    half = slot // 2
    offset, zl, c = where_ref[0], where_ref[1], where_ref[2]

    def span(tile):
        return pl.ds(tile * slot, slot)

    for tile in range(4):
        position = lax.rem(offset + tile, 8)
        back = lax.rem(zl + 4 - lax.div(position, 2), 4)
        source = 2 * back + lax.rem(position + c, 2)
        for i, ref in enumerate(given):

            @pl.when(source == i)
            def _():
                slots_ref[tile] = ref[...]

    total = jnp.zeros((8, slot // 2), jnp.float32)
    for tile in range(4):
        values = slots_ref[tile].astype(jnp.float32)
        squares = values * values
        total = total + lanes(squares[:, :slot]) + 2.0 * lanes(squares[:, slot:])
    inverse = 1.0 / jnp.sqrt(jnp.sum(total))

    row_ids = lax.broadcasted_iota(jnp.int32, (slot, slot), 0)
    col_ids = lax.broadcasted_iota(jnp.int32, (slot, slot), 1)
    eye = jnp.where(row_ids == col_ids, 1.0, 0.0).astype(jnp.float32)

    def place(row, column, normed, diagonal):
        start_ref[span(row), span(column)] = normed.astype(jnp.bfloat16)
        term = 1.5 * eye - 0.5 * normed if diagonal else -0.5 * normed
        first_ref[span(row), span(column)] = term.astype(jnp.bfloat16)

    for tile in range(4):
        after = (tile + 1) % 4
        place(tile, tile, slots_ref[tile, :, :slot].astype(jnp.float32) * inverse, True)
        normed = slots_ref[tile, :, slot : 2 * slot].astype(jnp.float32) * inverse
        place(tile, after, normed, False)
        place(after, tile, normed.T, False)
    for tile in range(2):
        parts = [slots_ref[at, :, 2 * slot :].astype(jnp.float32) * inverse for at in (tile, tile + 2)]
        normed = jnp.concatenate(parts, axis=1)
        place(tile, tile + 2, normed, False)
        place(tile + 2, tile, normed.T, False)

    def eye_rows(tile):
        row_ids = lax.broadcasted_iota(jnp.int32, (slot, size), 0) + tile * slot
        col_ids = lax.broadcasted_iota(jnp.int32, (slot, size), 1)
        return jnp.where(row_ids == col_ids, 1.0, 0.0).astype(jnp.float32)

    for tile in range(4):
        product = jnp.dot(start_ref[span(tile), :], first_ref[...], preferred_element_type=jnp.float32)
        second_ref[span(tile), :] = product.astype(jnp.bfloat16)
    for tile in range(4):
        product = jnp.dot(first_ref[span(tile), :], second_ref[...], preferred_element_type=jnp.float32)
        third_ref[span(tile), :] = (1.5 * eye_rows(tile) - 0.5 * product).astype(jnp.bfloat16)
    for tile in range(4):
        product = jnp.dot(third_ref[span(tile), :], first_ref[...], preferred_element_type=jnp.float32)
        out_ref[span(tile), :] = product.astype(jnp.bfloat16)


def left_inverse_root(where, slots):
    rows, kept = slots[0].shape
    size = 4 * rows
    return call(
        root_kernel,
        "left_root",
        jax.ShapeDtypeStruct((size, size), jnp.bfloat16),
        [SMEM] + [VMEM] * 8,
        (where,) + slots,
        scratch=[pltpu.VMEM((4, rows, kept), jnp.bfloat16)] + [pltpu.VMEM((size, size), jnp.bfloat16)] * 4,
        flops=6 * size**3,
        moved=4 * size * size,
    )


def base_kernel(where_ref, *refs):
    given, (first_ref, diagonal_ref, slots_ref) = refs[:8], refs[8:]
    size = first_ref.shape[0]
    slot = size // 4
    half = slot // 2
    offset, zl, c = where_ref[0], where_ref[1], where_ref[2]

    def span(tile):
        return pl.ds(tile * slot, slot)

    for tile in range(4):
        position = lax.rem(offset + (4 + tile), 8)
        back = lax.rem(zl + 4 - lax.div(position, 2), 4)
        source = 2 * back + lax.rem(position + c, 2)
        for i, ref in enumerate(given):

            @pl.when(source == i)
            def _():
                slots_ref[tile] = ref[...]

    total = jnp.zeros((8, slot // 2), jnp.float32)
    for tile in range(4):
        values = slots_ref[tile].astype(jnp.float32)
        squares = values * values
        total = total + lanes(squares[:, :slot]) + 2.0 * lanes(squares[:, slot:])
    inverse = 1.0 / jnp.sqrt(jnp.sum(total))

    row_ids = lax.broadcasted_iota(jnp.int32, (slot, slot), 0)
    col_ids = lax.broadcasted_iota(jnp.int32, (slot, slot), 1)
    eye = jnp.where(row_ids == col_ids, 1.0, 0.0).astype(jnp.float32)

    def place(row, column, normed):
        first_ref[span(row), span(column)] = (-0.5 * normed).astype(jnp.bfloat16)

    for tile in range(4):
        following = (tile + 1) % 4
        normed = slots_ref[tile, :, :slot].astype(jnp.float32) * inverse
        first = (1.5 * eye - 0.5 * normed).astype(jnp.bfloat16)
        first_ref[span(tile), span(tile)] = first
        start = normed.astype(jnp.bfloat16).astype(jnp.float32)
        both = eye * (start + 2.0 * first.astype(jnp.float32))
        row = jnp.sum(both, axis=0, keepdims=True)
        diagonal_ref[:, span(tile)] = jnp.broadcast_to(row, (diagonal_ref.shape[0], slot))
        normed = slots_ref[tile, :, slot : 2 * slot].astype(jnp.float32) * inverse
        place(tile, following, normed)
        place(following, tile, normed.T)
    for tile in range(2):
        parts = [slots_ref[at, :, 2 * slot :].astype(jnp.float32) * inverse for at in (tile, tile + 2)]
        normed = jnp.concatenate(parts, axis=1)
        place(tile, tile + 2, normed)
        place(tile + 2, tile, normed.T)


def right_base(where, slots):
    rows, kept = slots[0].shape
    size = 4 * rows
    return call(
        base_kernel,
        "right_base",
        (
            jax.ShapeDtypeStruct((size, size), jnp.bfloat16),
            jax.ShapeDtypeStruct((8, size), jnp.float32),
        ),
        [SMEM] + [VMEM] * 8,
        (where,) + slots,
        scratch=[pltpu.VMEM((4, rows, kept), jnp.bfloat16)],
        flops=4 * size * size,
        moved=4 * size * size,
    )


def lanes(squares):
    rows, columns = squares.shape
    total = jnp.sum(squares.reshape(rows // 8, 8, columns), axis=0)
    return sum(total[:, at : at + 128] for at in range(0, columns, 128))


def mix_kernel(pieces_ref, left_ref, out_ref, energy_ref, grad_ref):
    count, rows, _ = out_ref.shape
    energy = jnp.zeros(energy_ref.shape, jnp.float32)
    for piece in range(count):
        grad = narrow(pieces_ref[piece], pieces_ref[count + piece])
        grad_ref[pl.ds(piece * rows, rows), :] = grad
        wide = grad.astype(jnp.float32)
        energy = energy + lanes(wide * wide)
    energy_ref[...] = energy
    for piece in range(0, count, 2):
        product = jnp.dot(
            left_ref[pl.ds(piece * rows, 2 * rows), :], grad_ref[...], preferred_element_type=jnp.float32
        ).astype(jnp.bfloat16)
        out_ref[piece] = product[:rows]
        out_ref[piece + 1] = product[rows:]


def mix(pieces, left_root):
    _, rows, width = pieces.shape
    return call(
        mix_kernel,
        "mix",
        (jax.ShapeDtypeStruct((8, rows, width), jnp.bfloat16), jax.ShapeDtypeStruct((8, 128), jnp.float32)),
        [VMEM] * 2,
        (pieces, left_root),
        scratch=[pltpu.VMEM((8 * rows, width), jnp.bfloat16)],
        flops=2 * left_root.size * width,
        moved=2 * left_root.size,
    )


def condition_kernel(mixed_ref, first_ref, diagonal_ref, energy_ref, out_ref, totals_ref, wide_ref, even_ref, odd_ref):
    count, _, width = mixed_ref.shape
    for piece in range(count):
        odd_ref[:, pl.ds(piece * width, width)] = mixed_ref[piece]

    def products(slab_ref):
        for column in range(0, out_ref.shape[1], 2 * width):
            at = pl.ds(column, 2 * width)
            yield at, jnp.dot(slab_ref[...], first_ref[:, at], preferred_element_type=jnp.float32)

    for at, product in products(odd_ref):
        wide_ref[:, at] = product
        even_ref[:, at] = product.astype(jnp.bfloat16)
    for at, product in products(even_ref):
        odd_ref[:, at] = product.astype(jnp.bfloat16)
    for at, product in products(odd_ref):
        started = diagonal_ref[:1, at] * odd_ref[:, at].astype(jnp.float32) - 2.0 * product
        even_ref[:, at] = started.astype(jnp.bfloat16)
    total = jnp.zeros(energy_ref.shape, jnp.float32)
    for at, product in products(even_ref):
        precond = 1.5 * wide_ref[:, at] - 0.5 * product
        out_ref[:, at] = precond
        total = total + lanes(precond * precond)
    totals_ref[:8] = energy_ref[...]
    totals_ref[8:] = total


def condition(mixed, first, diagonal, energy):
    _, rows, width = mixed.shape
    slab = (rows, 8 * width)
    return call(
        condition_kernel,
        "condition",
        (jax.ShapeDtypeStruct(slab, jnp.float32), jax.ShapeDtypeStruct((16, 128), jnp.float32)),
        [VMEM] * 4,
        (mixed, first, diagonal, energy),
        scratch=[pltpu.VMEM(slab, jnp.float32), pltpu.VMEM(slab, jnp.bfloat16), pltpu.VMEM(slab, jnp.bfloat16)],
        flops=8 * rows * first.size,
        moved=2 * first.size,
    )


def finish_kernel(count, totals_ref, precond_ref, out_ref):
    grad_mean = jnp.sum(totals_ref[:8]) / count
    cond_mean = jnp.sum(totals_ref[8:]) / count
    factor = jnp.sqrt(grad_mean / (cond_mean + 1e-06))
    for row in range(0, out_ref.shape[0], 32):
        at = pl.ds(row, 32)
        out_ref[at] = precond_ref[at] * factor


def finish(totals, precond, count):
    return call(
        functools.partial(finish_kernel, count),
        "finish",
        jax.ShapeDtypeStruct(precond.shape, jnp.float32),
        [VMEM] * 2,
        (totals, precond),
        flops=precond.size,
        moved=8 * precond.size,
    )


def after(dep, *values):
    return lax.optimization_barrier((dep,) + values)[1:]


def local(grad_partial, factor_stats, owner_table):
    size = grad_partial.shape[3]
    rows_here = grad_partial.shape[2]
    owner = ("zl", "c")
    grads = grad_partial.reshape(2, 4, 4, rows_here, size)
    zh, y, x, zl, c = (lax.axis_index(axis).astype(jnp.int32) for axis in FINE)
    place = jnp.stack((x, y))

    x_up, x_down, y_up, y_down = pack(send_kernel, 48, place, grads)
    x_ends = ring_first(x_up, x_down, "x")
    y_ends = ring_first(y_up, y_down, "y")

    place, table = after(x_up, place, owner_table)
    near = [trim((2 * zl + c - table + 8) % 4, factor_stats[0, 0])]
    near.append(shift(near[0], "zl", 1))
    x_mid, x_own, y_mid, y_own = pack(keep_kernel, 16, place, grads)
    near.append(shift(*after(x_mid, near[1]), "zl", 1))
    near.append(shift(near[2], "zl", 1))
    (x_mid,) = after(near[2], x_mid)
    x_last = pass_on(x_mid, *x_ends)
    y_last = pass_on(y_mid, *y_ends)
    far = [swap(each, "c", 1) for each in near[:3]]
    far.append(swap(*after(x_last[0], near[3]), "c", 1))
    slots = tuple(each for pair in zip(near, far) for each in pair)
    where = jnp.stack((table[0], zl, c))

    x_last = ring_first(*x_last, "x")
    y_last = ring_first(*y_last, "y")

    lower_up, lower_down, lower_mid, lower_own = turn(y[None], x_own, *x_ends, *x_last)
    lower_ends = ring_first(lower_up, lower_down, "y")
    upper_up, upper_down, upper_mid, upper_own = turn(x[None], y_own, *y_ends, *y_last)
    upper_ends = ring_first(upper_up, upper_down, "x")
    lower_last = ring_first(*pass_on(lower_mid, *lower_ends), "y")
    upper_last = ring_first(*pass_on(upper_mid, *upper_ends), "x")
    pieces = make_pieces(lower_own, *lower_ends, *lower_last, upper_own, *upper_ends, *upper_last)

    slots = after(pieces, *slots)
    pieces = lax.all_to_all(pieces, ("zh",) + owner, split_axis=0, concat_axis=0, tiled=True)
    mixed, energy = mix(pieces, left_inverse_root(where, slots))
    right = right_base(where, after(mixed, *slots))
    mixed = lax.all_to_all(mixed, owner, split_axis=0, concat_axis=0, tiled=True)
    precond, totals = condition(mixed, *right, energy)
    totals = totals + swap(totals, "c", 1)
    totals = totals + shift(totals, "zl", 1) + shift(totals, "zl", 2) + shift(totals, "zl", 3)
    return finish(totals, precond, float(size * size))[None]


def solution(mesh):
    dp, owner = ("zh", "y", "x"), ("zl", "c")
    placed = (P(dp, None, owner, None), P(dp, owner, None, None), P(dp))
    return jax.shard_map(
        local, mesh=fine_mesh(mesh), in_specs=placed, out_specs=P(dp, owner, None), check_vma=False
    )
```

```python
import functools

import jax
import jax.numpy as jnp
from jax import lax
from jax.experimental import pallas as pl
from jax.experimental.pallas import tpu as pltpu
from jax.sharding import Mesh
from jax.sharding import PartitionSpec as P

FINE = ("zh", "y", "x", "zl", "c")


def fine_mesh(mesh):
    return Mesh(mesh.devices.reshape(2, 4, 4, 4, 2), FINE)


def shift(array, axis, step):
    size = lax.axis_size(axis)
    return lax.ppermute(array, axis, [(i, (i + step) % size) for i in range(size)])


def swap(array, axis, mask):
    size = lax.axis_size(axis)
    return lax.ppermute(array, axis, [(i, i ^ mask) for i in range(size)])


def f32sum(*terms):
    total = terms[0].astype(jnp.float32)
    for term in terms[1:]:
        total = total + term.astype(jnp.float32)
    return total


def narrow(*terms):
    return f32sum(*terms).astype(jnp.bfloat16)


VMEM = pl.BlockSpec(memory_space=pltpu.VMEM)
SMEM = pl.BlockSpec(memory_space=pltpu.SMEM)
HBM = pl.BlockSpec(memory_space=pltpu.HBM)


def call(kernel, name, out_shape, in_specs, operands, scratch=(), mib=16, flops=0, moved=0):
    outs = (VMEM,) * len(out_shape) if isinstance(out_shape, tuple) else VMEM
    return pl.pallas_call(
        kernel,
        out_shape=out_shape,
        in_specs=in_specs,
        out_specs=outs,
        scratch_shapes=list(scratch),
        compiler_params=pltpu.CompilerParams(vmem_limit_bytes=mib * 2**20),
        cost_estimate=pl.CostEstimate(flops=flops, bytes_accessed=moved, transcendentals=0),
        name=name,
    )(*operands)


def ring_first(up, down, axis):
    return shift(up, axis, 1), shift(down, axis, -1)


def pass_kernel(mid_ref, up_ref, down_ref, last_up_ref, last_down_ref):
    count, rows, _ = last_up_ref.shape
    for block in range(count):
        for row in range(0, rows, 32):
            at = pl.ds(row, 32)
            last_up_ref[block, at] = narrow(mid_ref[block, at], up_ref[block, at])
            last_down_ref[block, at] = narrow(mid_ref[count + block, at], down_ref[block, at])


def pass_on(mid, up, down):
    count = mid.shape[0] // 2
    last = jax.ShapeDtypeStruct((count,) + mid.shape[1:], mid.dtype)
    last_up, last_down = call(
        pass_kernel, "pass_on", (last, last), [VMEM] * 3, (mid, up, down), flops=mid.size, moved=6 * mid.size
    )
    return last_up, last_down


def turn_kernel(which, place_ref, own_ref, up_ref, down_ref, last_up_ref, last_down_ref, next_up, next_down, next_mid, next_own, sum_ref):
    rows = own_ref.shape[1]
    half = rows // 2
    for block in range(2):
        for row in range(0, rows, 32):
            at = pl.ds(row, 32)
            sum_ref[block, at] = narrow(own_ref[block, at], last_up_ref[block, at], down_ref[2 + block, at])
            sum_ref[2 + block, at] = narrow(own_ref[2 + block, at], up_ref[2 + block, at], last_down_ref[block, at])
    low, high = pl.ds(0, half), pl.ds(half, half)
    here = place_ref[which]
    ahead, across, behind = (lax.rem(here + step, 4) for step in (1, 2, 3))
    next_up[0] = sum_ref[across, low]
    next_up[1] = sum_ref[ahead, high]
    next_down[0] = sum_ref[across, high]
    next_down[1] = sum_ref[behind, low]
    next_mid[0] = sum_ref[ahead, low]
    next_mid[1] = sum_ref[behind, high]
    next_own[0] = sum_ref[here, low]
    next_own[1] = sum_ref[here, high]


def turn(which, place, own, up, down, last_up, last_down):
    rows, size = own.shape[1:]
    part = jax.ShapeDtypeStruct((2, rows // 2, size), own.dtype)
    return call(
        functools.partial(turn_kernel, which),
        "turn",
        (part,) * 4,
        [SMEM] + [VMEM] * 5,
        (place, own, up, down, last_up, last_down),
        scratch=[pltpu.VMEM(own.shape, own.dtype)],
        flops=2 * own.size,
        moved=8 * own.size,
    )


def pieces_kernel(*refs):
    out_ref = refs[-1]
    width = out_ref.shape[2]
    for side in range(2):
        own, up, down, last_up, last_down = refs[5 * side : 5 * side + 5]
        half = own.shape[1]
        for row in range(0, half, 32):
            at = pl.ds(row, 32)
            low = narrow(own[0, at], last_up[0, at], down[1, at])
            high = narrow(own[1, at], up[1, at], last_down[0, at])
            for piece in range(8):
                columns = slice(piece * width, (piece + 1) * width)
                out_ref[8 * side + piece, at] = low[:, columns]
                out_ref[8 * side + piece, pl.ds(half + row, 32)] = high[:, columns]


def make_pieces(*parts):
    rows, size = 2 * parts[0].shape[1], parts[0].shape[2]
    out = jax.ShapeDtypeStruct((16, rows, size // 8), jnp.bfloat16)
    return call(
        pieces_kernel, "pieces", out, [VMEM] * 10, parts, flops=4 * rows * size, moved=16 * rows * size
    )


def copy_blocks(grads_ref, moves, cut, sems):
    rows = grads_ref.shape[3] // cut
    copies = [
        pltpu.make_async_copy(
            grads_ref.at[where + (pl.ds(part * rows, rows),)],
            out.at[slot, pl.ds(part * rows, rows)],
            sems.at[cut * i + part],
        )
        for i, (where, out, slot) in enumerate(moves)
        for part in range(cut)
    ]
    for each in copies:
        each.start()
    for each in copies:
        each.wait()


def steps(place_ref, which):
    return tuple(lax.rem(place_ref[which] + step, 4) for step in range(4))


def trim_kernel(place_ref, table_ref, stats_ref, out_ref):
    rows = stats_ref.shape[0]
    half = rows // 2
    slot = lax.rem(2 * place_ref[2] + place_ref[3] + 8 - table_ref[0], 4)

    def block(at):
        return pl.ds(at % 4 * rows, rows)

    for index in range(4):

        @pl.when(slot == index)
        def _():
            out_ref[:, block(0)] = stats_ref[:, block(index)].astype(jnp.bfloat16)
            out_ref[:, block(1)] = stats_ref[:, block(index + 1)].astype(jnp.bfloat16)
            if index < 2:
                opposite = stats_ref[:, pl.ds((index + 2) * rows, half)]
            else:
                opposite = stats_ref[pl.ds(half, half), block(index + 2)].T
            out_ref[:, pl.ds(2 * rows, half)] = opposite.astype(jnp.bfloat16)


def trim(place, table, stats):
    rows = stats.shape[0]
    out = jax.ShapeDtypeStruct((rows, 2 * rows + rows // 2), jnp.bfloat16)
    return call(trim_kernel, "trim", out, [SMEM, SMEM, VMEM], (place, table, stats), flops=stats.size, moved=6 * stats.size)


def send_kernel(place_ref, grads_ref, x_up, x_down, y_up, y_down, sems):
    x, y = steps(place_ref, 0), steps(place_ref, 1)
    moves = []
    for i in range(2):
        moves += [
            ((0, i, x[2]), x_up, i),
            ((0, 2 + i, x[1]), x_up, 2 + i),
            ((0, 2 + i, x[2]), x_down, i),
            ((0, i, x[3]), x_down, 2 + i),
            ((1, y[2], i), y_up, i),
            ((1, y[1], 2 + i), y_up, 2 + i),
            ((1, y[2], 2 + i), y_down, i),
            ((1, y[3], i), y_down, 2 + i),
        ]
    copy_blocks(grads_ref, moves, 4, sems)


def keep_kernel(place_ref, grads_ref, x_mid, x_own, y_mid, y_own, sems):
    x, y = steps(place_ref, 0), steps(place_ref, 1)
    moves = []
    for i in range(2):
        moves += [
            ((0, i, x[1]), x_mid, i),
            ((0, 2 + i, x[3]), x_mid, 2 + i),
            ((1, y[1], i), y_mid, i),
            ((1, y[3], 2 + i), y_mid, 2 + i),
        ]
    for i in range(4):
        moves += [((0, i, x[0]), x_own, i), ((1, y[0], i), y_own, i)]
    copy_blocks(grads_ref, moves, 1, sems)


def pack(kernel, mib, place, grads):
    payload = jax.ShapeDtypeStruct((4,) + grads.shape[3:], grads.dtype)
    return call(
        kernel,
        kernel.__name__[:4],
        (payload,) * 4,
        [SMEM, HBM],
        (place, grads),
        scratch=[pltpu.SemaphoreType.DMA((64,))],
        mib=mib,
        moved=2**23,
    )


def root_kernel(place_ref, table_ref, *refs):
    given, (out_ref, right_ref, slots_ref, rights_ref, start_ref, first_ref, second_ref, third_ref, sem) = refs[:8], refs[8:]
    size = out_ref.shape[0]
    slot = size // 4
    half = slot // 2
    offset, zl, c = table_ref[0], place_ref[2], place_ref[3]

    def span(tile):
        return pl.ds(tile * slot, slot)

    for first_tile, to_ref in ((4, rights_ref), (0, slots_ref)):
        for tile in range(4):
            position = lax.rem(offset + first_tile + tile, 8)
            back = lax.rem(zl + 4 - lax.div(position, 2), 4)
            source = 2 * back + lax.rem(position + c, 2)
            for i, ref in enumerate(given):

                @pl.when(source == i)
                def _():
                    to_ref[tile] = ref[...]

    passed = pltpu.make_async_copy(rights_ref, right_ref, sem)
    passed.start()

    total = jnp.zeros((8, slot // 2), jnp.float32)
    for tile in range(4):
        values = slots_ref[tile].astype(jnp.float32)
        squares = values * values
        total = total + lanes(squares[:, :slot]) + 2.0 * lanes(squares[:, slot:])
    inverse = 1.0 / jnp.sqrt(jnp.sum(total))

    row_ids = lax.broadcasted_iota(jnp.int32, (slot, slot), 0)
    col_ids = lax.broadcasted_iota(jnp.int32, (slot, slot), 1)
    eye = jnp.where(row_ids == col_ids, 1.0, 0.0).astype(jnp.float32)

    def place(row, column, normed, diagonal):
        start_ref[span(row), span(column)] = normed.astype(jnp.bfloat16)
        term = 1.5 * eye - 0.5 * normed if diagonal else -0.5 * normed
        first_ref[span(row), span(column)] = term.astype(jnp.bfloat16)

    for tile in range(4):
        after = (tile + 1) % 4
        place(tile, tile, slots_ref[tile, :, :slot].astype(jnp.float32) * inverse, True)
        normed = slots_ref[tile, :, slot : 2 * slot].astype(jnp.float32) * inverse
        place(tile, after, normed, False)
        place(after, tile, normed.T, False)
    for tile in range(2):
        parts = [slots_ref[at, :, 2 * slot :].astype(jnp.float32) * inverse for at in (tile, tile + 2)]
        normed = jnp.concatenate(parts, axis=1)
        place(tile, tile + 2, normed, False)
        place(tile + 2, tile, normed.T, False)

    def eye_rows(tile):
        row_ids = lax.broadcasted_iota(jnp.int32, (slot, size), 0) + tile * slot
        col_ids = lax.broadcasted_iota(jnp.int32, (slot, size), 1)
        return jnp.where(row_ids == col_ids, 1.0, 0.0).astype(jnp.float32)

    for tile in range(4):
        product = jnp.dot(start_ref[span(tile), :], first_ref[...], preferred_element_type=jnp.float32)
        second_ref[span(tile), :] = product.astype(jnp.bfloat16)
    for tile in range(4):
        product = jnp.dot(first_ref[span(tile), :], second_ref[...], preferred_element_type=jnp.float32)
        third_ref[span(tile), :] = (1.5 * eye_rows(tile) - 0.5 * product).astype(jnp.bfloat16)
    for tile in range(4):
        product = jnp.dot(third_ref[span(tile), :], first_ref[...], preferred_element_type=jnp.float32)
        out_ref[span(tile), :] = product.astype(jnp.bfloat16)
    passed.wait()


def left_inverse_root(place, table, slots):
    rows, kept = slots[0].shape
    size = 4 * rows
    matrix, side = (size, size), (4, rows, kept)
    return pl.pallas_call(
        root_kernel,
        out_shape=(jax.ShapeDtypeStruct(matrix, jnp.bfloat16), jax.ShapeDtypeStruct(side, jnp.bfloat16)),
        in_specs=[SMEM] * 2 + [VMEM] * 8,
        out_specs=(VMEM, HBM),
        scratch_shapes=[pltpu.VMEM(side, jnp.bfloat16)] * 2
        + [pltpu.VMEM(matrix, jnp.bfloat16)] * 4
        + [pltpu.SemaphoreType.DMA(())],
        compiler_params=pltpu.CompilerParams(vmem_limit_bytes=18 * 2**20),
        cost_estimate=pl.CostEstimate(flops=6 * size**3, bytes_accessed=4 * size * size, transcendentals=0),
        name="left_root",
    )(place, table, *slots)


def base_kernel(slots_ref, first_ref, diagonal_ref):
    size = first_ref.shape[0]
    slot = size // 4

    def span(tile):
        return pl.ds(tile * slot, slot)

    total = jnp.zeros((8, slot // 2), jnp.float32)
    for tile in range(4):
        values = slots_ref[tile].astype(jnp.float32)
        squares = values * values
        total = total + lanes(squares[:, :slot]) + 2.0 * lanes(squares[:, slot:])
    inverse = 1.0 / jnp.sqrt(jnp.sum(total))

    row_ids = lax.broadcasted_iota(jnp.int32, (slot, slot), 0)
    col_ids = lax.broadcasted_iota(jnp.int32, (slot, slot), 1)
    eye = jnp.where(row_ids == col_ids, 1.0, 0.0).astype(jnp.float32)

    def place(row, column, normed):
        first_ref[span(row), span(column)] = (-0.5 * normed).astype(jnp.bfloat16)

    for tile in range(4):
        following = (tile + 1) % 4
        normed = slots_ref[tile, :, :slot].astype(jnp.float32) * inverse
        first = (1.5 * eye - 0.5 * normed).astype(jnp.bfloat16)
        first_ref[span(tile), span(tile)] = first
        start = normed.astype(jnp.bfloat16).astype(jnp.float32)
        both = eye * (start + 2.0 * first.astype(jnp.float32))
        row = jnp.sum(both, axis=0, keepdims=True)
        diagonal_ref[:, span(tile)] = jnp.broadcast_to(row, (diagonal_ref.shape[0], slot))
        normed = slots_ref[tile, :, slot : 2 * slot].astype(jnp.float32) * inverse
        place(tile, following, normed)
        place(following, tile, normed.T)
    for tile in range(2):
        parts = [slots_ref[at, :, 2 * slot :].astype(jnp.float32) * inverse for at in (tile, tile + 2)]
        normed = jnp.concatenate(parts, axis=1)
        place(tile, tile + 2, normed)
        place(tile + 2, tile, normed.T)


def right_base(slots):
    size = 4 * slots.shape[1]
    return call(
        base_kernel,
        "right_base",
        (jax.ShapeDtypeStruct((size, size), jnp.bfloat16), jax.ShapeDtypeStruct((8, size), jnp.float32)),
        [VMEM],
        (slots,),
        flops=4 * size * size,
        moved=4 * size * size,
    )


def lanes(squares):
    rows, columns = squares.shape
    total = jnp.sum(squares.reshape(rows // 8, 8, columns), axis=0)
    return sum(total[:, at : at + 128] for at in range(0, columns, 128))


def mix_kernel(pieces_ref, left_ref, out_ref, energy_ref, grad_ref):
    count, rows, _ = out_ref.shape
    energy = jnp.zeros(energy_ref.shape, jnp.float32)
    for piece in range(count):
        grad = narrow(pieces_ref[piece], pieces_ref[count + piece])
        grad_ref[pl.ds(piece * rows, rows), :] = grad
        wide = grad.astype(jnp.float32)
        energy = energy + lanes(wide * wide)
    energy_ref[...] = energy
    for piece in range(0, count, 2):
        product = jnp.dot(
            left_ref[pl.ds(piece * rows, 2 * rows), :], grad_ref[...], preferred_element_type=jnp.float32
        ).astype(jnp.bfloat16)
        out_ref[piece] = product[:rows]
        out_ref[piece + 1] = product[rows:]


def mix(pieces, left_root):
    _, rows, width = pieces.shape
    return call(
        mix_kernel,
        "mix",
        (jax.ShapeDtypeStruct((8, rows, width), jnp.bfloat16), jax.ShapeDtypeStruct((8, 128), jnp.float32)),
        [VMEM] * 2,
        (pieces, left_root),
        scratch=[pltpu.VMEM((8 * rows, width), jnp.bfloat16)],
        flops=2 * left_root.size * width,
        moved=2 * left_root.size,
    )


def condition_kernel(mixed_ref, first_ref, diagonal_ref, energy_ref, out_ref, totals_ref, wide_ref, even_ref, odd_ref):
    count, _, width = mixed_ref.shape
    for piece in range(count):
        odd_ref[:, pl.ds(piece * width, width)] = mixed_ref[piece]

    def products(slab_ref):
        for column in range(0, out_ref.shape[1], 2 * width):
            at = pl.ds(column, 2 * width)
            yield at, jnp.dot(slab_ref[...], first_ref[:, at], preferred_element_type=jnp.float32)

    for at, product in products(odd_ref):
        wide_ref[:, at] = product
        even_ref[:, at] = product.astype(jnp.bfloat16)
    for at, product in products(even_ref):
        odd_ref[:, at] = product.astype(jnp.bfloat16)
    for at, product in products(odd_ref):
        started = diagonal_ref[:1, at] * odd_ref[:, at].astype(jnp.float32) - 2.0 * product
        even_ref[:, at] = started.astype(jnp.bfloat16)
    total = jnp.zeros(energy_ref.shape, jnp.float32)
    for at, product in products(even_ref):
        precond = 1.5 * wide_ref[:, at] - 0.5 * product
        out_ref[:, at] = precond
        total = total + lanes(precond * precond)
    totals_ref[:8] = energy_ref[...]
    totals_ref[8:] = total


def condition(mixed, first, diagonal, energy):
    _, rows, width = mixed.shape
    slab = (rows, 8 * width)
    return call(
        condition_kernel,
        "condition",
        (jax.ShapeDtypeStruct(slab, jnp.float32), jax.ShapeDtypeStruct((16, 128), jnp.float32)),
        [VMEM] * 4,
        (mixed, first, diagonal, energy),
        scratch=[pltpu.VMEM(slab, jnp.float32), pltpu.VMEM(slab, jnp.bfloat16), pltpu.VMEM(slab, jnp.bfloat16)],
        flops=8 * rows * first.size,
        moved=2 * first.size,
    )


def finish_kernel(count, totals_ref, precond_ref, out_ref):
    grad_mean = jnp.sum(totals_ref[:8]) / count
    cond_mean = jnp.sum(totals_ref[8:]) / count
    factor = jnp.sqrt(grad_mean / (cond_mean + 1e-06))
    for row in range(0, out_ref.shape[0], 32):
        at = pl.ds(row, 32)
        out_ref[at] = precond_ref[at] * factor


def finish(totals, precond, count):
    return call(
        functools.partial(finish_kernel, count),
        "finish",
        jax.ShapeDtypeStruct(precond.shape, jnp.float32),
        [VMEM] * 2,
        (totals, precond),
        flops=precond.size,
        moved=8 * precond.size,
    )


def after(dep, *values):
    return lax.optimization_barrier((dep,) + values)[1:]


def local(grad_partial, factor_stats, owner_table):
    size = grad_partial.shape[3]
    rows_here = grad_partial.shape[2]
    owner = ("zl", "c")
    grads = grad_partial.reshape(2, 4, 4, rows_here, size)
    place = jnp.stack([lax.axis_index(axis).astype(jnp.int32) for axis in ("x", "y", "zl", "c")])

    x_up, x_down, y_up, y_down = pack(send_kernel, 48, place, grads)
    x_ends = ring_first(x_up, x_down, "x")
    y_ends = ring_first(y_up, y_down, "y")

    (sent,) = after(x_up, place)
    near = [trim(sent, owner_table, factor_stats[0, 0])]
    near.append(shift(near[0], "zl", 1))
    x_mid, x_own, y_mid, y_own = pack(keep_kernel, 16, sent, grads)
    near.append(shift(*after(x_mid, near[1]), "zl", 1))
    near.append(shift(near[2], "zl", 1))
    (x_mid,) = after(near[2], x_mid)
    x_last = pass_on(x_mid, *x_ends)
    y_last = pass_on(y_mid, *y_ends)
    far = [swap(each, "c", 1) for each in near[:3]]
    far.append(swap(*after(x_last[0], near[3]), "c", 1))
    slots = tuple(each for pair in zip(near, far) for each in pair)

    x_last = ring_first(*x_last, "x")
    y_last = ring_first(*y_last, "y")

    lower_up, lower_down, lower_mid, lower_own = turn(1, place, x_own, *x_ends, *x_last)
    lower_ends = ring_first(lower_up, lower_down, "y")
    upper_up, upper_down, upper_mid, upper_own = turn(0, place, y_own, *y_ends, *y_last)
    upper_ends = ring_first(upper_up, upper_down, "x")
    lower_last = ring_first(*pass_on(lower_mid, *lower_ends), "y")
    upper_last = ring_first(*pass_on(upper_mid, *upper_ends), "x")
    pieces = make_pieces(lower_own, *lower_ends, *lower_last, upper_own, *upper_ends, *upper_last)

    slots = after(pieces, *slots)
    pieces = lax.all_to_all(pieces, ("zh",) + owner, split_axis=0, concat_axis=0, tiled=True)
    left_root, right_slots = left_inverse_root(place, owner_table, slots)
    mixed, energy = mix(pieces, left_root)
    right = right_base(*after(mixed, right_slots))
    mixed = lax.all_to_all(mixed, owner, split_axis=0, concat_axis=0, tiled=True)
    precond, totals = condition(mixed, *right, energy)
    totals = totals + swap(totals, "c", 1)
    totals = totals + shift(totals, "zl", 1) + shift(totals, "zl", 2) + shift(totals, "zl", 3)
    return finish(totals, precond, float(size * size))[None]


def solution(mesh):
    dp, owner = ("zh", "y", "x"), ("zl", "c")
    placed = (P(dp, None, owner, None), P(dp, owner, None, None), P(dp))
    return jax.shard_map(
        local, mesh=fine_mesh(mesh), in_specs=placed, out_specs=P(dp, owner, None), check_vma=False
    )
```

```python
import functools

import jax
import jax.numpy as jnp
from jax import lax
from jax.experimental import pallas as pl
from jax.experimental.pallas import tpu as pltpu
from jax.sharding import Mesh
from jax.sharding import PartitionSpec as P

FINE = ("zh", "y", "x", "zl", "c")


def fine_mesh(mesh):
    return Mesh(mesh.devices.reshape(2, 4, 4, 4, 2), FINE)


def shift(array, axis, step):
    size = lax.axis_size(axis)
    return lax.ppermute(array, axis, [(i, (i + step) % size) for i in range(size)])


def swap(array, axis, mask):
    size = lax.axis_size(axis)
    return lax.ppermute(array, axis, [(i, i ^ mask) for i in range(size)])


def f32sum(*terms):
    total = terms[0].astype(jnp.float32)
    for term in terms[1:]:
        total = total + term.astype(jnp.float32)
    return total


def narrow(*terms):
    return f32sum(*terms).astype(jnp.bfloat16)


VMEM = pl.BlockSpec(memory_space=pltpu.VMEM)
SMEM = pl.BlockSpec(memory_space=pltpu.SMEM)
HBM = pl.BlockSpec(memory_space=pltpu.HBM)


def call(kernel, name, out_shape, in_specs, operands, scratch=(), mib=16, flops=0, moved=0):
    outs = (VMEM,) * len(out_shape) if isinstance(out_shape, tuple) else VMEM
    return pl.pallas_call(
        kernel,
        out_shape=out_shape,
        in_specs=in_specs,
        out_specs=outs,
        scratch_shapes=list(scratch),
        compiler_params=pltpu.CompilerParams(vmem_limit_bytes=mib * 2**20),
        cost_estimate=pl.CostEstimate(flops=flops, bytes_accessed=moved, transcendentals=0),
        name=name,
    )(*operands)


def ring_first(up, down, axis):
    return shift(up, axis, 1), shift(down, axis, -1)


def pass_kernel(mid_ref, up_ref, down_ref, last_up_ref, last_down_ref):
    count, rows, _ = last_up_ref.shape
    for block in range(count):
        for row in range(0, rows, 32):
            at = pl.ds(row, 32)
            last_up_ref[block, at] = narrow(mid_ref[block, at], up_ref[block, at])
            last_down_ref[block, at] = narrow(mid_ref[count + block, at], down_ref[block, at])


def pass_on(mid, up, down):
    count = mid.shape[0] // 2
    last = jax.ShapeDtypeStruct((count,) + mid.shape[1:], mid.dtype)
    last_up, last_down = call(
        pass_kernel, "pass_on", (last, last), [VMEM] * 3, (mid, up, down), flops=mid.size, moved=6 * mid.size
    )
    return last_up, last_down


def turn_kernel(which, place_ref, own_ref, up_ref, down_ref, last_up_ref, last_down_ref, far_ref, ahead_ref, behind_ref, here_ref, sum_ref):
    for block in range(2):
        for row in range(0, own_ref.shape[1], 32):
            at = pl.ds(row, 32)
            sum_ref[block, at] = narrow(own_ref[block, at], last_up_ref[block, at], down_ref[2 + block, at])
            sum_ref[2 + block, at] = narrow(own_ref[2 + block, at], up_ref[2 + block, at], last_down_ref[block, at])
    for step, ref in enumerate((here_ref, ahead_ref, far_ref, behind_ref)):
        ref[...] = sum_ref[lax.rem(place_ref[which] + step, 4)]


def turn(which, place, own, up, down, last_up, last_down):
    part = jax.ShapeDtypeStruct(own.shape[1:], own.dtype)
    return call(
        functools.partial(turn_kernel, which),
        "turn",
        (part,) * 4,
        [SMEM] + [VMEM] * 5,
        (place, own, up, down, last_up, last_down),
        scratch=[pltpu.VMEM(own.shape, own.dtype)],
        flops=2 * own.size,
        moved=8 * own.size,
    )


def second_stage(far, ahead, behind, here, axis):
    return here, shift(far, axis, 2), shift(ahead, axis, 1), shift(behind, axis, -1)


def pieces_kernel(*refs):
    out_ref = refs[-1]
    _, rows, width = out_ref.shape
    for side in range(2):
        terms = refs[4 * side : 4 * side + 4]
        for row in range(0, rows, 32):
            at = pl.ds(row, 32)
            total = narrow(*(ref[at] for ref in terms))
            for piece in range(8):
                out_ref[8 * side + piece, at] = total[:, piece * width : (piece + 1) * width]


def make_pieces(*terms):
    rows, size = terms[0].shape
    out = jax.ShapeDtypeStruct((16, rows, size // 8), jnp.bfloat16)
    return call(
        pieces_kernel, "pieces", out, [VMEM] * 8, terms, flops=8 * rows * size, moved=20 * rows * size
    )


def copy_blocks(grads_ref, moves, cut, sems):
    rows = grads_ref.shape[3] // cut
    copies = [
        pltpu.make_async_copy(
            grads_ref.at[where + (pl.ds(part * rows, rows),)],
            out.at[slot, pl.ds(part * rows, rows)],
            sems.at[cut * i + part],
        )
        for i, (where, out, slot) in enumerate(moves)
        for part in range(cut)
    ]
    for each in copies:
        each.start()
    for each in copies:
        each.wait()


def steps(place_ref, which):
    return tuple(lax.rem(place_ref[which] + step, 4) for step in range(4))


def trim_kernel(place_ref, table_ref, stats_ref, out_ref):
    rows = stats_ref.shape[0]
    half = rows // 2
    slot = lax.rem(2 * place_ref[2] + place_ref[3] + 8 - table_ref[0], 4)

    def block(at):
        return pl.ds(at % 4 * rows, rows)

    for index in range(4):

        @pl.when(slot == index)
        def _():
            out_ref[:, block(0)] = stats_ref[:, block(index)].astype(jnp.bfloat16)
            out_ref[:, block(1)] = stats_ref[:, block(index + 1)].astype(jnp.bfloat16)
            if index < 2:
                opposite = stats_ref[:, pl.ds((index + 2) * rows, half)]
            else:
                opposite = stats_ref[pl.ds(half, half), block(index + 2)].T
            out_ref[:, pl.ds(2 * rows, half)] = opposite.astype(jnp.bfloat16)


def trim(place, table, stats):
    rows = stats.shape[0]
    out = jax.ShapeDtypeStruct((rows, 2 * rows + rows // 2), jnp.bfloat16)
    return call(trim_kernel, "trim", out, [SMEM, SMEM, VMEM], (place, table, stats), flops=stats.size, moved=6 * stats.size)


def send_kernel(place_ref, grads_ref, x_up, x_down, y_up, y_down, sems):
    x, y = steps(place_ref, 0), steps(place_ref, 1)
    moves = []
    for i in range(2):
        moves += [
            ((0, i, x[2]), x_up, i),
            ((0, 2 + i, x[1]), x_up, 2 + i),
            ((0, 2 + i, x[2]), x_down, i),
            ((0, i, x[3]), x_down, 2 + i),
            ((1, y[2], i), y_up, i),
            ((1, y[1], 2 + i), y_up, 2 + i),
            ((1, y[2], 2 + i), y_down, i),
            ((1, y[3], i), y_down, 2 + i),
        ]
    copy_blocks(grads_ref, moves, 4, sems)


def keep_kernel(place_ref, grads_ref, x_mid, x_own, y_mid, y_own, sems):
    x, y = steps(place_ref, 0), steps(place_ref, 1)
    moves = []
    for i in range(2):
        moves += [
            ((0, i, x[1]), x_mid, i),
            ((0, 2 + i, x[3]), x_mid, 2 + i),
            ((1, y[1], i), y_mid, i),
            ((1, y[3], 2 + i), y_mid, 2 + i),
        ]
    for i in range(4):
        moves += [((0, i, x[0]), x_own, i), ((1, y[0], i), y_own, i)]
    copy_blocks(grads_ref, moves, 1, sems)


def pack(kernel, mib, place, grads):
    payload = jax.ShapeDtypeStruct((4,) + grads.shape[3:], grads.dtype)
    return call(
        kernel,
        kernel.__name__[:4],
        (payload,) * 4,
        [SMEM, HBM],
        (place, grads),
        scratch=[pltpu.SemaphoreType.DMA((64,))],
        mib=mib,
        moved=2**23,
    )


def root_kernel(place_ref, table_ref, *refs):
    given, (out_ref, right_ref, slots_ref, rights_ref, start_ref, first_ref, second_ref, third_ref, sem) = refs[:8], refs[8:]
    size = out_ref.shape[0]
    slot = size // 4
    half = slot // 2
    offset, zl, c = table_ref[0], place_ref[2], place_ref[3]

    def span(tile):
        return pl.ds(tile * slot, slot)

    for first_tile, to_ref in ((4, rights_ref), (0, slots_ref)):
        for tile in range(4):
            position = lax.rem(offset + first_tile + tile, 8)
            back = lax.rem(zl + 4 - lax.div(position, 2), 4)
            source = 2 * back + lax.rem(position + c, 2)
            for i, ref in enumerate(given):

                @pl.when(source == i)
                def _():
                    to_ref[tile] = ref[...]

    passed = pltpu.make_async_copy(rights_ref, right_ref, sem)
    passed.start()

    total = jnp.zeros((8, slot // 2), jnp.float32)
    for tile in range(4):
        values = slots_ref[tile].astype(jnp.float32)
        squares = values * values
        total = total + lanes(squares[:, :slot]) + 2.0 * lanes(squares[:, slot:])
    inverse = 1.0 / jnp.sqrt(jnp.sum(total))

    row_ids = lax.broadcasted_iota(jnp.int32, (slot, slot), 0)
    col_ids = lax.broadcasted_iota(jnp.int32, (slot, slot), 1)
    eye = jnp.where(row_ids == col_ids, 1.0, 0.0).astype(jnp.float32)

    def place(row, column, normed, diagonal):
        start_ref[span(row), span(column)] = normed.astype(jnp.bfloat16)
        term = 1.5 * eye - 0.5 * normed if diagonal else -0.5 * normed
        first_ref[span(row), span(column)] = term.astype(jnp.bfloat16)

    for tile in range(4):
        after = (tile + 1) % 4
        place(tile, tile, slots_ref[tile, :, :slot].astype(jnp.float32) * inverse, True)
        normed = slots_ref[tile, :, slot : 2 * slot].astype(jnp.float32) * inverse
        place(tile, after, normed, False)
        place(after, tile, normed.T, False)
    for tile in range(2):
        parts = [slots_ref[at, :, 2 * slot :].astype(jnp.float32) * inverse for at in (tile, tile + 2)]
        normed = jnp.concatenate(parts, axis=1)
        place(tile, tile + 2, normed, False)
        place(tile + 2, tile, normed.T, False)

    def eye_rows(tile):
        row_ids = lax.broadcasted_iota(jnp.int32, (slot, size), 0) + tile * slot
        col_ids = lax.broadcasted_iota(jnp.int32, (slot, size), 1)
        return jnp.where(row_ids == col_ids, 1.0, 0.0).astype(jnp.float32)

    for tile in range(4):
        product = jnp.dot(start_ref[span(tile), :], first_ref[...], preferred_element_type=jnp.float32)
        second_ref[span(tile), :] = product.astype(jnp.bfloat16)
    for tile in range(4):
        product = jnp.dot(first_ref[span(tile), :], second_ref[...], preferred_element_type=jnp.float32)
        third_ref[span(tile), :] = (1.5 * eye_rows(tile) - 0.5 * product).astype(jnp.bfloat16)
    for tile in range(4):
        product = jnp.dot(third_ref[span(tile), :], first_ref[...], preferred_element_type=jnp.float32)
        out_ref[span(tile), :] = product.astype(jnp.bfloat16)
    passed.wait()


def left_inverse_root(place, table, slots):
    rows, kept = slots[0].shape
    size = 4 * rows
    matrix, side = (size, size), (4, rows, kept)
    return pl.pallas_call(
        root_kernel,
        out_shape=(jax.ShapeDtypeStruct(matrix, jnp.bfloat16), jax.ShapeDtypeStruct(side, jnp.bfloat16)),
        in_specs=[SMEM] * 2 + [VMEM] * 8,
        out_specs=(VMEM, HBM),
        scratch_shapes=[pltpu.VMEM(side, jnp.bfloat16)] * 2
        + [pltpu.VMEM(matrix, jnp.bfloat16)] * 4
        + [pltpu.SemaphoreType.DMA(())],
        compiler_params=pltpu.CompilerParams(vmem_limit_bytes=18 * 2**20),
        cost_estimate=pl.CostEstimate(flops=6 * size**3, bytes_accessed=4 * size * size, transcendentals=0),
        name="left_root",
    )(place, table, *slots)


def base_kernel(slots_ref, first_ref, diagonal_ref):
    size = first_ref.shape[0]
    slot = size // 4

    def span(tile):
        return pl.ds(tile * slot, slot)

    total = jnp.zeros((8, slot // 2), jnp.float32)
    for tile in range(4):
        values = slots_ref[tile].astype(jnp.float32)
        squares = values * values
        total = total + lanes(squares[:, :slot]) + 2.0 * lanes(squares[:, slot:])
    inverse = 1.0 / jnp.sqrt(jnp.sum(total))

    row_ids = lax.broadcasted_iota(jnp.int32, (slot, slot), 0)
    col_ids = lax.broadcasted_iota(jnp.int32, (slot, slot), 1)
    eye = jnp.where(row_ids == col_ids, 1.0, 0.0).astype(jnp.float32)

    def place(row, column, normed):
        first_ref[span(row), span(column)] = (-0.5 * normed).astype(jnp.bfloat16)

    for tile in range(4):
        following = (tile + 1) % 4
        normed = slots_ref[tile, :, :slot].astype(jnp.float32) * inverse
        first = (1.5 * eye - 0.5 * normed).astype(jnp.bfloat16)
        first_ref[span(tile), span(tile)] = first
        start = normed.astype(jnp.bfloat16).astype(jnp.float32)
        both = eye * (start + 2.0 * first.astype(jnp.float32))
        row = jnp.sum(both, axis=0, keepdims=True)
        diagonal_ref[:, span(tile)] = jnp.broadcast_to(row, (diagonal_ref.shape[0], slot))
        normed = slots_ref[tile, :, slot : 2 * slot].astype(jnp.float32) * inverse
        place(tile, following, normed)
        place(following, tile, normed.T)
    for tile in range(2):
        parts = [slots_ref[at, :, 2 * slot :].astype(jnp.float32) * inverse for at in (tile, tile + 2)]
        normed = jnp.concatenate(parts, axis=1)
        place(tile, tile + 2, normed)
        place(tile + 2, tile, normed.T)


def right_base(slots):
    size = 4 * slots.shape[1]
    return call(
        base_kernel,
        "right_base",
        (jax.ShapeDtypeStruct((size, size), jnp.bfloat16), jax.ShapeDtypeStruct((8, size), jnp.float32)),
        [VMEM],
        (slots,),
        flops=4 * size * size,
        moved=4 * size * size,
    )


def lanes(squares):
    rows, columns = squares.shape
    total = jnp.sum(squares.reshape(rows // 8, 8, columns), axis=0)
    return sum(total[:, at : at + 128] for at in range(0, columns, 128))


def mix_kernel(pieces_ref, left_ref, out_ref, energy_ref, grad_ref):
    count, rows, _ = out_ref.shape
    energy = jnp.zeros(energy_ref.shape, jnp.float32)
    for piece in range(count):
        grad = narrow(pieces_ref[piece], pieces_ref[count + piece])
        grad_ref[pl.ds(piece * rows, rows), :] = grad
        wide = grad.astype(jnp.float32)
        energy = energy + lanes(wide * wide)
    energy_ref[...] = energy
    for piece in range(0, count, 2):
        product = jnp.dot(
            left_ref[pl.ds(piece * rows, 2 * rows), :], grad_ref[...], preferred_element_type=jnp.float32
        ).astype(jnp.bfloat16)
        out_ref[piece] = product[:rows]
        out_ref[piece + 1] = product[rows:]


def mix(pieces, left_root):
    _, rows, width = pieces.shape
    return call(
        mix_kernel,
        "mix",
        (jax.ShapeDtypeStruct((8, rows, width), jnp.bfloat16), jax.ShapeDtypeStruct((8, 128), jnp.float32)),
        [VMEM] * 2,
        (pieces, left_root),
        scratch=[pltpu.VMEM((8 * rows, width), jnp.bfloat16)],
        flops=2 * left_root.size * width,
        moved=2 * left_root.size,
    )


def condition_kernel(mixed_ref, first_ref, diagonal_ref, energy_ref, out_ref, totals_ref, wide_ref, even_ref, odd_ref):
    count, _, width = mixed_ref.shape
    for piece in range(count):
        odd_ref[:, pl.ds(piece * width, width)] = mixed_ref[piece]

    def products(slab_ref):
        for column in range(0, out_ref.shape[1], 2 * width):
            at = pl.ds(column, 2 * width)
            yield at, jnp.dot(slab_ref[...], first_ref[:, at], preferred_element_type=jnp.float32)

    for at, product in products(odd_ref):
        wide_ref[:, at] = product
        even_ref[:, at] = product.astype(jnp.bfloat16)
    for at, product in products(even_ref):
        odd_ref[:, at] = product.astype(jnp.bfloat16)
    for at, product in products(odd_ref):
        started = diagonal_ref[:1, at] * odd_ref[:, at].astype(jnp.float32) - 2.0 * product
        even_ref[:, at] = started.astype(jnp.bfloat16)
    total = jnp.zeros(energy_ref.shape, jnp.float32)
    for at, product in products(even_ref):
        precond = 1.5 * wide_ref[:, at] - 0.5 * product
        out_ref[:, at] = precond
        total = total + lanes(precond * precond)
    totals_ref[:8] = energy_ref[...]
    totals_ref[8:] = total


def condition(mixed, first, diagonal, energy):
    _, rows, width = mixed.shape
    slab = (rows, 8 * width)
    return call(
        condition_kernel,
        "condition",
        (jax.ShapeDtypeStruct(slab, jnp.float32), jax.ShapeDtypeStruct((16, 128), jnp.float32)),
        [VMEM] * 4,
        (mixed, first, diagonal, energy),
        scratch=[pltpu.VMEM(slab, jnp.float32), pltpu.VMEM(slab, jnp.bfloat16), pltpu.VMEM(slab, jnp.bfloat16)],
        flops=8 * rows * first.size,
        moved=2 * first.size,
    )


def finish_kernel(count, totals_ref, precond_ref, out_ref):
    grad_mean = jnp.sum(totals_ref[:8]) / count
    cond_mean = jnp.sum(totals_ref[8:]) / count
    factor = jnp.sqrt(grad_mean / (cond_mean + 1e-06))
    for row in range(0, out_ref.shape[0], 32):
        at = pl.ds(row, 32)
        out_ref[at] = precond_ref[at] * factor


def finish(totals, precond, count):
    return call(
        functools.partial(finish_kernel, count),
        "finish",
        jax.ShapeDtypeStruct(precond.shape, jnp.float32),
        [VMEM] * 2,
        (totals, precond),
        flops=precond.size,
        moved=8 * precond.size,
    )


def after(dep, *values):
    return lax.optimization_barrier((dep,) + values)[1:]


def local(grad_partial, factor_stats, owner_table):
    size = grad_partial.shape[3]
    rows_here = grad_partial.shape[2]
    owner = ("zl", "c")
    grads = grad_partial.reshape(2, 4, 4, rows_here, size)
    place = jnp.stack([lax.axis_index(axis).astype(jnp.int32) for axis in ("x", "y", "zl", "c")])

    x_up, x_down, y_up, y_down = pack(send_kernel, 48, place, grads)
    x_ends = ring_first(x_up, x_down, "x")
    y_ends = ring_first(y_up, y_down, "y")

    (sent,) = after(x_up, place)
    near = [trim(sent, owner_table, factor_stats[0, 0])]
    near.append(shift(near[0], "zl", 1))
    x_mid, x_own, y_mid, y_own = pack(keep_kernel, 16, sent, grads)
    near.append(shift(*after(x_mid, near[1]), "zl", 1))
    near.append(shift(near[2], "zl", 1))
    (x_mid,) = after(near[2], x_mid)
    x_last = pass_on(x_mid, *x_ends)
    y_last = pass_on(y_mid, *y_ends)
    far = [swap(each, "c", 1) for each in near[:3]]
    far.append(swap(*after(x_last[0], near[3]), "c", 1))
    slots = tuple(each for pair in zip(near, far) for each in pair)

    x_last = ring_first(*x_last, "x")
    y_last = ring_first(*y_last, "y")

    lower = second_stage(*turn(1, place, x_own, *x_ends, *x_last), "y")
    upper = second_stage(*turn(0, place, y_own, *y_ends, *y_last), "x")
    pieces = make_pieces(*lower, *upper)

    slots = after(pieces, *slots)

    pieces = lax.all_to_all(pieces, ("zh",) + owner, split_axis=0, concat_axis=0, tiled=True)
    left_root, right_slots = left_inverse_root(place, owner_table, slots)
    mixed, energy = mix(pieces, left_root)
    right = right_base(*after(mixed, right_slots))
    mixed = lax.all_to_all(mixed, owner, split_axis=0, concat_axis=0, tiled=True)
    precond, totals = condition(mixed, *right, energy)
    totals = totals + swap(totals, "c", 1)
    totals = totals + shift(totals, "zl", 1) + shift(totals, "zl", 2) + shift(totals, "zl", 3)
    return finish(totals, precond, float(size * size))[None]


def solution(mesh):
    dp, owner = ("zh", "y", "x"), ("zl", "c")
    placed = (P(dp, None, owner, None), P(dp, owner, None, None), P(dp))
    return jax.shard_map(
        local, mesh=fine_mesh(mesh), in_specs=placed, out_specs=P(dp, owner, None), check_vma=False
    )
```

```python
import functools

import jax
import jax.numpy as jnp
from jax import lax
from jax.experimental import pallas as pl
from jax.experimental.pallas import tpu as pltpu
from jax.sharding import Mesh
from jax.sharding import PartitionSpec as P

FINE = ("zh", "y", "x", "zl", "c")


def fine_mesh(mesh):
    return Mesh(mesh.devices.reshape(2, 4, 4, 4, 2), FINE)


def shift(array, axis, step):
    size = lax.axis_size(axis)
    return lax.ppermute(array, axis, [(i, (i + step) % size) for i in range(size)])


def swap(array, axis, mask):
    size = lax.axis_size(axis)
    return lax.ppermute(array, axis, [(i, i ^ mask) for i in range(size)])


def f32sum(*terms):
    total = terms[0].astype(jnp.float32)
    for term in terms[1:]:
        total = total + term.astype(jnp.float32)
    return total


def narrow(*terms):
    return f32sum(*terms).astype(jnp.bfloat16)


VMEM = pl.BlockSpec(memory_space=pltpu.VMEM)
SMEM = pl.BlockSpec(memory_space=pltpu.SMEM)
HBM = pl.BlockSpec(memory_space=pltpu.HBM)


def call(kernel, name, out_shape, in_specs, operands, scratch=(), mib=16, flops=0, moved=0):
    outs = (VMEM,) * len(out_shape) if isinstance(out_shape, tuple) else VMEM
    return pl.pallas_call(
        kernel,
        out_shape=out_shape,
        in_specs=in_specs,
        out_specs=outs,
        scratch_shapes=list(scratch),
        compiler_params=pltpu.CompilerParams(vmem_limit_bytes=mib * 2**20),
        cost_estimate=pl.CostEstimate(flops=flops, bytes_accessed=moved, transcendentals=0),
        name=name,
    )(*operands)


def ring_first(up, down, axis):
    return shift(up, axis, 1), shift(down, axis, -1)


def pass_kernel(mid_ref, up_ref, down_ref, last_up_ref, last_down_ref):
    count, rows, _ = last_up_ref.shape
    for block in range(count):
        for row in range(0, rows, 32):
            at = pl.ds(row, 32)
            last_up_ref[block, at] = narrow(mid_ref[block, at], up_ref[block, at])
            last_down_ref[block, at] = narrow(mid_ref[count + block, at], down_ref[block, at])


def pass_on(mid, up, down):
    count = mid.shape[0] // 2
    last = jax.ShapeDtypeStruct((count,) + mid.shape[1:], mid.dtype)
    last_up, last_down = call(
        pass_kernel, "pass_on", (last, last), [VMEM] * 3, (mid, up, down), flops=mid.size, moved=6 * mid.size
    )
    return last_up, last_down


def turn_kernel(place_ref, own_ref, up_ref, down_ref, last_up_ref, last_down_ref, next_up, next_down, next_mid, next_own, sum_ref):
    rows = own_ref.shape[1]
    half = rows // 2
    for block in range(2):
        for row in range(0, rows, 32):
            at = pl.ds(row, 32)
            sum_ref[block, at] = narrow(own_ref[block, at], last_up_ref[block, at], down_ref[2 + block, at])
            sum_ref[2 + block, at] = narrow(own_ref[2 + block, at], up_ref[2 + block, at], last_down_ref[block, at])
    low, high = pl.ds(0, half), pl.ds(half, half)
    here = place_ref[0]
    ahead, across, behind = (lax.rem(here + step, 4) for step in (1, 2, 3))
    next_up[0] = sum_ref[across, low]
    next_up[1] = sum_ref[ahead, high]
    next_down[0] = sum_ref[across, high]
    next_down[1] = sum_ref[behind, low]
    next_mid[0] = sum_ref[ahead, low]
    next_mid[1] = sum_ref[behind, high]
    next_own[0] = sum_ref[here, low]
    next_own[1] = sum_ref[here, high]


def turn(place, own, up, down, last_up, last_down):
    rows, size = own.shape[1:]
    part = jax.ShapeDtypeStruct((2, rows // 2, size), own.dtype)
    return call(
        turn_kernel,
        "turn",
        (part,) * 4,
        [SMEM] + [VMEM] * 5,
        (place, own, up, down, last_up, last_down),
        scratch=[pltpu.VMEM(own.shape, own.dtype)],
        flops=2 * own.size,
        moved=8 * own.size,
    )


def pieces_kernel(*refs):
    out_ref = refs[-1]
    width = out_ref.shape[2]
    for side in range(2):
        own, up, down, last_up, last_down = refs[5 * side : 5 * side + 5]
        half = own.shape[1]
        for row in range(0, half, 32):
            at = pl.ds(row, 32)
            low = narrow(own[0, at], last_up[0, at], down[1, at])
            high = narrow(own[1, at], up[1, at], last_down[0, at])
            for piece in range(8):
                columns = slice(piece * width, (piece + 1) * width)
                out_ref[8 * side + piece, at] = low[:, columns]
                out_ref[8 * side + piece, pl.ds(half + row, 32)] = high[:, columns]


def make_pieces(*parts):
    rows, size = 2 * parts[0].shape[1], parts[0].shape[2]
    out = jax.ShapeDtypeStruct((16, rows, size // 8), jnp.bfloat16)
    return call(
        pieces_kernel, "pieces", out, [VMEM] * 10, parts, flops=4 * rows * size, moved=16 * rows * size
    )


def copy_blocks(grads_ref, moves, cut, sems):
    rows = grads_ref.shape[3] // cut
    copies = [
        pltpu.make_async_copy(
            grads_ref.at[where + (pl.ds(part * rows, rows),)],
            out.at[slot, pl.ds(part * rows, rows)],
            sems.at[cut * i + part],
        )
        for i, (where, out, slot) in enumerate(moves)
        for part in range(cut)
    ]
    for each in copies:
        each.start()
    for each in copies:
        each.wait()


def steps(place_ref, which):
    return tuple(lax.rem(place_ref[which] + step, 4) for step in range(4))


def trim_kernel(place_ref, table_ref, stats_ref, out_ref):
    rows = stats_ref.shape[0]
    half = rows // 2
    slot = lax.rem(2 * place_ref[2] + place_ref[3] + 8 - table_ref[0], 4)

    def block(at):
        return pl.ds(at % 4 * rows, rows)

    for index in range(4):

        @pl.when(slot == index)
        def _():
            out_ref[:, block(0)] = stats_ref[:, block(index)].astype(jnp.bfloat16)
            out_ref[:, block(1)] = stats_ref[:, block(index + 1)].astype(jnp.bfloat16)
            if index < 2:
                opposite = stats_ref[:, pl.ds((index + 2) * rows, half)]
            else:
                opposite = stats_ref[pl.ds(half, half), block(index + 2)].T
            out_ref[:, pl.ds(2 * rows, half)] = opposite.astype(jnp.bfloat16)


def trim(place, table, stats):
    rows = stats.shape[0]
    out = jax.ShapeDtypeStruct((rows, 2 * rows + rows // 2), jnp.bfloat16)
    return call(trim_kernel, "trim", out, [SMEM, SMEM, VMEM], (place, table, stats), flops=stats.size, moved=6 * stats.size)


def send_kernel(place_ref, grads_ref, x_up, x_down, y_up, y_down, sems):
    x, y = steps(place_ref, 0), steps(place_ref, 1)
    moves = []
    for i in range(2):
        moves += [
            ((0, i, x[2]), x_up, i),
            ((0, 2 + i, x[1]), x_up, 2 + i),
            ((0, 2 + i, x[2]), x_down, i),
            ((0, i, x[3]), x_down, 2 + i),
            ((1, y[2], i), y_up, i),
            ((1, y[1], 2 + i), y_up, 2 + i),
            ((1, y[2], 2 + i), y_down, i),
            ((1, y[3], i), y_down, 2 + i),
        ]
    copy_blocks(grads_ref, moves, 4, sems)


def keep_kernel(place_ref, grads_ref, x_mid, x_own, y_mid, y_own, sems):
    x, y = steps(place_ref, 0), steps(place_ref, 1)
    moves = []
    for i in range(2):
        moves += [
            ((0, i, x[1]), x_mid, i),
            ((0, 2 + i, x[3]), x_mid, 2 + i),
            ((1, y[1], i), y_mid, i),
            ((1, y[3], 2 + i), y_mid, 2 + i),
        ]
    for i in range(4):
        moves += [((0, i, x[0]), x_own, i), ((1, y[0], i), y_own, i)]
    copy_blocks(grads_ref, moves, 1, sems)


def pack(kernel, mib, place, grads):
    payload = jax.ShapeDtypeStruct((4,) + grads.shape[3:], grads.dtype)
    return call(
        kernel,
        kernel.__name__[:4],
        (payload,) * 4,
        [SMEM, HBM],
        (place, grads),
        scratch=[pltpu.SemaphoreType.DMA((64,))],
        mib=mib,
        moved=2**23,
    )


def root_kernel(place_ref, table_ref, *refs):
    given, (out_ref, right_ref, slots_ref, rights_ref, start_ref, first_ref, second_ref, third_ref, sem) = refs[:8], refs[8:]
    size = out_ref.shape[0]
    slot = size // 4
    half = slot // 2
    offset, zl, c = table_ref[0], place_ref[2], place_ref[3]

    def span(tile):
        return pl.ds(tile * slot, slot)

    for first_tile, to_ref in ((4, rights_ref), (0, slots_ref)):
        for tile in range(4):
            position = lax.rem(offset + first_tile + tile, 8)
            back = lax.rem(zl + 4 - lax.div(position, 2), 4)
            source = 2 * back + lax.rem(position + c, 2)
            for i, ref in enumerate(given):

                @pl.when(source == i)
                def _():
                    to_ref[tile] = ref[...]

    passed = pltpu.make_async_copy(rights_ref, right_ref, sem)
    passed.start()

    total = jnp.zeros((8, slot // 2), jnp.float32)
    for tile in range(4):
        values = slots_ref[tile].astype(jnp.float32)
        squares = values * values
        total = total + lanes(squares[:, :slot]) + 2.0 * lanes(squares[:, slot:])
    inverse = 1.0 / jnp.sqrt(jnp.sum(total))

    row_ids = lax.broadcasted_iota(jnp.int32, (slot, slot), 0)
    col_ids = lax.broadcasted_iota(jnp.int32, (slot, slot), 1)
    eye = jnp.where(row_ids == col_ids, 1.0, 0.0).astype(jnp.float32)

    def place(row, column, normed, diagonal):
        start_ref[span(row), span(column)] = normed.astype(jnp.bfloat16)
        term = 1.5 * eye - 0.5 * normed if diagonal else -0.5 * normed
        first_ref[span(row), span(column)] = term.astype(jnp.bfloat16)

    for tile in range(4):
        after = (tile + 1) % 4
        place(tile, tile, slots_ref[tile, :, :slot].astype(jnp.float32) * inverse, True)
        normed = slots_ref[tile, :, slot : 2 * slot].astype(jnp.float32) * inverse
        place(tile, after, normed, False)
        place(after, tile, normed.T, False)
    for tile in range(2):
        parts = [slots_ref[at, :, 2 * slot :].astype(jnp.float32) * inverse for at in (tile, tile + 2)]
        normed = jnp.concatenate(parts, axis=1)
        place(tile, tile + 2, normed, False)
        place(tile + 2, tile, normed.T, False)

    def eye_rows(tile):
        row_ids = lax.broadcasted_iota(jnp.int32, (slot, size), 0) + tile * slot
        col_ids = lax.broadcasted_iota(jnp.int32, (slot, size), 1)
        return jnp.where(row_ids == col_ids, 1.0, 0.0).astype(jnp.float32)

    for tile in range(4):
        product = jnp.dot(start_ref[span(tile), :], first_ref[...], preferred_element_type=jnp.float32)
        second_ref[span(tile), :] = product.astype(jnp.bfloat16)
    for tile in range(4):
        product = jnp.dot(first_ref[span(tile), :], second_ref[...], preferred_element_type=jnp.float32)
        third_ref[span(tile), :] = (1.5 * eye_rows(tile) - 0.5 * product).astype(jnp.bfloat16)
    for tile in range(4):
        product = jnp.dot(third_ref[span(tile), :], first_ref[...], preferred_element_type=jnp.float32)
        out_ref[span(tile), :] = product.astype(jnp.bfloat16)
    passed.wait()


def left_inverse_root(place, table, slots):
    rows, kept = slots[0].shape
    size = 4 * rows
    matrix, side = (size, size), (4, rows, kept)
    return pl.pallas_call(
        root_kernel,
        out_shape=(jax.ShapeDtypeStruct(matrix, jnp.bfloat16), jax.ShapeDtypeStruct(side, jnp.bfloat16)),
        in_specs=[SMEM] * 2 + [VMEM] * 8,
        out_specs=(VMEM, HBM),
        scratch_shapes=[pltpu.VMEM(side, jnp.bfloat16)] * 2
        + [pltpu.VMEM(matrix, jnp.bfloat16)] * 4
        + [pltpu.SemaphoreType.DMA(())],
        compiler_params=pltpu.CompilerParams(vmem_limit_bytes=18 * 2**20),
        cost_estimate=pl.CostEstimate(flops=6 * size**3, bytes_accessed=4 * size * size, transcendentals=0),
        name="left_root",
    )(place, table, *slots)


def base_kernel(slots_ref, first_ref, diagonal_ref):
    size = first_ref.shape[0]
    slot = size // 4

    def span(tile):
        return pl.ds(tile * slot, slot)

    total = jnp.zeros((8, slot // 2), jnp.float32)
    for tile in range(4):
        values = slots_ref[tile].astype(jnp.float32)
        squares = values * values
        total = total + lanes(squares[:, :slot]) + 2.0 * lanes(squares[:, slot:])
    inverse = 1.0 / jnp.sqrt(jnp.sum(total))

    row_ids = lax.broadcasted_iota(jnp.int32, (slot, slot), 0)
    col_ids = lax.broadcasted_iota(jnp.int32, (slot, slot), 1)
    eye = jnp.where(row_ids == col_ids, 1.0, 0.0).astype(jnp.float32)

    def place(row, column, normed):
        first_ref[span(row), span(column)] = (-0.5 * normed).astype(jnp.bfloat16)

    for tile in range(4):
        following = (tile + 1) % 4
        normed = slots_ref[tile, :, :slot].astype(jnp.float32) * inverse
        first = (1.5 * eye - 0.5 * normed).astype(jnp.bfloat16)
        first_ref[span(tile), span(tile)] = first
        start = normed.astype(jnp.bfloat16).astype(jnp.float32)
        both = eye * (start + 2.0 * first.astype(jnp.float32))
        row = jnp.sum(both, axis=0, keepdims=True)
        diagonal_ref[:, span(tile)] = jnp.broadcast_to(row, (diagonal_ref.shape[0], slot))
        normed = slots_ref[tile, :, slot : 2 * slot].astype(jnp.float32) * inverse
        place(tile, following, normed)
        place(following, tile, normed.T)
    for tile in range(2):
        parts = [slots_ref[at, :, 2 * slot :].astype(jnp.float32) * inverse for at in (tile, tile + 2)]
        normed = jnp.concatenate(parts, axis=1)
        place(tile, tile + 2, normed)
        place(tile + 2, tile, normed.T)


def right_base(slots):
    size = 4 * slots.shape[1]
    return call(
        base_kernel,
        "right_base",
        (jax.ShapeDtypeStruct((size, size), jnp.bfloat16), jax.ShapeDtypeStruct((8, size), jnp.float32)),
        [VMEM],
        (slots,),
        flops=4 * size * size,
        moved=4 * size * size,
    )


def lanes(squares):
    rows, columns = squares.shape
    total = jnp.sum(squares.reshape(rows // 8, 8, columns), axis=0)
    return sum(total[:, at : at + 128] for at in range(0, columns, 128))


def mix_kernel(pieces_ref, left_ref, out_ref, energy_ref, grad_ref):
    count, rows, _ = out_ref.shape
    energy = jnp.zeros(energy_ref.shape, jnp.float32)
    for piece in range(count):
        grad = narrow(pieces_ref[piece], pieces_ref[count + piece])
        grad_ref[pl.ds(piece * rows, rows), :] = grad
        wide = grad.astype(jnp.float32)
        energy = energy + lanes(wide * wide)
    energy_ref[...] = energy
    for piece in range(0, count, 2):
        product = jnp.dot(
            left_ref[pl.ds(piece * rows, 2 * rows), :], grad_ref[...], preferred_element_type=jnp.float32
        ).astype(jnp.bfloat16)
        out_ref[piece] = product[:rows]
        out_ref[piece + 1] = product[rows:]


def mix(pieces, left_root):
    _, rows, width = pieces.shape
    return call(
        mix_kernel,
        "mix",
        (jax.ShapeDtypeStruct((8, rows, width), jnp.bfloat16), jax.ShapeDtypeStruct((8, 128), jnp.float32)),
        [VMEM] * 2,
        (pieces, left_root),
        scratch=[pltpu.VMEM((8 * rows, width), jnp.bfloat16)],
        flops=2 * left_root.size * width,
        moved=2 * left_root.size,
    )


def condition_kernel(mixed_ref, first_ref, diagonal_ref, energy_ref, out_ref, totals_ref, wide_ref, even_ref, odd_ref):
    count, _, width = mixed_ref.shape
    for piece in range(count):
        odd_ref[:, pl.ds(piece * width, width)] = mixed_ref[piece]

    def products(slab_ref):
        for column in range(0, out_ref.shape[1], 2 * width):
            at = pl.ds(column, 2 * width)
            yield at, jnp.dot(slab_ref[...], first_ref[:, at], preferred_element_type=jnp.float32)

    for at, product in products(odd_ref):
        wide_ref[:, at] = product
        even_ref[:, at] = product.astype(jnp.bfloat16)
    for at, product in products(even_ref):
        odd_ref[:, at] = product.astype(jnp.bfloat16)
    for at, product in products(odd_ref):
        started = diagonal_ref[:1, at] * odd_ref[:, at].astype(jnp.float32) - 2.0 * product
        even_ref[:, at] = started.astype(jnp.bfloat16)
    total = jnp.zeros(energy_ref.shape, jnp.float32)
    for at, product in products(even_ref):
        precond = 1.5 * wide_ref[:, at] - 0.5 * product
        out_ref[:, at] = precond
        total = total + lanes(precond * precond)
    row_ids = lax.broadcasted_iota(jnp.int32, energy_ref.shape, 0)
    grad_sums = jnp.sum(energy_ref[...], axis=0, keepdims=True)
    cond_sums = jnp.sum(total, axis=0, keepdims=True)
    sums = jnp.where(row_ids == 0, grad_sums, jnp.where(row_ids == 1, cond_sums, 0.0))
    for piece in range(count):
        totals_ref[piece] = sums


def condition(mixed, first, diagonal, energy):
    _, rows, width = mixed.shape
    slab = (rows, 8 * width)
    return call(
        condition_kernel,
        "condition",
        (jax.ShapeDtypeStruct(slab, jnp.float32), jax.ShapeDtypeStruct((8, 8, 128), jnp.float32)),
        [VMEM] * 4,
        (mixed, first, diagonal, energy),
        scratch=[pltpu.VMEM(slab, jnp.float32), pltpu.VMEM(slab, jnp.bfloat16), pltpu.VMEM(slab, jnp.bfloat16)],
        flops=8 * rows * first.size,
        moved=2 * first.size,
    )


def finish_kernel(count, totals_ref, precond_ref, out_ref):
    totals = sum(totals_ref[piece] for piece in range(totals_ref.shape[0]))
    grad_mean = jnp.sum(totals[:1]) / count
    cond_mean = jnp.sum(totals[1:2]) / count
    factor = jnp.sqrt(grad_mean / (cond_mean + 1e-06))
    for row in range(0, out_ref.shape[0], 32):
        at = pl.ds(row, 32)
        out_ref[at] = precond_ref[at] * factor


def finish(totals, precond, count):
    return call(
        functools.partial(finish_kernel, count),
        "finish",
        jax.ShapeDtypeStruct(precond.shape, jnp.float32),
        [VMEM] * 2,
        (totals, precond),
        flops=precond.size,
        moved=8 * precond.size,
    )


def after(dep, *values):
    return lax.optimization_barrier((dep,) + values)[1:]


def local(grad_partial, factor_stats, owner_table):
    size = grad_partial.shape[3]
    rows_here = grad_partial.shape[2]
    owner = ("zl", "c")
    grads = grad_partial.reshape(2, 4, 4, rows_here, size)
    x, y, zl, c = (lax.axis_index(axis).astype(jnp.int32) for axis in ("x", "y", "zl", "c"))
    place = jnp.stack((x, y, zl, c))

    x_up, x_down, y_up, y_down = pack(send_kernel, 48, place, grads)
    x_ends = ring_first(x_up, x_down, "x")
    y_ends = ring_first(y_up, y_down, "y")

    (sent,) = after(x_up, place)
    near = [trim(sent, owner_table, factor_stats[0, 0])]
    near.append(shift(near[0], "zl", 1))
    x_mid, x_own, y_mid, y_own = pack(keep_kernel, 16, sent, grads)
    near.append(shift(*after(x_mid, near[1]), "zl", 1))
    near.append(shift(near[2], "zl", 1))
    (x_mid,) = after(near[2], x_mid)
    x_last = pass_on(x_mid, *x_ends)
    y_last = pass_on(y_mid, *y_ends)
    far = [swap(each, "c", 1) for each in near[:3]]
    far.append(swap(*after(x_last[0], near[3]), "c", 1))
    slots = tuple(each for pair in zip(near, far) for each in pair)

    x_last = ring_first(*x_last, "x")
    y_last = ring_first(*y_last, "y")

    lower_up, lower_down, lower_mid, lower_own = turn(y[None], x_own, *x_ends, *x_last)
    lower_ends = ring_first(lower_up, lower_down, "y")
    upper_up, upper_down, upper_mid, upper_own = turn(x[None], y_own, *y_ends, *y_last)
    upper_ends = ring_first(upper_up, upper_down, "x")
    lower_last = ring_first(*pass_on(lower_mid, *lower_ends), "y")
    upper_last = ring_first(*pass_on(upper_mid, *upper_ends), "x")
    pieces = make_pieces(lower_own, *lower_ends, *lower_last, upper_own, *upper_ends, *upper_last)

    slots = after(pieces, *slots)
    pieces = lax.all_to_all(pieces, ("zh",) + owner, split_axis=0, concat_axis=0, tiled=True)
    left_root, right_slots = left_inverse_root(place, owner_table, slots)
    mixed, energy = mix(pieces, left_root)
    right = right_base(*after(mixed, right_slots))
    mixed = lax.all_to_all(mixed, owner, split_axis=0, concat_axis=0, tiled=True)
    precond, totals = condition(mixed, *right, energy)
    totals = lax.all_to_all(totals, owner, split_axis=0, concat_axis=0, tiled=True)
    return finish(totals, precond, float(size * size))[None]


def solution(mesh):
    dp, owner = ("zh", "y", "x"), ("zl", "c")
    placed = (P(dp, None, owner, None), P(dp, owner, None, None), P(dp))
    return jax.shard_map(
        local, mesh=fine_mesh(mesh), in_specs=placed, out_specs=P(dp, owner, None), check_vma=False
    )
```

```python
import functools

import jax
import jax.numpy as jnp
from jax import lax
from jax.experimental import pallas as pl
from jax.experimental.pallas import tpu as pltpu
from jax.sharding import Mesh
from jax.sharding import PartitionSpec as P

FINE = ("zh", "y", "x", "zl", "c")


def fine_mesh(mesh):
    return Mesh(mesh.devices.reshape(2, 4, 4, 4, 2), FINE)


def shift(array, axis, step):
    size = lax.axis_size(axis)
    return lax.ppermute(array, axis, [(i, (i + step) % size) for i in range(size)])


def swap(array, axis, mask):
    size = lax.axis_size(axis)
    return lax.ppermute(array, axis, [(i, i ^ mask) for i in range(size)])


def f32sum(*terms):
    total = terms[0].astype(jnp.float32)
    for term in terms[1:]:
        total = total + term.astype(jnp.float32)
    return total


def narrow(*terms):
    return f32sum(*terms).astype(jnp.bfloat16)


VMEM = pl.BlockSpec(memory_space=pltpu.VMEM)
SMEM = pl.BlockSpec(memory_space=pltpu.SMEM)
HBM = pl.BlockSpec(memory_space=pltpu.HBM)


def call(kernel, name, out_shape, in_specs, operands, scratch=(), mib=16, flops=0, moved=0):
    outs = (VMEM,) * len(out_shape) if isinstance(out_shape, tuple) else VMEM
    return pl.pallas_call(
        kernel,
        out_shape=out_shape,
        in_specs=in_specs,
        out_specs=outs,
        scratch_shapes=list(scratch),
        compiler_params=pltpu.CompilerParams(vmem_limit_bytes=mib * 2**20),
        cost_estimate=pl.CostEstimate(flops=flops, bytes_accessed=moved, transcendentals=0),
        name=name,
    )(*operands)


def ring_first(up, down, axis):
    return shift(up, axis, 1), shift(down, axis, -1)


def pass_kernel(mid_ref, up_ref, down_ref, last_up_ref, last_down_ref):
    count, rows, _ = last_up_ref.shape
    for block in range(count):
        for row in range(0, rows, 32):
            at = pl.ds(row, 32)
            last_up_ref[block, at] = narrow(mid_ref[block, at], up_ref[block, at])
            last_down_ref[block, at] = narrow(mid_ref[count + block, at], down_ref[block, at])


def pass_on(mid, up, down):
    count = mid.shape[0] // 2
    last = jax.ShapeDtypeStruct((count,) + mid.shape[1:], mid.dtype)
    last_up, last_down = call(
        pass_kernel, "pass_on", (last, last), [VMEM] * 3, (mid, up, down), flops=mid.size, moved=6 * mid.size
    )
    return last_up, last_down


def turn_kernel(place_ref, own_ref, up_ref, down_ref, last_up_ref, last_down_ref, next_up, next_down, next_mid, next_own, sum_ref):
    rows = own_ref.shape[1]
    half = rows // 2
    for block in range(2):
        for row in range(0, rows, 32):
            at = pl.ds(row, 32)
            sum_ref[block, at] = narrow(own_ref[block, at], last_up_ref[block, at], down_ref[2 + block, at])
            sum_ref[2 + block, at] = narrow(own_ref[2 + block, at], up_ref[2 + block, at], last_down_ref[block, at])
    low, high = pl.ds(0, half), pl.ds(half, half)
    here = place_ref[0]
    ahead, across, behind = (lax.rem(here + step, 4) for step in (1, 2, 3))
    next_up[0] = sum_ref[across, low]
    next_up[1] = sum_ref[ahead, high]
    next_down[0] = sum_ref[across, high]
    next_down[1] = sum_ref[behind, low]
    next_mid[0] = sum_ref[ahead, low]
    next_mid[1] = sum_ref[behind, high]
    next_own[0] = sum_ref[here, low]
    next_own[1] = sum_ref[here, high]


def turn(place, own, up, down, last_up, last_down):
    rows, size = own.shape[1:]
    part = jax.ShapeDtypeStruct((2, rows // 2, size), own.dtype)
    return call(
        turn_kernel,
        "turn",
        (part,) * 4,
        [SMEM] + [VMEM] * 5,
        (place, own, up, down, last_up, last_down),
        scratch=[pltpu.VMEM(own.shape, own.dtype)],
        flops=2 * own.size,
        moved=8 * own.size,
    )


def pieces_kernel(*refs):
    out_ref = refs[-1]
    width = out_ref.shape[2]
    for side in range(2):
        own, up, down, last_up, last_down = refs[5 * side : 5 * side + 5]
        half = own.shape[1]
        for row in range(0, half, 32):
            at = pl.ds(row, 32)
            low = narrow(own[0, at], last_up[0, at], down[1, at])
            high = narrow(own[1, at], up[1, at], last_down[0, at])
            for piece in range(8):
                columns = slice(piece * width, (piece + 1) * width)
                out_ref[8 * side + piece, at] = low[:, columns]
                out_ref[8 * side + piece, pl.ds(half + row, 32)] = high[:, columns]


def make_pieces(*parts):
    rows, size = 2 * parts[0].shape[1], parts[0].shape[2]
    out = jax.ShapeDtypeStruct((16, rows, size // 8), jnp.bfloat16)
    return call(
        pieces_kernel, "pieces", out, [VMEM] * 10, parts, flops=4 * rows * size, moved=16 * rows * size
    )


def copy_blocks(grads_ref, moves, cut, sems):
    rows = grads_ref.shape[3] // cut
    copies = [
        pltpu.make_async_copy(
            grads_ref.at[where + (pl.ds(part * rows, rows),)],
            out.at[slot, pl.ds(part * rows, rows)],
            sems.at[cut * i + part],
        )
        for i, (where, out, slot) in enumerate(moves)
        for part in range(cut)
    ]
    for each in copies:
        each.start()
    for each in copies:
        each.wait()


def steps(place_ref, which):
    return tuple(lax.rem(place_ref[which] + step, 4) for step in range(4))


def trim_kernel(place_ref, table_ref, stats_ref, out_ref):
    rows = stats_ref.shape[0]
    half = rows // 2
    slot = lax.rem(2 * place_ref[2] + place_ref[3] + 8 - table_ref[0], 4)

    def block(at):
        return pl.ds(at % 4 * rows, rows)

    for index in range(4):

        @pl.when(slot == index)
        def _():
            out_ref[:, block(0)] = stats_ref[:, block(index)].astype(jnp.bfloat16)
            out_ref[:, block(1)] = stats_ref[:, block(index + 1)].astype(jnp.bfloat16)
            if index < 2:
                opposite = stats_ref[:, pl.ds((index + 2) * rows, half)]
            else:
                opposite = stats_ref[pl.ds(half, half), block(index + 2)].T
            out_ref[:, pl.ds(2 * rows, half)] = opposite.astype(jnp.bfloat16)


def trim(place, table, stats):
    rows = stats.shape[0]
    out = jax.ShapeDtypeStruct((rows, 2 * rows + rows // 2), jnp.bfloat16)
    return call(trim_kernel, "trim", out, [SMEM, SMEM, VMEM], (place, table, stats), flops=stats.size, moved=6 * stats.size)


def send_kernel(place_ref, grads_ref, x_up, x_down, y_up, y_down, sems):
    x, y = steps(place_ref, 0), steps(place_ref, 1)
    moves = []
    for i in range(2):
        moves += [
            ((0, i, x[2]), x_up, i),
            ((0, 2 + i, x[1]), x_up, 2 + i),
            ((0, 2 + i, x[2]), x_down, i),
            ((0, i, x[3]), x_down, 2 + i),
            ((1, y[2], i), y_up, i),
            ((1, y[1], 2 + i), y_up, 2 + i),
            ((1, y[2], 2 + i), y_down, i),
            ((1, y[3], i), y_down, 2 + i),
        ]
    copy_blocks(grads_ref, moves, 4, sems)


def keep_kernel(place_ref, grads_ref, x_mid, x_own, y_mid, y_own, sems):
    x, y = steps(place_ref, 0), steps(place_ref, 1)
    moves = []
    for i in range(2):
        moves += [
            ((0, i, x[1]), x_mid, i),
            ((0, 2 + i, x[3]), x_mid, 2 + i),
            ((1, y[1], i), y_mid, i),
            ((1, y[3], 2 + i), y_mid, 2 + i),
        ]
    for i in range(4):
        moves += [((0, i, x[0]), x_own, i), ((1, y[0], i), y_own, i)]
    copy_blocks(grads_ref, moves, 1, sems)


def pack(kernel, mib, place, grads):
    payload = jax.ShapeDtypeStruct((4,) + grads.shape[3:], grads.dtype)
    return call(
        kernel,
        kernel.__name__[:4],
        (payload,) * 4,
        [SMEM, HBM],
        (place, grads),
        scratch=[pltpu.SemaphoreType.DMA((64,))],
        mib=mib,
        moved=2**23,
    )


def root_kernel(place_ref, table_ref, *refs):
    given, (out_ref, right_ref, slots_ref, rights_ref, start_ref, first_ref, second_ref, third_ref, sem) = refs[:8], refs[8:]
    size = out_ref.shape[0]
    slot = size // 4
    half = slot // 2
    offset, zl, c = table_ref[0], place_ref[2], place_ref[3]

    def span(tile):
        return pl.ds(tile * slot, slot)

    for first_tile, to_ref in ((4, rights_ref), (0, slots_ref)):
        for tile in range(4):
            position = lax.rem(offset + first_tile + tile, 8)
            back = lax.rem(zl + 4 - lax.div(position, 2), 4)
            source = 2 * back + lax.rem(position + c, 2)
            for i, ref in enumerate(given):

                @pl.when(source == i)
                def _():
                    to_ref[tile] = ref[...]

    passed = pltpu.make_async_copy(rights_ref, right_ref, sem)
    passed.start()

    total = jnp.zeros((8, slot // 2), jnp.float32)
    for tile in range(4):
        values = slots_ref[tile].astype(jnp.float32)
        squares = values * values
        total = total + lanes(squares[:, :slot]) + 2.0 * lanes(squares[:, slot:])
    inverse = 1.0 / jnp.sqrt(jnp.sum(total))

    row_ids = lax.broadcasted_iota(jnp.int32, (slot, slot), 0)
    col_ids = lax.broadcasted_iota(jnp.int32, (slot, slot), 1)
    eye = jnp.where(row_ids == col_ids, 1.0, 0.0).astype(jnp.float32)

    def place(row, column, normed, diagonal):
        start_ref[span(row), span(column)] = normed.astype(jnp.bfloat16)
        term = 1.5 * eye - 0.5 * normed if diagonal else -0.5 * normed
        first_ref[span(row), span(column)] = term.astype(jnp.bfloat16)

    for tile in range(4):
        after = (tile + 1) % 4
        place(tile, tile, slots_ref[tile, :, :slot].astype(jnp.float32) * inverse, True)
        normed = slots_ref[tile, :, slot : 2 * slot].astype(jnp.float32) * inverse
        place(tile, after, normed, False)
        place(after, tile, normed.T, False)
    for tile in range(2):
        parts = [slots_ref[at, :, 2 * slot :].astype(jnp.float32) * inverse for at in (tile, tile + 2)]
        normed = jnp.concatenate(parts, axis=1)
        place(tile, tile + 2, normed, False)
        place(tile + 2, tile, normed.T, False)

    def eye_rows(tile):
        row_ids = lax.broadcasted_iota(jnp.int32, (slot, size), 0) + tile * slot
        col_ids = lax.broadcasted_iota(jnp.int32, (slot, size), 1)
        return jnp.where(row_ids == col_ids, 1.0, 0.0).astype(jnp.float32)

    for tile in range(4):
        product = jnp.dot(start_ref[span(tile), :], first_ref[...], preferred_element_type=jnp.float32)
        second_ref[span(tile), :] = product.astype(jnp.bfloat16)
    for tile in range(4):
        product = jnp.dot(first_ref[span(tile), :], second_ref[...], preferred_element_type=jnp.float32)
        third_ref[span(tile), :] = (1.5 * eye_rows(tile) - 0.5 * product).astype(jnp.bfloat16)
    for tile in range(4):
        product = jnp.dot(third_ref[span(tile), :], first_ref[...], preferred_element_type=jnp.float32)
        out_ref[span(tile), :] = product.astype(jnp.bfloat16)
    passed.wait()


def left_inverse_root(place, table, slots):
    rows, kept = slots[0].shape
    size = 4 * rows
    matrix, side = (size, size), (4, rows, kept)
    return pl.pallas_call(
        root_kernel,
        out_shape=(jax.ShapeDtypeStruct(matrix, jnp.bfloat16), jax.ShapeDtypeStruct(side, jnp.bfloat16)),
        in_specs=[SMEM] * 2 + [VMEM] * 8,
        out_specs=(VMEM, HBM),
        scratch_shapes=[pltpu.VMEM(side, jnp.bfloat16)] * 2
        + [pltpu.VMEM(matrix, jnp.bfloat16)] * 4
        + [pltpu.SemaphoreType.DMA(())],
        compiler_params=pltpu.CompilerParams(vmem_limit_bytes=18 * 2**20),
        cost_estimate=pl.CostEstimate(flops=6 * size**3, bytes_accessed=4 * size * size, transcendentals=0),
        name="left_root",
    )(place, table, *slots)


def base_kernel(slots_ref, first_ref, diagonal_ref):
    size = first_ref.shape[0]
    slot = size // 4

    def span(tile):
        return pl.ds(tile * slot, slot)

    total = jnp.zeros((8, slot // 2), jnp.float32)
    for tile in range(4):
        values = slots_ref[tile].astype(jnp.float32)
        squares = values * values
        total = total + lanes(squares[:, :slot]) + 2.0 * lanes(squares[:, slot:])
    inverse = 1.0 / jnp.sqrt(jnp.sum(total))

    row_ids = lax.broadcasted_iota(jnp.int32, (slot, slot), 0)
    col_ids = lax.broadcasted_iota(jnp.int32, (slot, slot), 1)
    eye = jnp.where(row_ids == col_ids, 1.0, 0.0).astype(jnp.float32)

    def place(row, column, normed):
        first_ref[span(row), span(column)] = (-0.5 * normed).astype(jnp.bfloat16)

    for tile in range(4):
        following = (tile + 1) % 4
        normed = slots_ref[tile, :, :slot].astype(jnp.float32) * inverse
        first = (1.5 * eye - 0.5 * normed).astype(jnp.bfloat16)
        first_ref[span(tile), span(tile)] = first
        start = normed.astype(jnp.bfloat16).astype(jnp.float32)
        both = eye * (start + 2.0 * first.astype(jnp.float32))
        row = jnp.sum(both, axis=0, keepdims=True)
        diagonal_ref[:, span(tile)] = jnp.broadcast_to(row, (diagonal_ref.shape[0], slot))
        normed = slots_ref[tile, :, slot : 2 * slot].astype(jnp.float32) * inverse
        place(tile, following, normed)
        place(following, tile, normed.T)
    for tile in range(2):
        parts = [slots_ref[at, :, 2 * slot :].astype(jnp.float32) * inverse for at in (tile, tile + 2)]
        normed = jnp.concatenate(parts, axis=1)
        place(tile, tile + 2, normed)
        place(tile + 2, tile, normed.T)


def right_base(slots):
    size = 4 * slots.shape[1]
    return call(
        base_kernel,
        "right_base",
        (jax.ShapeDtypeStruct((size, size), jnp.bfloat16), jax.ShapeDtypeStruct((8, size), jnp.float32)),
        [VMEM],
        (slots,),
        flops=4 * size * size,
        moved=4 * size * size,
    )


def lanes(squares):
    rows, columns = squares.shape
    total = jnp.sum(squares.reshape(rows // 8, 8, columns), axis=0)
    return sum(total[:, at : at + 128] for at in range(0, columns, 128))


def mix_kernel(zl_ref, pieces_ref, left_ref, *refs):
    out_refs, (energy_ref, grad_ref, held_ref) = refs[:4], refs[4:]
    count, rows = pieces_ref.shape[0] // 2, pieces_ref.shape[1]
    energy = jnp.zeros(energy_ref.shape, jnp.float32)
    for piece in range(count):
        grad = narrow(pieces_ref[piece], pieces_ref[count + piece])
        grad_ref[pl.ds(piece * rows, rows), :] = grad
        wide = grad.astype(jnp.float32)
        energy = energy + lanes(wide * wide)
    energy_ref[...] = energy
    for piece in range(0, count, 2):
        product = jnp.dot(
            left_ref[pl.ds(piece * rows, 2 * rows), :], grad_ref[...], preferred_element_type=jnp.float32
        ).astype(jnp.bfloat16)
        held_ref[piece // 2, 0] = product[:rows]
        held_ref[piece // 2, 1] = product[rows:]
    for step, out_ref in enumerate(out_refs):
        out_ref[...] = held_ref[lax.rem(zl_ref[0] + step, 4)]


def mix(zl, pieces, left_root):
    _, rows, width = pieces.shape
    out = jax.ShapeDtypeStruct((2, rows, width), jnp.bfloat16)
    return call(
        mix_kernel,
        "mix",
        (out,) * 4 + (jax.ShapeDtypeStruct((8, 128), jnp.float32),),
        [SMEM] + [VMEM] * 2,
        (zl, pieces, left_root),
        scratch=[pltpu.VMEM((8 * rows, width), jnp.bfloat16), pltpu.VMEM((4,) + out.shape, jnp.bfloat16)],
        flops=2 * left_root.size * width,
        moved=2 * left_root.size,
    )


def split_kernel(c_ref, *refs):
    got, out_ref = refs[:4], refs[4]
    for step, ref in enumerate(got):
        out_ref[step] = ref[1 - c_ref[0]]


def exchange(c, mixed, dep):
    got = after(dep, mixed[0]) + tuple(shift(each, "zl", step) for step, each in enumerate(mixed) if step)
    give = jax.ShapeDtypeStruct((4,) + mixed[0].shape[1:], mixed[0].dtype)
    give = call(split_kernel, "split", give, [SMEM] + [VMEM] * 4, (c,) + got, moved=4 * give.size)
    return got + (swap(give, "c", 1),)


def condition_kernel(zl_ref, c_ref, *refs):
    got, other_ref, refs = refs[:4], refs[4], refs[5:]
    first_ref, diagonal_ref, energy_ref, out_ref, totals_ref, wide_ref, even_ref, odd_ref, held_ref = refs
    count, _, width = held_ref.shape
    zl, c = zl_ref[0], c_ref[0]
    for step, ref in enumerate(got):
        chip = lax.rem(zl + (4 - step), 4)
        held_ref[2 * chip + c] = ref[c]
        held_ref[2 * chip + 1 - c] = other_ref[step]
    for piece in range(count):
        odd_ref[:, pl.ds(piece * width, width)] = held_ref[piece]

    def products(slab_ref):
        for column in range(0, out_ref.shape[1], 2 * width):
            at = pl.ds(column, 2 * width)
            yield at, jnp.dot(slab_ref[...], first_ref[:, at], preferred_element_type=jnp.float32)

    for at, product in products(odd_ref):
        wide_ref[:, at] = product
        even_ref[:, at] = product.astype(jnp.bfloat16)
    for at, product in products(even_ref):
        odd_ref[:, at] = product.astype(jnp.bfloat16)
    for at, product in products(odd_ref):
        started = diagonal_ref[:1, at] * odd_ref[:, at].astype(jnp.float32) - 2.0 * product
        even_ref[:, at] = started.astype(jnp.bfloat16)
    total = jnp.zeros(energy_ref.shape, jnp.float32)
    for at, product in products(even_ref):
        precond = 1.5 * wide_ref[:, at] - 0.5 * product
        out_ref[:, at] = precond
        total = total + lanes(precond * precond)
    row_ids = lax.broadcasted_iota(jnp.int32, energy_ref.shape, 0)
    grad_sums = jnp.sum(energy_ref[...], axis=0, keepdims=True)
    cond_sums = jnp.sum(total, axis=0, keepdims=True)
    sums = jnp.where(row_ids == 0, grad_sums, jnp.where(row_ids == 1, cond_sums, 0.0))
    for piece in range(count):
        totals_ref[piece] = sums


def condition(zl, c, mixed, first, diagonal, energy):
    _, rows, width = mixed[0].shape
    slab = (rows, 8 * width)
    return call(
        condition_kernel,
        "condition",
        (jax.ShapeDtypeStruct(slab, jnp.float32), jax.ShapeDtypeStruct((8, 8, 128), jnp.float32)),
        [SMEM] * 2 + [VMEM] * 8,
        (zl, c) + mixed + (first, diagonal, energy),
        scratch=[pltpu.VMEM(slab, jnp.float32), pltpu.VMEM(slab, jnp.bfloat16), pltpu.VMEM(slab, jnp.bfloat16), pltpu.VMEM((8, rows, width), jnp.bfloat16)],
        flops=8 * rows * first.size,
        moved=2 * first.size,
    )


def finish_kernel(count, totals_ref, precond_ref, out_ref):
    totals = sum(totals_ref[piece] for piece in range(totals_ref.shape[0]))
    grad_mean = jnp.sum(totals[:1]) / count
    cond_mean = jnp.sum(totals[1:2]) / count
    factor = jnp.sqrt(grad_mean / (cond_mean + 1e-06))
    for row in range(0, out_ref.shape[0], 32):
        at = pl.ds(row, 32)
        out_ref[at] = precond_ref[at] * factor


def finish(totals, precond, count):
    return call(
        functools.partial(finish_kernel, count),
        "finish",
        jax.ShapeDtypeStruct(precond.shape, jnp.float32),
        [VMEM] * 2,
        (totals, precond),
        flops=precond.size,
        moved=8 * precond.size,
    )


def after(dep, *values):
    return lax.optimization_barrier((dep,) + values)[1:]


def local(grad_partial, factor_stats, owner_table):
    size = grad_partial.shape[3]
    rows_here = grad_partial.shape[2]
    owner = ("zl", "c")
    grads = grad_partial.reshape(2, 4, 4, rows_here, size)
    x, y, zl, c = (lax.axis_index(axis).astype(jnp.int32) for axis in ("x", "y", "zl", "c"))
    place = jnp.stack((x, y, zl, c))

    x_up, x_down, y_up, y_down = pack(send_kernel, 48, place, grads)
    x_ends = ring_first(x_up, x_down, "x")
    y_ends = ring_first(y_up, y_down, "y")

    (sent,) = after(x_up, place)
    near = [trim(sent, owner_table, factor_stats[0, 0])]
    near.append(shift(near[0], "zl", 1))
    x_mid, x_own, y_mid, y_own = pack(keep_kernel, 16, sent, grads)
    near.append(shift(*after(x_mid, near[1]), "zl", 1))
    near.append(shift(near[2], "zl", 1))
    (x_mid,) = after(near[2], x_mid)
    x_last = pass_on(x_mid, *x_ends)
    y_last = pass_on(y_mid, *y_ends)
    far = [swap(each, "c", 1) for each in near[:3]]
    far.append(swap(*after(x_last[0], near[3]), "c", 1))
    slots = tuple(each for pair in zip(near, far) for each in pair)

    x_last = ring_first(*x_last, "x")
    y_last = ring_first(*y_last, "y")

    lower_up, lower_down, lower_mid, lower_own = turn(y[None], x_own, *x_ends, *x_last)
    lower_ends = ring_first(lower_up, lower_down, "y")
    upper_up, upper_down, upper_mid, upper_own = turn(x[None], y_own, *y_ends, *y_last)
    upper_ends = ring_first(upper_up, upper_down, "x")
    lower_last = ring_first(*pass_on(lower_mid, *lower_ends), "y")
    upper_last = ring_first(*pass_on(upper_mid, *upper_ends), "x")
    pieces = make_pieces(lower_own, *lower_ends, *lower_last, upper_own, *upper_ends, *upper_last)

    slots = after(pieces, *slots)
    pieces = lax.all_to_all(pieces, ("zh",) + owner, split_axis=0, concat_axis=0, tiled=True)
    left_root, right_slots = left_inverse_root(place, owner_table, slots)
    *mixed, energy = mix(zl[None], pieces, left_root)
    right = right_base(*after(mixed[0], right_slots))
    mixed = exchange(c[None], tuple(mixed), right[0])
    precond, totals = condition(zl[None], c[None], mixed, *right, energy)
    totals = lax.all_to_all(totals, owner, split_axis=0, concat_axis=0, tiled=True)
    return finish(totals, precond, float(size * size))[None]


def solution(mesh):
    dp, owner = ("zh", "y", "x"), ("zl", "c")
    placed = (P(dp, None, owner, None), P(dp, owner, None, None), P(dp))
    return jax.shard_map(
        local, mesh=fine_mesh(mesh), in_specs=placed, out_specs=P(dp, owner, None), check_vma=False
    )
```

```python
import functools

import jax
import jax.numpy as jnp
from jax import lax
from jax.experimental import pallas as pl
from jax.experimental.pallas import tpu as pltpu
from jax.sharding import Mesh
from jax.sharding import PartitionSpec as P

FINE = ("zh", "y", "x", "zl", "c")


def fine_mesh(mesh):
    return Mesh(mesh.devices.reshape(2, 4, 4, 4, 2), FINE)


def shift(array, axis, step):
    size = lax.axis_size(axis)
    return lax.ppermute(array, axis, [(i, (i + step) % size) for i in range(size)])


def swap(array, axis, mask):
    size = lax.axis_size(axis)
    return lax.ppermute(array, axis, [(i, i ^ mask) for i in range(size)])


def f32sum(*terms):
    total = terms[0].astype(jnp.float32)
    for term in terms[1:]:
        total = total + term.astype(jnp.float32)
    return total


def narrow(*terms):
    return f32sum(*terms).astype(jnp.bfloat16)


VMEM = pl.BlockSpec(memory_space=pltpu.VMEM)
SMEM = pl.BlockSpec(memory_space=pltpu.SMEM)
HBM = pl.BlockSpec(memory_space=pltpu.HBM)


def call(kernel, name, out_shape, in_specs, operands, scratch=(), mib=16, flops=0, moved=0):
    outs = (VMEM,) * len(out_shape) if isinstance(out_shape, tuple) else VMEM
    return pl.pallas_call(
        kernel,
        out_shape=out_shape,
        in_specs=in_specs,
        out_specs=outs,
        scratch_shapes=list(scratch),
        compiler_params=pltpu.CompilerParams(vmem_limit_bytes=mib * 2**20),
        cost_estimate=pl.CostEstimate(flops=flops, bytes_accessed=moved, transcendentals=0),
        name=name,
    )(*operands)


def ring_first(up, down, axis):
    return shift(up, axis, 1), shift(down, axis, -1)


def pass_kernel(mid_ref, up_ref, down_ref, last_up_ref, last_down_ref):
    count, rows, _ = last_up_ref.shape
    for block in range(count):
        for row in range(0, rows, 32):
            at = pl.ds(row, 32)
            last_up_ref[block, at] = narrow(mid_ref[block, at], up_ref[block, at])
            last_down_ref[block, at] = narrow(mid_ref[count + block, at], down_ref[block, at])


def pass_on(mid, up, down):
    count = mid.shape[0] // 2
    last = jax.ShapeDtypeStruct((count,) + mid.shape[1:], mid.dtype)
    last_up, last_down = call(
        pass_kernel, "pass_on", (last, last), [VMEM] * 3, (mid, up, down), flops=mid.size, moved=6 * mid.size
    )
    return last_up, last_down


def turn_kernel(place_ref, own_ref, up_ref, down_ref, last_up_ref, last_down_ref, next_up, next_down, next_mid, next_own, sum_ref):
    rows = own_ref.shape[1]
    half = rows // 2
    for block in range(2):
        for row in range(0, rows, 32):
            at = pl.ds(row, 32)
            sum_ref[block, at] = narrow(own_ref[block, at], last_up_ref[block, at], down_ref[2 + block, at])
            sum_ref[2 + block, at] = narrow(own_ref[2 + block, at], up_ref[2 + block, at], last_down_ref[block, at])
    low, high = pl.ds(0, half), pl.ds(half, half)
    here = place_ref[0]
    ahead, across, behind = (lax.rem(here + step, 4) for step in (1, 2, 3))
    next_up[0] = sum_ref[across, low]
    next_up[1] = sum_ref[ahead, high]
    next_down[0] = sum_ref[across, high]
    next_down[1] = sum_ref[behind, low]
    next_mid[0] = sum_ref[ahead, low]
    next_mid[1] = sum_ref[behind, high]
    next_own[0] = sum_ref[here, low]
    next_own[1] = sum_ref[here, high]


def turn(place, own, up, down, last_up, last_down):
    rows, size = own.shape[1:]
    part = jax.ShapeDtypeStruct((2, rows // 2, size), own.dtype)
    return call(
        turn_kernel,
        "turn",
        (part,) * 4,
        [SMEM] + [VMEM] * 5,
        (place, own, up, down, last_up, last_down),
        scratch=[pltpu.VMEM(own.shape, own.dtype)],
        flops=2 * own.size,
        moved=8 * own.size,
    )


def pieces_kernel(*refs):
    out_ref = refs[-1]
    width = out_ref.shape[2]
    for side in range(2):
        own, up, down, last_up, last_down = refs[5 * side : 5 * side + 5]
        half = own.shape[1]
        for row in range(0, half, 32):
            at = pl.ds(row, 32)
            low = narrow(own[0, at], last_up[0, at], down[1, at])
            high = narrow(own[1, at], up[1, at], last_down[0, at])
            for piece in range(8):
                columns = slice(piece * width, (piece + 1) * width)
                out_ref[8 * side + piece, at] = low[:, columns]
                out_ref[8 * side + piece, pl.ds(half + row, 32)] = high[:, columns]


def make_pieces(*parts):
    rows, size = 2 * parts[0].shape[1], parts[0].shape[2]
    out = jax.ShapeDtypeStruct((16, rows, size // 8), jnp.bfloat16)
    return call(
        pieces_kernel, "pieces", out, [VMEM] * 10, parts, flops=4 * rows * size, moved=16 * rows * size
    )


def copy_blocks(grads_ref, moves, cut, sems):
    rows = grads_ref.shape[3] // cut
    copies = [
        pltpu.make_async_copy(
            grads_ref.at[where + (pl.ds(part * rows, rows),)],
            out.at[slot, pl.ds(part * rows, rows)],
            sems.at[cut * i + part],
        )
        for i, (where, out, slot) in enumerate(moves)
        for part in range(cut)
    ]
    for each in copies:
        each.start()
    for each in copies:
        each.wait()


def steps(place_ref, which):
    return tuple(lax.rem(place_ref[which] + step, 4) for step in range(4))


def trim_kernel(place_ref, table_ref, stats_ref, out_ref):
    rows = stats_ref.shape[0]
    half = rows // 2
    slot = lax.rem(2 * place_ref[2] + place_ref[3] + 8 - table_ref[0], 4)

    def block(at):
        return pl.ds(at % 4 * rows, rows)

    for index in range(4):

        @pl.when(slot == index)
        def _():
            out_ref[:, block(0)] = stats_ref[:, block(index)].astype(jnp.bfloat16)
            out_ref[:, block(1)] = stats_ref[:, block(index + 1)].astype(jnp.bfloat16)
            if index < 2:
                opposite = stats_ref[:, pl.ds((index + 2) * rows, half)]
            else:
                opposite = stats_ref[pl.ds(half, half), block(index + 2)].T
            out_ref[:, pl.ds(2 * rows, half)] = opposite.astype(jnp.bfloat16)


def trim(place, table, stats):
    rows = stats.shape[0]
    out = jax.ShapeDtypeStruct((rows, 2 * rows + rows // 2), jnp.bfloat16)
    return call(trim_kernel, "trim", out, [SMEM, SMEM, VMEM], (place, table, stats), flops=stats.size, moved=6 * stats.size)


def send_kernel(place_ref, grads_ref, x_up, x_down, y_up, y_down, sems):
    x, y = steps(place_ref, 0), steps(place_ref, 1)
    moves = []
    for i in range(2):
        moves += [
            ((0, i, x[2]), x_up, i),
            ((0, 2 + i, x[1]), x_up, 2 + i),
            ((0, 2 + i, x[2]), x_down, i),
            ((0, i, x[3]), x_down, 2 + i),
            ((1, y[2], i), y_up, i),
            ((1, y[1], 2 + i), y_up, 2 + i),
            ((1, y[2], 2 + i), y_down, i),
            ((1, y[3], i), y_down, 2 + i),
        ]
    copy_blocks(grads_ref, moves, 4, sems)


def keep_kernel(place_ref, grads_ref, x_mid, x_own, y_mid, y_own, sems):
    x, y = steps(place_ref, 0), steps(place_ref, 1)
    moves = []
    for i in range(2):
        moves += [
            ((0, i, x[1]), x_mid, i),
            ((0, 2 + i, x[3]), x_mid, 2 + i),
            ((1, y[1], i), y_mid, i),
            ((1, y[3], 2 + i), y_mid, 2 + i),
        ]
    for i in range(4):
        moves += [((0, i, x[0]), x_own, i), ((1, y[0], i), y_own, i)]
    copy_blocks(grads_ref, moves, 1, sems)


def pack(kernel, mib, place, grads):
    payload = jax.ShapeDtypeStruct((4,) + grads.shape[3:], grads.dtype)
    return call(
        kernel,
        kernel.__name__[:4],
        (payload,) * 4,
        [SMEM, HBM],
        (place, grads),
        scratch=[pltpu.SemaphoreType.DMA((64,))],
        mib=mib,
        moved=2**23,
    )


def root_kernel(place_ref, table_ref, *refs):
    given, (out_ref, right_ref, slots_ref, rights_ref, start_ref, first_ref, second_ref, third_ref, sem) = refs[:8], refs[8:]
    size = out_ref.shape[0]
    slot = size // 4
    half = slot // 2
    offset, zl, c = table_ref[0], place_ref[2], place_ref[3]

    def span(tile):
        return pl.ds(tile * slot, slot)

    for first_tile, to_ref in ((4, rights_ref), (0, slots_ref)):
        for tile in range(4):
            position = lax.rem(offset + first_tile + tile, 8)
            back = lax.rem(zl + 4 - lax.div(position, 2), 4)
            source = 2 * back + lax.rem(position + c, 2)
            for i, ref in enumerate(given):

                @pl.when(source == i)
                def _():
                    to_ref[tile] = ref[...]

    passed = pltpu.make_async_copy(rights_ref, right_ref, sem)
    passed.start()

    total = jnp.zeros((8, slot // 2), jnp.float32)
    for tile in range(4):
        values = slots_ref[tile].astype(jnp.float32)
        squares = values * values
        total = total + lanes(squares[:, :slot]) + 2.0 * lanes(squares[:, slot:])
    inverse = 1.0 / jnp.sqrt(jnp.sum(total))

    row_ids = lax.broadcasted_iota(jnp.int32, (slot, slot), 0)
    col_ids = lax.broadcasted_iota(jnp.int32, (slot, slot), 1)
    eye = jnp.where(row_ids == col_ids, 1.0, 0.0).astype(jnp.float32)

    def place(row, column, normed, diagonal):
        start_ref[span(row), span(column)] = normed.astype(jnp.bfloat16)
        term = 1.5 * eye - 0.5 * normed if diagonal else -0.5 * normed
        first_ref[span(row), span(column)] = term.astype(jnp.bfloat16)

    for tile in range(4):
        after = (tile + 1) % 4
        place(tile, tile, slots_ref[tile, :, :slot].astype(jnp.float32) * inverse, True)
        normed = slots_ref[tile, :, slot : 2 * slot].astype(jnp.float32) * inverse
        place(tile, after, normed, False)
        place(after, tile, normed.T, False)
    for tile in range(2):
        parts = [slots_ref[at, :, 2 * slot :].astype(jnp.float32) * inverse for at in (tile, tile + 2)]
        normed = jnp.concatenate(parts, axis=1)
        place(tile, tile + 2, normed, False)
        place(tile + 2, tile, normed.T, False)

    def eye_rows(tile):
        row_ids = lax.broadcasted_iota(jnp.int32, (slot, size), 0) + tile * slot
        col_ids = lax.broadcasted_iota(jnp.int32, (slot, size), 1)
        return jnp.where(row_ids == col_ids, 1.0, 0.0).astype(jnp.float32)

    for tile in range(4):
        product = jnp.dot(start_ref[span(tile), :], first_ref[...], preferred_element_type=jnp.float32)
        second_ref[span(tile), :] = product.astype(jnp.bfloat16)
    for tile in range(4):
        product = jnp.dot(first_ref[span(tile), :], second_ref[...], preferred_element_type=jnp.float32)
        third_ref[span(tile), :] = (1.5 * eye_rows(tile) - 0.5 * product).astype(jnp.bfloat16)
    for tile in range(4):
        product = jnp.dot(third_ref[span(tile), :], first_ref[...], preferred_element_type=jnp.float32)
        out_ref[span(tile), :] = product.astype(jnp.bfloat16)
    passed.wait()


def left_inverse_root(place, table, slots):
    rows, kept = slots[0].shape
    size = 4 * rows
    matrix, side = (size, size), (4, rows, kept)
    return pl.pallas_call(
        root_kernel,
        out_shape=(jax.ShapeDtypeStruct(matrix, jnp.bfloat16), jax.ShapeDtypeStruct(side, jnp.bfloat16)),
        in_specs=[SMEM] * 2 + [VMEM] * 8,
        out_specs=(VMEM, HBM),
        scratch_shapes=[pltpu.VMEM(side, jnp.bfloat16)] * 2
        + [pltpu.VMEM(matrix, jnp.bfloat16)] * 4
        + [pltpu.SemaphoreType.DMA(())],
        compiler_params=pltpu.CompilerParams(vmem_limit_bytes=18 * 2**20),
        cost_estimate=pl.CostEstimate(flops=6 * size**3, bytes_accessed=4 * size * size, transcendentals=0),
        name="left_root",
    )(place, table, *slots)


def base_kernel(slots_ref, first_ref, diagonal_ref):
    size = first_ref.shape[0]
    slot = size // 4

    def span(tile):
        return pl.ds(tile * slot, slot)

    total = jnp.zeros((8, slot // 2), jnp.float32)
    for tile in range(4):
        values = slots_ref[tile].astype(jnp.float32)
        squares = values * values
        total = total + lanes(squares[:, :slot]) + 2.0 * lanes(squares[:, slot:])
    inverse = 1.0 / jnp.sqrt(jnp.sum(total))

    row_ids = lax.broadcasted_iota(jnp.int32, (slot, slot), 0)
    col_ids = lax.broadcasted_iota(jnp.int32, (slot, slot), 1)
    eye = jnp.where(row_ids == col_ids, 1.0, 0.0).astype(jnp.float32)

    def place(row, column, normed):
        first_ref[span(row), span(column)] = (-0.5 * normed).astype(jnp.bfloat16)

    for tile in range(4):
        following = (tile + 1) % 4
        normed = slots_ref[tile, :, :slot].astype(jnp.float32) * inverse
        first = (1.5 * eye - 0.5 * normed).astype(jnp.bfloat16)
        first_ref[span(tile), span(tile)] = first
        start = normed.astype(jnp.bfloat16).astype(jnp.float32)
        both = eye * (start + 2.0 * first.astype(jnp.float32))
        row = jnp.sum(both, axis=0, keepdims=True)
        diagonal_ref[:, span(tile)] = jnp.broadcast_to(row, (diagonal_ref.shape[0], slot))
        normed = slots_ref[tile, :, slot : 2 * slot].astype(jnp.float32) * inverse
        place(tile, following, normed)
        place(following, tile, normed.T)
    for tile in range(2):
        parts = [slots_ref[at, :, 2 * slot :].astype(jnp.float32) * inverse for at in (tile, tile + 2)]
        normed = jnp.concatenate(parts, axis=1)
        place(tile, tile + 2, normed)
        place(tile + 2, tile, normed.T)


def right_base(slots):
    size = 4 * slots.shape[1]
    return call(
        base_kernel,
        "right_base",
        (jax.ShapeDtypeStruct((size, size), jnp.bfloat16), jax.ShapeDtypeStruct((8, size), jnp.float32)),
        [VMEM],
        (slots,),
        flops=4 * size * size,
        moved=4 * size * size,
    )


def lanes(squares):
    rows, columns = squares.shape
    total = jnp.sum(squares.reshape(rows // 8, 8, columns), axis=0)
    return sum(total[:, at : at + 128] for at in range(0, columns, 128))


def mix_kernel(zl_ref, pieces_ref, left_ref, *refs):
    out_refs, (energy_ref, grad_ref, held_ref) = refs[:4], refs[4:]
    count, rows = pieces_ref.shape[0] // 2, pieces_ref.shape[1]
    energy = jnp.zeros(energy_ref.shape, jnp.float32)
    for piece in range(count):
        grad = narrow(pieces_ref[piece], pieces_ref[count + piece])
        grad_ref[pl.ds(piece * rows, rows), :] = grad
        wide = grad.astype(jnp.float32)
        energy = energy + lanes(wide * wide)
    energy_ref[...] = energy
    for piece in range(0, count, 2):
        product = jnp.dot(
            left_ref[pl.ds(piece * rows, 2 * rows), :], grad_ref[...], preferred_element_type=jnp.float32
        ).astype(jnp.bfloat16)
        held_ref[piece // 2, 0] = product[:rows]
        held_ref[piece // 2, 1] = product[rows:]
    for step, out_ref in enumerate(out_refs):
        out_ref[...] = held_ref[lax.rem(zl_ref[0] + step, 4)]


def mix(zl, pieces, left_root):
    _, rows, width = pieces.shape
    out = jax.ShapeDtypeStruct((2, rows, width), jnp.bfloat16)
    return call(
        mix_kernel,
        "mix",
        (out,) * 4 + (jax.ShapeDtypeStruct((8, 128), jnp.float32),),
        [SMEM] + [VMEM] * 2,
        (zl, pieces, left_root),
        scratch=[pltpu.VMEM((8 * rows, width), jnp.bfloat16), pltpu.VMEM((4,) + out.shape, jnp.bfloat16)],
        flops=2 * left_root.size * width,
        moved=2 * left_root.size,
    )


def split_kernel(c_ref, *refs):
    got, out_ref = refs[:4], refs[4]
    for step, ref in enumerate(got):
        out_ref[step] = ref[1 - c_ref[0]]


def exchange(c, mixed, dep):
    got = after(dep, mixed[0]) + tuple(shift(each, "zl", step) for step, each in enumerate(mixed) if step)
    give = jax.ShapeDtypeStruct((4,) + mixed[0].shape[1:], mixed[0].dtype)
    give = call(split_kernel, "split", give, [SMEM] + [VMEM] * 4, (c,) + got, moved=4 * give.size)
    return got + (swap(give, "c", 1),)


def condition_kernel(zl_ref, c_ref, *refs):
    got, other_ref, refs = refs[:4], refs[4], refs[5:]
    first_ref, diagonal_ref, energy_ref, out_ref, totals_ref, wide_ref, even_ref, odd_ref, held_ref = refs
    count, _, width = held_ref.shape
    zl, c = zl_ref[0], c_ref[0]
    for step, ref in enumerate(got):
        chip = lax.rem(zl + (4 - step), 4)
        held_ref[2 * chip + c] = ref[c]
        held_ref[2 * chip + 1 - c] = other_ref[step]
    for piece in range(count):
        odd_ref[:, pl.ds(piece * width, width)] = held_ref[piece]

    def products(slab_ref):
        for column in range(0, out_ref.shape[1], 2 * width):
            at = pl.ds(column, 2 * width)
            yield at, jnp.dot(slab_ref[...], first_ref[:, at], preferred_element_type=jnp.float32)

    for at, product in products(odd_ref):
        wide_ref[:, at] = product
        even_ref[:, at] = product.astype(jnp.bfloat16)
    for at, product in products(even_ref):
        odd_ref[:, at] = product.astype(jnp.bfloat16)
    for at, product in products(odd_ref):
        started = diagonal_ref[:1, at] * odd_ref[:, at].astype(jnp.float32) - 2.0 * product
        even_ref[:, at] = started.astype(jnp.bfloat16)
    total = jnp.zeros(energy_ref.shape, jnp.float32)
    for at, product in products(even_ref):
        precond = 1.5 * wide_ref[:, at] - 0.5 * product
        out_ref[:, at] = precond
        total = total + lanes(precond * precond)
    row_ids = lax.broadcasted_iota(jnp.int32, energy_ref.shape, 0)
    grad_sums = jnp.sum(energy_ref[...], axis=0, keepdims=True)
    cond_sums = jnp.sum(total, axis=0, keepdims=True)
    sums = jnp.where(row_ids == 0, grad_sums, jnp.where(row_ids == 1, cond_sums, 0.0))
    for piece in range(count):
        totals_ref[piece] = sums


def condition(zl, c, mixed, first, diagonal, energy):
    _, rows, width = mixed[0].shape
    slab = (rows, 8 * width)
    return call(
        condition_kernel,
        "condition",
        (jax.ShapeDtypeStruct(slab, jnp.float32), jax.ShapeDtypeStruct((8, 8, 128), jnp.float32)),
        [SMEM] * 2 + [VMEM] * 8,
        (zl, c) + mixed + (first, diagonal, energy),
        scratch=[pltpu.VMEM(slab, jnp.float32), pltpu.VMEM(slab, jnp.bfloat16), pltpu.VMEM(slab, jnp.bfloat16), pltpu.VMEM((8, rows, width), jnp.bfloat16)],
        flops=8 * rows * first.size,
        moved=2 * first.size,
    )


def finish_kernel(count, totals_ref, precond_ref, out_ref):
    totals = sum(totals_ref[piece] for piece in range(totals_ref.shape[0]))
    grad_mean = jnp.sum(totals[:1]) / count
    cond_mean = jnp.sum(totals[1:2]) / count
    factor = jnp.sqrt(grad_mean / (cond_mean + 1e-06))
    for row in range(0, out_ref.shape[0], 32):
        at = pl.ds(row, 32)
        out_ref[at] = precond_ref[at] * factor


def finish(totals, precond, count):
    return call(
        functools.partial(finish_kernel, count),
        "finish",
        jax.ShapeDtypeStruct(precond.shape, jnp.float32),
        [VMEM] * 2,
        (totals, precond),
        flops=precond.size,
        moved=8 * precond.size,
    )


def after(dep, *values):
    return lax.optimization_barrier((dep,) + values)[1:]


def local(grad_partial, factor_stats, owner_table):
    size = grad_partial.shape[3]
    rows_here = grad_partial.shape[2]
    owner = ("zl", "c")
    grads = grad_partial.reshape(2, 4, 4, rows_here, size)
    x, y, zl, c = (lax.axis_index(axis).astype(jnp.int32) for axis in ("x", "y", "zl", "c"))
    place = jnp.stack((x, y, zl, c))

    x_up, x_down, y_up, y_down = pack(send_kernel, 48, place, grads)
    x_ends = ring_first(x_up, x_down, "x")
    y_ends = ring_first(y_up, y_down, "y")

    (sent,) = after(x_up, place)
    near = [trim(sent, owner_table, factor_stats[0, 0])]
    near.append(shift(near[0], "zl", 1))
    x_mid, x_own, y_mid, y_own = pack(keep_kernel, 16, sent, grads)
    near.append(shift(*after(x_mid, near[1]), "zl", 1))
    near.append(shift(near[2], "zl", 1))
    (x_mid,) = after(near[2], x_mid)
    x_last = pass_on(x_mid, *x_ends)
    y_last = pass_on(y_mid, *y_ends)
    far = [swap(each, "c", 1) for each in near[:3]]
    far.append(swap(*after(x_last[0], near[3]), "c", 1))
    slots = tuple(each for pair in zip(near, far) for each in pair)

    x_last = ring_first(*x_last, "x")
    y_last = ring_first(*y_last, "y")
    for each in (near[3], *far[:3]):
        (y_own,) = after(each, y_own)

    lower_up, lower_down, lower_mid, lower_own = turn(y[None], x_own, *x_ends, *x_last)
    lower_ends = ring_first(lower_up, lower_down, "y")
    upper_up, upper_down, upper_mid, upper_own = turn(x[None], y_own, *y_ends, *y_last)
    upper_ends = ring_first(upper_up, upper_down, "x")
    lower_last = ring_first(*pass_on(lower_mid, *lower_ends), "y")
    upper_last = ring_first(*pass_on(upper_mid, *upper_ends), "x")
    pieces = make_pieces(lower_own, *lower_ends, *lower_last, upper_own, *upper_ends, *upper_last)

    slots = after(pieces, *slots)
    pieces = lax.all_to_all(pieces, ("zh",) + owner, split_axis=0, concat_axis=0, tiled=True)
    left_root, right_slots = left_inverse_root(place, owner_table, slots)
    *mixed, energy = mix(zl[None], pieces, left_root)
    right = right_base(*after(mixed[0], right_slots))
    mixed = exchange(c[None], tuple(mixed), right[0])
    precond, totals = condition(zl[None], c[None], mixed, *right, energy)
    totals = lax.all_to_all(totals, owner, split_axis=0, concat_axis=0, tiled=True)
    return finish(totals, precond, float(size * size))[None]


def solution(mesh):
    dp, owner = ("zh", "y", "x"), ("zl", "c")
    placed = (P(dp, None, owner, None), P(dp, owner, None, None), P(dp))
    return jax.shard_map(
        local, mesh=fine_mesh(mesh), in_specs=placed, out_specs=P(dp, owner, None), check_vma=False
    )
```

```python
import functools

import jax
import jax.numpy as jnp
from jax import lax
from jax.experimental import pallas as pl
from jax.experimental.pallas import tpu as pltpu
from jax.sharding import Mesh
from jax.sharding import PartitionSpec as P

FINE = ("zh", "y", "x", "zl", "c")


def fine_mesh(mesh):
    return Mesh(mesh.devices.reshape(2, 4, 4, 4, 2), FINE)


def shift(array, axis, step):
    size = lax.axis_size(axis)
    return lax.ppermute(array, axis, [(i, (i + step) % size) for i in range(size)])


def swap(array, axis, mask):
    size = lax.axis_size(axis)
    return lax.ppermute(array, axis, [(i, i ^ mask) for i in range(size)])


def f32sum(*terms):
    total = terms[0].astype(jnp.float32)
    for term in terms[1:]:
        total = total + term.astype(jnp.float32)
    return total


def narrow(*terms):
    return f32sum(*terms).astype(jnp.bfloat16)


VMEM = pl.BlockSpec(memory_space=pltpu.VMEM)
SMEM = pl.BlockSpec(memory_space=pltpu.SMEM)
HBM = pl.BlockSpec(memory_space=pltpu.HBM)


def call(kernel, name, out_shape, in_specs, operands, scratch=(), mib=16, flops=0, moved=0):
    outs = (VMEM,) * len(out_shape) if isinstance(out_shape, tuple) else VMEM
    return pl.pallas_call(
        kernel,
        out_shape=out_shape,
        in_specs=in_specs,
        out_specs=outs,
        scratch_shapes=list(scratch),
        compiler_params=pltpu.CompilerParams(vmem_limit_bytes=mib * 2**20),
        cost_estimate=pl.CostEstimate(flops=flops, bytes_accessed=moved, transcendentals=0),
        name=name,
    )(*operands)


def ring_first(up, down, axis):
    return shift(up, axis, 1), shift(down, axis, -1)


def pass_kernel(mid_ref, up_ref, down_ref, last_up_ref, last_down_ref):
    count, rows, _ = last_up_ref.shape
    for block in range(count):
        for row in range(0, rows, 32):
            at = pl.ds(row, 32)
            last_up_ref[block, at] = narrow(mid_ref[block, at], up_ref[block, at])
            last_down_ref[block, at] = narrow(mid_ref[count + block, at], down_ref[block, at])


def pass_on(mid, up, down):
    count = mid.shape[0] // 2
    last = jax.ShapeDtypeStruct((count,) + mid.shape[1:], mid.dtype)
    last_up, last_down = call(
        pass_kernel, "pass_on", (last, last), [VMEM] * 3, (mid, up, down), flops=mid.size, moved=6 * mid.size
    )
    return last_up, last_down


def turn_kernel(place_ref, own_ref, up_ref, down_ref, last_up_ref, last_down_ref, next_up, next_down, next_mid, next_own, sum_ref):
    rows = own_ref.shape[1]
    half = rows // 2
    for block in range(2):
        for row in range(0, rows, 32):
            at = pl.ds(row, 32)
            sum_ref[block, at] = narrow(own_ref[block, at], last_up_ref[block, at], down_ref[2 + block, at])
            sum_ref[2 + block, at] = narrow(own_ref[2 + block, at], up_ref[2 + block, at], last_down_ref[block, at])
    low, high = pl.ds(0, half), pl.ds(half, half)
    here = place_ref[0]
    ahead, across, behind = (lax.rem(here + step, 4) for step in (1, 2, 3))
    next_up[0] = sum_ref[across, low]
    next_up[1] = sum_ref[ahead, high]
    next_down[0] = sum_ref[across, high]
    next_down[1] = sum_ref[behind, low]
    next_mid[0] = sum_ref[ahead, low]
    next_mid[1] = sum_ref[behind, high]
    next_own[0] = sum_ref[here, low]
    next_own[1] = sum_ref[here, high]


def turn(place, own, up, down, last_up, last_down):
    rows, size = own.shape[1:]
    part = jax.ShapeDtypeStruct((2, rows // 2, size), own.dtype)
    return call(
        turn_kernel,
        "turn",
        (part,) * 4,
        [SMEM] + [VMEM] * 5,
        (place, own, up, down, last_up, last_down),
        scratch=[pltpu.VMEM(own.shape, own.dtype)],
        flops=2 * own.size,
        moved=8 * own.size,
    )


def pieces_kernel(*refs):
    out_ref = refs[-1]
    width = out_ref.shape[2]
    for side in range(2):
        own, up, down, last_up, last_down = refs[5 * side : 5 * side + 5]
        half = own.shape[1]
        for row in range(0, half, 32):
            at = pl.ds(row, 32)
            low = narrow(own[0, at], last_up[0, at], down[1, at])
            high = narrow(own[1, at], up[1, at], last_down[0, at])
            for piece in range(8):
                columns = slice(piece * width, (piece + 1) * width)
                out_ref[8 * side + piece, at] = low[:, columns]
                out_ref[8 * side + piece, pl.ds(half + row, 32)] = high[:, columns]


def make_pieces(*parts):
    rows, size = 2 * parts[0].shape[1], parts[0].shape[2]
    out = jax.ShapeDtypeStruct((16, rows, size // 8), jnp.bfloat16)
    return call(
        pieces_kernel, "pieces", out, [VMEM] * 10, parts, flops=4 * rows * size, moved=16 * rows * size
    )


def copy_blocks(grads_ref, moves, cut, sems):
    rows = grads_ref.shape[3] // cut
    copies = [
        pltpu.make_async_copy(
            grads_ref.at[where + (pl.ds(part * rows, rows),)],
            out.at[slot, pl.ds(part * rows, rows)],
            sems.at[cut * i + part],
        )
        for i, (where, out, slot) in enumerate(moves)
        for part in range(cut)
    ]
    for each in copies:
        each.start()
    for each in copies:
        each.wait()


def steps(place_ref, which):
    return tuple(lax.rem(place_ref[which] + step, 4) for step in range(4))


def trim_kernel(place_ref, table_ref, stats_ref, out_ref):
    rows = stats_ref.shape[0]
    half = rows // 2
    slot = lax.rem(2 * place_ref[2] + place_ref[3] + 8 - table_ref[0], 4)

    def block(at):
        return pl.ds(at % 4 * rows, rows)

    for index in range(4):

        @pl.when(slot == index)
        def _():
            out_ref[:, block(0)] = stats_ref[:, block(index)].astype(jnp.bfloat16)
            out_ref[:, block(1)] = stats_ref[:, block(index + 1)].astype(jnp.bfloat16)
            if index < 2:
                opposite = stats_ref[:, pl.ds((index + 2) * rows, half)]
            else:
                opposite = stats_ref[pl.ds(half, half), block(index + 2)].T
            out_ref[:, pl.ds(2 * rows, half)] = opposite.astype(jnp.bfloat16)


def trim(place, table, stats):
    rows = stats.shape[0]
    out = jax.ShapeDtypeStruct((rows, 2 * rows + rows // 2), jnp.bfloat16)
    return call(trim_kernel, "trim", out, [SMEM, SMEM, VMEM], (place, table, stats), flops=stats.size, moved=6 * stats.size)


def send_kernel(place_ref, grads_ref, x_up, x_down, y_up, y_down, sems):
    x, y = steps(place_ref, 0), steps(place_ref, 1)
    moves = []
    for i in range(2):
        moves += [
            ((0, i, x[2]), x_up, i),
            ((0, 2 + i, x[1]), x_up, 2 + i),
            ((0, 2 + i, x[2]), x_down, i),
            ((0, i, x[3]), x_down, 2 + i),
            ((1, y[2], i), y_up, i),
            ((1, y[1], 2 + i), y_up, 2 + i),
            ((1, y[2], 2 + i), y_down, i),
            ((1, y[3], i), y_down, 2 + i),
        ]
    copy_blocks(grads_ref, moves, 4, sems)


def keep_kernel(place_ref, grads_ref, x_mid, x_own, y_mid, y_own, sems):
    x, y = steps(place_ref, 0), steps(place_ref, 1)
    moves = []
    for i in range(2):
        moves += [
            ((0, i, x[1]), x_mid, i),
            ((0, 2 + i, x[3]), x_mid, 2 + i),
            ((1, y[1], i), y_mid, i),
            ((1, y[3], 2 + i), y_mid, 2 + i),
        ]
    for i in range(4):
        moves += [((0, i, x[0]), x_own, i), ((1, y[0], i), y_own, i)]
    copy_blocks(grads_ref, moves, 1, sems)


def pack(kernel, mib, place, grads):
    payload = jax.ShapeDtypeStruct((4,) + grads.shape[3:], grads.dtype)
    return call(
        kernel,
        kernel.__name__[:4],
        (payload,) * 4,
        [SMEM, HBM],
        (place, grads),
        scratch=[pltpu.SemaphoreType.DMA((64,))],
        mib=mib,
        moved=2**23,
    )


def root_kernel(place_ref, table_ref, *refs):
    given, (out_ref, right_ref, slots_ref, rights_ref, start_ref, first_ref, second_ref, third_ref, sem) = refs[:8], refs[8:]
    size = out_ref.shape[0]
    slot = size // 4
    half = slot // 2
    offset, zl, c = table_ref[0], place_ref[2], place_ref[3]

    def span(tile):
        return pl.ds(tile * slot, slot)

    for first_tile, to_ref in ((4, rights_ref), (0, slots_ref)):
        for tile in range(4):
            position = lax.rem(offset + first_tile + tile, 8)
            back = lax.rem(zl + 4 - lax.div(position, 2), 4)
            source = 2 * back + lax.rem(position + c, 2)
            for i, ref in enumerate(given):

                @pl.when(source == i)
                def _():
                    to_ref[tile] = ref[...]

    passed = pltpu.make_async_copy(rights_ref, right_ref, sem)
    passed.start()

    total = jnp.zeros((8, slot // 2), jnp.float32)
    for tile in range(4):
        values = slots_ref[tile].astype(jnp.float32)
        squares = values * values
        total = total + lanes(squares[:, :slot]) + 2.0 * lanes(squares[:, slot:])
    inverse = 1.0 / jnp.sqrt(jnp.sum(total))

    row_ids = lax.broadcasted_iota(jnp.int32, (slot, slot), 0)
    col_ids = lax.broadcasted_iota(jnp.int32, (slot, slot), 1)
    eye = jnp.where(row_ids == col_ids, 1.0, 0.0).astype(jnp.float32)

    def place(row, column, normed, diagonal):
        start_ref[span(row), span(column)] = normed.astype(jnp.bfloat16)
        term = 1.5 * eye - 0.5 * normed if diagonal else -0.5 * normed
        first_ref[span(row), span(column)] = term.astype(jnp.bfloat16)

    for tile in range(4):
        after = (tile + 1) % 4
        place(tile, tile, slots_ref[tile, :, :slot].astype(jnp.float32) * inverse, True)
        normed = slots_ref[tile, :, slot : 2 * slot].astype(jnp.float32) * inverse
        place(tile, after, normed, False)
        place(after, tile, normed.T, False)
    for tile in range(2):
        parts = [slots_ref[at, :, 2 * slot :].astype(jnp.float32) * inverse for at in (tile, tile + 2)]
        normed = jnp.concatenate(parts, axis=1)
        place(tile, tile + 2, normed, False)
        place(tile + 2, tile, normed.T, False)

    def eye_rows(tile):
        row_ids = lax.broadcasted_iota(jnp.int32, (slot, size), 0) + tile * slot
        col_ids = lax.broadcasted_iota(jnp.int32, (slot, size), 1)
        return jnp.where(row_ids == col_ids, 1.0, 0.0).astype(jnp.float32)

    for tile in range(4):
        product = jnp.dot(start_ref[span(tile), :], first_ref[...], preferred_element_type=jnp.float32)
        second_ref[span(tile), :] = product.astype(jnp.bfloat16)
    for tile in range(4):
        product = jnp.dot(first_ref[span(tile), :], second_ref[...], preferred_element_type=jnp.float32)
        third_ref[span(tile), :] = (1.5 * eye_rows(tile) - 0.5 * product).astype(jnp.bfloat16)
    for tile in range(4):
        product = jnp.dot(third_ref[span(tile), :], first_ref[...], preferred_element_type=jnp.float32)
        out_ref[span(tile), :] = product.astype(jnp.bfloat16)
    passed.wait()


def left_inverse_root(place, table, slots):
    rows, kept = slots[0].shape
    size = 4 * rows
    matrix, side = (size, size), (4, rows, kept)
    return pl.pallas_call(
        root_kernel,
        out_shape=(jax.ShapeDtypeStruct(matrix, jnp.bfloat16), jax.ShapeDtypeStruct(side, jnp.bfloat16)),
        in_specs=[SMEM] * 2 + [VMEM] * 8,
        out_specs=(VMEM, HBM),
        scratch_shapes=[pltpu.VMEM(side, jnp.bfloat16)] * 2
        + [pltpu.VMEM(matrix, jnp.bfloat16)] * 4
        + [pltpu.SemaphoreType.DMA(())],
        compiler_params=pltpu.CompilerParams(vmem_limit_bytes=18 * 2**20),
        cost_estimate=pl.CostEstimate(flops=6 * size**3, bytes_accessed=4 * size * size, transcendentals=0),
        name="left_root",
    )(place, table, *slots)


def base_kernel(slots_ref, first_ref, diagonal_ref):
    size = first_ref.shape[0]
    slot = size // 4

    def span(tile):
        return pl.ds(tile * slot, slot)

    total = jnp.zeros((8, slot // 2), jnp.float32)
    for tile in range(4):
        values = slots_ref[tile].astype(jnp.float32)
        squares = values * values
        total = total + lanes(squares[:, :slot]) + 2.0 * lanes(squares[:, slot:])
    inverse = 1.0 / jnp.sqrt(jnp.sum(total))

    row_ids = lax.broadcasted_iota(jnp.int32, (slot, slot), 0)
    col_ids = lax.broadcasted_iota(jnp.int32, (slot, slot), 1)
    eye = jnp.where(row_ids == col_ids, 1.0, 0.0).astype(jnp.float32)

    def place(row, column, normed):
        first_ref[span(row), span(column)] = (-0.5 * normed).astype(jnp.bfloat16)

    for tile in range(4):
        following = (tile + 1) % 4
        normed = slots_ref[tile, :, :slot].astype(jnp.float32) * inverse
        first = (1.5 * eye - 0.5 * normed).astype(jnp.bfloat16)
        first_ref[span(tile), span(tile)] = first
        start = normed.astype(jnp.bfloat16).astype(jnp.float32)
        both = eye * (start + 2.0 * first.astype(jnp.float32))
        row = jnp.sum(both, axis=0, keepdims=True)
        diagonal_ref[:, span(tile)] = jnp.broadcast_to(row, (diagonal_ref.shape[0], slot))
        normed = slots_ref[tile, :, slot : 2 * slot].astype(jnp.float32) * inverse
        place(tile, following, normed)
        place(following, tile, normed.T)
    for tile in range(2):
        parts = [slots_ref[at, :, 2 * slot :].astype(jnp.float32) * inverse for at in (tile, tile + 2)]
        normed = jnp.concatenate(parts, axis=1)
        place(tile, tile + 2, normed)
        place(tile + 2, tile, normed.T)


def right_base(slots):
    size = 4 * slots.shape[1]
    return call(
        base_kernel,
        "right_base",
        (jax.ShapeDtypeStruct((size, size), jnp.bfloat16), jax.ShapeDtypeStruct((8, size), jnp.float32)),
        [VMEM],
        (slots,),
        flops=4 * size * size,
        moved=4 * size * size,
    )


def lanes(squares):
    rows, columns = squares.shape
    total = jnp.sum(squares.reshape(rows // 8, 8, columns), axis=0)
    return sum(total[:, at : at + 128] for at in range(0, columns, 128))


def mix_kernel(zl_ref, pieces_ref, left_ref, *refs):
    out_refs, (energy_ref, grad_ref, held_ref) = refs[:4], refs[4:]
    count, rows = pieces_ref.shape[0] // 2, pieces_ref.shape[1]
    energy = jnp.zeros(energy_ref.shape, jnp.float32)
    for piece in range(count):
        grad = narrow(pieces_ref[piece], pieces_ref[count + piece])
        grad_ref[pl.ds(piece * rows, rows), :] = grad
        wide = grad.astype(jnp.float32)
        energy = energy + lanes(wide * wide)
    energy_ref[...] = energy
    for piece in range(0, count, 2):
        product = jnp.dot(
            left_ref[pl.ds(piece * rows, 2 * rows), :], grad_ref[...], preferred_element_type=jnp.float32
        ).astype(jnp.bfloat16)
        held_ref[piece // 2, 0] = product[:rows]
        held_ref[piece // 2, 1] = product[rows:]
    for step, out_ref in enumerate(out_refs):
        out_ref[...] = held_ref[lax.rem(zl_ref[0] + step, 4)]


def mix(zl, pieces, left_root):
    _, rows, width = pieces.shape
    out = jax.ShapeDtypeStruct((2, rows, width), jnp.bfloat16)
    return call(
        mix_kernel,
        "mix",
        (out,) * 4 + (jax.ShapeDtypeStruct((8, 128), jnp.float32),),
        [SMEM] + [VMEM] * 2,
        (zl, pieces, left_root),
        scratch=[pltpu.VMEM((8 * rows, width), jnp.bfloat16), pltpu.VMEM((4,) + out.shape, jnp.bfloat16)],
        flops=2 * left_root.size * width,
        moved=2 * left_root.size,
    )


def split_kernel(c_ref, *refs):
    got, out_ref = refs[:4], refs[4]
    for step, ref in enumerate(got):
        out_ref[step] = ref[1 - c_ref[0]]


def exchange(c, mixed, dep):
    got = after(dep, mixed[0]) + tuple(shift(each, "zl", step) for step, each in enumerate(mixed) if step)
    give = jax.ShapeDtypeStruct((4,) + mixed[0].shape[1:], mixed[0].dtype)
    give = call(split_kernel, "split", give, [SMEM] + [VMEM] * 4, (c,) + got, moved=4 * give.size)
    return got + (swap(give, "c", 1),)


def condition_kernel(zl_ref, c_ref, *refs):
    got, other_ref, refs = refs[:4], refs[4], refs[5:]
    first_ref, diagonal_ref, energy_ref, out_ref, totals_ref, wide_ref, even_ref, odd_ref, held_ref = refs
    count, _, width = held_ref.shape
    zl, c = zl_ref[0], c_ref[0]
    for step, ref in enumerate(got):
        chip = lax.rem(zl + (4 - step), 4)
        held_ref[2 * chip + c] = ref[c]
        held_ref[2 * chip + 1 - c] = other_ref[step]
    for piece in range(count):
        odd_ref[:, pl.ds(piece * width, width)] = held_ref[piece]

    def products(slab_ref):
        for column in range(0, out_ref.shape[1], 2 * width):
            at = pl.ds(column, 2 * width)
            yield at, jnp.dot(slab_ref[...], first_ref[:, at], preferred_element_type=jnp.float32)

    for at, product in products(odd_ref):
        wide_ref[:, at] = product
        even_ref[:, at] = product.astype(jnp.bfloat16)
    for at, product in products(even_ref):
        odd_ref[:, at] = product.astype(jnp.bfloat16)
    for at, product in products(odd_ref):
        started = diagonal_ref[:1, at] * odd_ref[:, at].astype(jnp.float32) - 2.0 * product
        even_ref[:, at] = started.astype(jnp.bfloat16)
    total = jnp.zeros(energy_ref.shape, jnp.float32)
    for at, product in products(even_ref):
        precond = 1.5 * wide_ref[:, at] - 0.5 * product
        out_ref[:, at] = precond
        total = total + lanes(precond * precond)
    row_ids = lax.broadcasted_iota(jnp.int32, energy_ref.shape, 0)
    grad_sums = jnp.sum(energy_ref[...], axis=0, keepdims=True)
    cond_sums = jnp.sum(total, axis=0, keepdims=True)
    sums = jnp.where(row_ids == 0, grad_sums, jnp.where(row_ids == 1, cond_sums, 0.0))
    for piece in range(count):
        totals_ref[piece] = sums


def condition(zl, c, mixed, first, diagonal, energy):
    _, rows, width = mixed[0].shape
    slab = (rows, 8 * width)
    return call(
        condition_kernel,
        "condition",
        (jax.ShapeDtypeStruct(slab, jnp.float32), jax.ShapeDtypeStruct((8, 8, 128), jnp.float32)),
        [SMEM] * 2 + [VMEM] * 8,
        (zl, c) + mixed + (first, diagonal, energy),
        scratch=[pltpu.VMEM(slab, jnp.float32), pltpu.VMEM(slab, jnp.bfloat16), pltpu.VMEM(slab, jnp.bfloat16), pltpu.VMEM((8, rows, width), jnp.bfloat16)],
        flops=8 * rows * first.size,
        moved=2 * first.size,
    )


def finish_kernel(count, totals_ref, precond_ref, out_ref):
    totals = sum(totals_ref[piece] for piece in range(totals_ref.shape[0]))
    grad_mean = jnp.sum(totals[:1]) / count
    cond_mean = jnp.sum(totals[1:2]) / count
    factor = jnp.sqrt(grad_mean / (cond_mean + 1e-06))
    for row in range(0, out_ref.shape[0], 32):
        at = pl.ds(row, 32)
        out_ref[at] = precond_ref[at] * factor


def finish(totals, precond, count):
    return call(
        functools.partial(finish_kernel, count),
        "finish",
        jax.ShapeDtypeStruct(precond.shape, jnp.float32),
        [VMEM] * 2,
        (totals, precond),
        flops=precond.size,
        moved=8 * precond.size,
    )


def after(dep, *values):
    return lax.optimization_barrier((dep,) + values)[1:]


def local(grad_partial, factor_stats, owner_table):
    size = grad_partial.shape[3]
    rows_here = grad_partial.shape[2]
    owner = ("zl", "c")
    grads = grad_partial.reshape(2, 4, 4, rows_here, size)
    x, y, zl, c = (lax.axis_index(axis).astype(jnp.int32) for axis in ("x", "y", "zl", "c"))
    place = jnp.stack((x, y, zl, c))

    x_up, x_down, y_up, y_down = pack(send_kernel, 48, place, grads)
    x_ends = ring_first(x_up, x_down, "x")
    y_ends = ring_first(y_up, y_down, "y")

    (sent,) = after(x_up, place)
    near = [trim(sent, owner_table, factor_stats[0, 0])]
    near.append(shift(near[0], "zl", 1))
    x_mid, x_own, y_mid, y_own = pack(keep_kernel, 16, sent, grads)
    near.append(shift(*after(x_mid, near[1]), "zl", 1))
    near.append(shift(near[2], "zl", 1))
    (y_mid,) = after(near[2], y_mid)
    x_last = pass_on(x_mid, *x_ends)
    y_last = pass_on(y_mid, *y_ends)
    far = [swap(each, "c", 1) for each in near[:3]]
    far.append(swap(*after(x_last[0], near[3]), "c", 1))
    slots = tuple(each for pair in zip(near, far) for each in pair)

    x_last = ring_first(*x_last, "x")
    y_last = ring_first(*y_last, "y")

    lower_up, lower_down, lower_mid, lower_own = turn(y[None], x_own, *x_ends, *x_last)
    lower_ends = ring_first(lower_up, lower_down, "y")
    upper_up, upper_down, upper_mid, upper_own = turn(x[None], y_own, *y_ends, *y_last)
    upper_ends = ring_first(upper_up, upper_down, "x")
    lower_last = ring_first(*pass_on(lower_mid, *lower_ends), "y")
    upper_last = ring_first(*pass_on(upper_mid, *upper_ends), "x")
    pieces = make_pieces(lower_own, *lower_ends, *lower_last, upper_own, *upper_ends, *upper_last)

    slots = after(pieces, *slots)
    pieces = lax.all_to_all(pieces, ("zh",) + owner, split_axis=0, concat_axis=0, tiled=True)
    left_root, right_slots = left_inverse_root(place, owner_table, slots)
    *mixed, energy = mix(zl[None], pieces, left_root)
    right = right_base(*after(mixed[0], right_slots))
    mixed = exchange(c[None], tuple(mixed), right[0])
    precond, totals = condition(zl[None], c[None], mixed, *right, energy)
    totals = lax.all_to_all(totals, owner, split_axis=0, concat_axis=0, tiled=True)
    return finish(totals, precond, float(size * size))[None]


def solution(mesh):
    dp, owner = ("zh", "y", "x"), ("zl", "c")
    placed = (P(dp, None, owner, None), P(dp, owner, None, None), P(dp))
    return jax.shard_map(
        local, mesh=fine_mesh(mesh), in_specs=placed, out_specs=P(dp, owner, None), check_vma=False
    )
```
